32 devices in a mesh: seq: 8 (over z, y), grp: 4 (over x, core).
Axes of the slice: x: 2, y: 2, z: 4, core: 2. Of those that a mesh axis runs over, the one named last changes fastest.
Arguments:
- q_nope: bfloat16 [128, 128, 128], P('seq', 'grp'), may hold values from -6 to 6
- q_rope: bfloat16 [128, 128, 64], P('seq', 'grp'), may hold values from -256 to 256
- cache: bfloat16 [8192, 576], P('seq'), may hold values from -6 to 6
- w_uk: bfloat16 [128, 65536], P('grp', 'seq'), may hold values from -0.5 to 0.5
- w_uv: bfloat16 [128, 65536], P('grp', 'seq'), may hold values from -0.25 to 0.25
- d_out: bfloat16 [128, 128, 128], P('seq', 'grp'), may hold values from -6 to 6
- sel: int32 [128, 32], P('seq'), may hold values from 0 to 63, as said below
- slot_blocks: int32 [8, 64], P('seq'), may hold values from 0 to 15, as said below
Outputs:
- attn_out: bfloat16 [128, 128, 128], P('seq', 'grp')
- d_q_nope: bfloat16 [128, 128, 128], P('seq', 'grp')
- d_q_rope: bfloat16 [128, 128, 64], P('seq', 'grp')
- d_cache: float32 [8192, 576], P('seq')
The draws below stay inside these ranges and needn't reach their ends.
Inputs may be any that keep to these rules, and one draw needn't show every extreme that they name: `sel`: each row names 32 different places; place s stands for the block that the row's device asks of device s // 8. `slot_blocks`: entry [r, s] is the index among device s // 8's own blocks of the block that device r asks for in place s; the 8 entries of a row toward one device differ.
All inputs are finite; a program needn't handle non-finite values.
Results may differ from the reference program's by a relative error of at most 0.015.
Values may be sent and summed in bfloat16 or wider, within the bound.
No kernel may reach another device: no remote copies, remote signals or barrier semaphores. Data moves between devices by JAX's collectives and lax.ppermute only.
A program may use at most 128 MiB of HBM per device.

```python
import math
import jax
import jax.numpy as jnp
from jax import lax

NUM_HEADS = 128
NOPE_DIM = 128
ROPE_DIM = 64
LATENT = 512
VALUE_DIM = 128
BLOCK_LEN = 64
PICKED = 32
SLOT_COUNT = 64
QUERY_DEV = 16
QUERIES = 128
CONTEXT = 8192
PER_PEER = 8
DEV_BLOCKS = 16


def pick_slots(key):
    base = jax.random.fold_in(key, 11)
    scores = jax.random.randint(base, (QUERIES, SLOT_COUNT), 0, 2 ** 20) * SLOT_COUNT
    scores = scores + jnp.arange(SLOT_COUNT, dtype=jnp.int32)[None, :]
    scores = scores.at[0, SLOT_COUNT - 1].set(-2)
    scores = scores.at[0, 0].set(-1)
    order = jnp.argsort(scores, axis=1)
    return order[:, :PICKED].astype(jnp.int32)


def pick_blocks(key):
    peers = QUERIES // QUERY_DEV
    base = jax.random.fold_in(key, 12)
    scores = jax.random.randint(base, (peers, peers, DEV_BLOCKS), 0, 2 ** 20) * DEV_BLOCKS
    scores = scores + jnp.arange(DEV_BLOCKS, dtype=jnp.int32)[None, None, :]
    scores = scores.at[0, 0, DEV_BLOCKS - 1].set(-1)
    scores = scores.at[0, 1, 0].set(-1)
    order = jnp.argsort(scores, axis=2)
    return order[:, :, :PER_PEER].reshape(peers, SLOT_COUNT).astype(jnp.int32)


def draw_sel(key, part):
    return pick_slots(key)


def draw_slot_blocks(key, part):
    return pick_blocks(key)


def draw_cache(key, part):
    whole = jnp.clip(jax.random.normal(jax.random.fold_in(key, 15), (CONTEXT, LATENT + ROPE_DIM), jnp.float32), -6.0, 6.0)
    return whole.astype(jnp.bfloat16)


def draw_q_rope(key, part):
    drawn = jnp.clip(jax.random.normal(jax.random.fold_in(key, 16), (QUERIES, NUM_HEADS, ROPE_DIM), jnp.float32), -6.0, 6.0)
    return drawn.astype(jnp.bfloat16)


def steps_of(rng, shape, pieces, smallest, largest):
    factor_of, own = 1.0, jax.random.fold_in(rng, 6)
    for axis_at, shards_of in pieces:
        heights = jnp.exp(jax.random.uniform(jax.random.fold_in(own, axis_at), (shards_of,), jnp.float32, smallest / len(pieces), largest / len(pieces)))
        factor_of = factor_of * jnp.repeat(heights, shape[axis_at] // shards_of).reshape([-1 if axis == axis_at else 1 for axis in range(len(shape))])
    return factor_of


def centred(stream_key, extent, width, limit, cuts=(), kind=jnp.bfloat16):
    factor_of = steps_of(stream_key, extent, cuts, -0.22, 0.18) if cuts else 1.0
    entries = jax.random.normal(stream_key, extent, jnp.float32) * width * factor_of
    return jnp.minimum(jnp.maximum(entries, -limit), limit).astype(kind)


def setup_inputs(seed: int = 0) -> dict:
    splits = jax.random.split(jax.random.key(seed), 9)
    q_nope = centred(splits[0], (QUERIES, NUM_HEADS, NOPE_DIM), 1.0, 6.0, ((0, 8), (1, 4)))
    q_rope = draw_q_rope(jax.random.fold_in(splits[8], 71), 0)
    cache = draw_cache(jax.random.fold_in(splits[8], 71), 0)
    w_uk = centred(splits[3], (NUM_HEADS, NOPE_DIM * LATENT), NOPE_DIM ** -0.5, 0.5, ((0, 4), (1, 8)))
    w_uv = centred(splits[4], (NUM_HEADS, LATENT * VALUE_DIM), LATENT ** -0.5, 0.25, ((0, 4), (1, 8)))
    d_out = centred(splits[5], (QUERIES, NUM_HEADS, VALUE_DIM), 1.0, 6.0, ((0, 8), (1, 4)))
    sel = draw_sel(jax.random.fold_in(splits[8], 71), 0)
    slot_blocks = draw_slot_blocks(jax.random.fold_in(splits[8], 71), 0)
    return {"q_nope": q_nope, "q_rope": q_rope, "cache": cache, "w_uk": w_uk, "w_uv": w_uv, "d_out": d_out, "sel": sel, "slot_blocks": slot_blocks}


def reference(q_nope, q_rope, cache, w_uk, w_uv, d_out, sel, slot_blocks):
    scale = 1.0 / math.sqrt(NOPE_DIM + ROPE_DIM)
    weight_k = w_uk.reshape(NUM_HEADS, NOPE_DIM, LATENT).astype(jnp.float32)
    weight_v = w_uv.reshape(NUM_HEADS, LATENT, VALUE_DIM).astype(jnp.float32)
    q_lat = jnp.einsum('qhn,hnl->qhl', q_nope.astype(jnp.float32), weight_k).astype(jnp.bfloat16)
    qfull = jnp.concatenate([q_lat, q_rope], axis=-1)
    d_olat = jnp.einsum('qhv,hlv->qhl', d_out.astype(jnp.float32), weight_v).astype(jnp.bfloat16)
    offsets = jnp.arange(BLOCK_LEN, dtype=jnp.int32)

    def one_query(grads, item):
        query_full, query_dol, picks, row = item
        owner = (picks // PER_PEER).astype(jnp.int32)
        requester = (row // QUERY_DEV).astype(jnp.int32)
        inner = slot_blocks[requester][picks].astype(jnp.int32)
        block = owner * DEV_BLOCKS + inner
        tokens = (block[:, None] * BLOCK_LEN + offsets[None, :]).reshape(-1).astype(jnp.int32)
        keys = cache[tokens]
        keys_lat = keys[:, :LATENT]
        score = jnp.dot(query_full, keys.T, preferred_element_type=jnp.float32) * scale
        prob = jax.nn.softmax(score, axis=-1)
        prob_low = prob.astype(jnp.bfloat16)
        olat = jnp.dot(prob_low, keys_lat, preferred_element_type=jnp.float32).astype(jnp.bfloat16)
        dprob = jnp.dot(query_dol, keys_lat.T, preferred_element_type=jnp.float32)
        delta = lax.optimization_barrier(jnp.sum(prob * dprob, axis=-1, keepdims=True))
        dscore = (prob * (dprob - delta) * scale).astype(jnp.bfloat16)
        dquery = jnp.dot(dscore, keys, preferred_element_type=jnp.float32)
        value_part = jnp.dot(prob_low.T, query_dol, preferred_element_type=jnp.float32)
        dkeys = jnp.dot(dscore.T, query_full, preferred_element_type=jnp.float32)
        dkeys = dkeys + jnp.pad(value_part, ((0, 0), (0, ROPE_DIM)))
        grads = grads.at[tokens].add(dkeys)
        return (grads, (olat, dquery[:, :LATENT].astype(jnp.bfloat16), dquery[:, LATENT:].astype(jnp.bfloat16)))
    start = jnp.zeros((CONTEXT, LATENT + ROPE_DIM), jnp.float32)
    rows = jnp.arange(QUERIES, dtype=jnp.int32)
    d_cache, outs = lax.scan(one_query, start, (qfull, d_olat, sel, rows))
    olat, d_qlat, d_q_rope = outs
    attn_out = jnp.einsum('qhl,hlv->qhv', olat.astype(jnp.float32), weight_v).astype(jnp.bfloat16)
    d_q_nope = jnp.einsum('qhl,hnl->qhn', d_qlat.astype(jnp.float32), weight_k).astype(jnp.bfloat16)
    return (attn_out, d_q_nope, d_q_rope, d_cache)
```

```python
import functools
import math

import jax
import jax.numpy as jnp
from jax import lax
from jax.experimental import pallas as pl
from jax.experimental.pallas import tpu as pltpu
from jax.sharding import PartitionSpec as P

BLOCK_LEN = 64
LANES = 128
HIDDEN = -1e30
VMEM = pl.BlockSpec(memory_space=pltpu.VMEM)
SMEM = pl.BlockSpec(memory_space=pltpu.SMEM)
F32 = jnp.float32
BF16 = jnp.bfloat16


def params(mib):
    return pltpu.CompilerParams(vmem_limit_bytes=mib * 2**20)


def nt(a, b):
    return lax.dot_general(a, b, (((1,), (1,)), ((), ())), preferred_element_type=F32)


def nn(a, b):
    return lax.dot_general(a, b, (((1,), (0,)), ((), ())), preferred_element_type=F32)


def tn(a, b):
    return lax.dot_general(a, b, (((0,), (0,)), ((), ())), preferred_element_type=F32)


def seq_swap(x):
    return lax.all_to_all(x, "seq", split_axis=0, concat_axis=0, tiled=True)


def grp_swap(x, bit):
    n = lax.axis_size("grp")
    return lax.ppermute(x, "grp", [(i, i ^ bit) for i in range(n)])


def weight_k_of(pack, head, uk_rows, tiles):
    rows = uk_rows // tiles
    peers = pack.shape[0]
    cols = []
    for t in range(tiles):
        cols.append(
            jnp.concatenate(
                [pack[r, head, t * rows : (t + 1) * rows, :] for r in range(peers)], axis=0
            )
        )
    return jnp.concatenate(cols, axis=1)


def stacked(pack, head, start, rows):
    peers = pack.shape[0]
    return jnp.concatenate([pack[r, head, start : start + rows, :] for r in range(peers)], axis=0)


def expand_kernel(sizes, pack, out):
    uk_rows, uv_rows, queries, tiles, latent = sizes
    peers, heads = pack.shape[0], pack.shape[1]
    for h in range(heads):
        wk = weight_k_of(pack, h, uk_rows, tiles)
        wv = stacked(pack, h, uk_rows, uv_rows)
        qn = stacked(pack, h, uk_rows + uv_rows, queries)
        do = stacked(pack, h, uk_rows + uv_rows + queries, queries)
        q_lat = nn(qn, wk).astype(BF16)
        d_olat = nt(do, wv).astype(BF16)
        for r in range(peers):
            out[r, h, :, :latent] = q_lat[r * queries : (r + 1) * queries]
            out[r, h, :, latent:] = d_olat[r * queries : (r + 1) * queries]


def reduce_kernel(sizes, pack, lat, out):
    uk_rows, uv_rows, queries, tiles, latent = sizes
    peers, heads = pack.shape[0], pack.shape[1]
    for h in range(heads):
        wk = weight_k_of(pack, h, uk_rows, tiles)
        wv = stacked(pack, h, uk_rows, uv_rows)
        both = jnp.concatenate([lat[r, h] for r in range(peers)], axis=0)
        attn = nn(both[:, :latent], wv).astype(BF16)
        dqn = nt(both[:, latent:], wk).astype(BF16)
        for r in range(peers):
            out[r, h, :, : attn.shape[1]] = attn[r * queries : (r + 1) * queries]
            out[r, h, :, attn.shape[1] :] = dqn[r * queries : (r + 1) * queries]


def attend_kernel(scale, qd, rope, bias, *refs):
    parts = 4
    keys, refs = refs[:parts], refs[parts:]
    out, d_rope, refs = refs[0], refs[1], refs[2:]
    dkeys, refs = refs[:parts], refs[parts:]
    qf, cat, sc, dp, o_acc, q_acc = refs
    rows, width = qf.shape
    slots, part_len, _ = keys[0].shape
    latent = width - rope.shape[1]
    step = min(slots, 32)
    tokens = step * part_len
    qf[:, :latent] = qd[:, :latent]
    qf[:, latent:] = rope[...]
    cat[:rows] = qd[:, :latent]
    cat[rows:] = qd[:, latent:]
    chunks = [(p, c) for p in range(parts) for c in range(0, slots, step)]
    scale2 = scale * math.log2(math.e)

    top = jnp.full((1, rows), -jnp.inf, F32)
    for i, (p, c) in enumerate(chunks):
        k = keys[p][c : c + step].reshape(tokens, width)
        s = nt(k, qf[...]) * scale2
        b = jnp.broadcast_to(bias[c : c + step][:, None, :], (step, part_len, rows))
        s = s + b.reshape(tokens, rows)
        sc[pl.ds(i * tokens, tokens), :] = s
        dp[pl.ds(i * tokens, tokens), :] = nt(k[:, :latent], cat[rows:])
        top = jnp.maximum(top, jnp.max(s, axis=0, keepdims=True))

    total = jnp.zeros((1, rows), F32)
    inner = jnp.zeros((1, rows), F32)
    for i in range(len(chunks)):
        e = jnp.exp2(sc[pl.ds(i * tokens, tokens), :] - top)
        sc[pl.ds(i * tokens, tokens), :] = e
        total = total + jnp.sum(e, axis=0, keepdims=True)
        inner = inner + jnp.sum(e * dp[pl.ds(i * tokens, tokens), :], axis=0, keepdims=True)
    inv = 1.0 / total
    delta = inner * inv

    for i, (p, c) in enumerate(chunks):
        k = keys[p][c : c + step].reshape(tokens, width)
        prob = sc[pl.ds(i * tokens, tokens), :] * inv
        pb = prob.astype(BF16)
        ds = (prob * (dp[pl.ds(i * tokens, tokens), :] - delta) * scale).astype(BF16)
        o_part = tn(k[:, :latent], pb)
        q_part = tn(k, ds)
        if i == 0:
            o_acc[...] = o_part
            q_acc[...] = q_part
        else:
            o_acc[...] += o_part
            q_acc[...] += q_part
        both = jnp.concatenate([ds, pb], axis=1)
        dkeys[p][c : c + step, :, :latent] = (
            nn(both, cat[...]).astype(BF16).reshape(step, part_len, latent)
        )
        dkeys[p][c : c + step, :, latent:] = (
            nn(ds, rope[...]).astype(BF16).reshape(step, part_len, width - latent)
        )

    out[:, :latent] = o_acc[...].T.astype(BF16)
    out[:, latent:] = q_acc[:latent].T.astype(BF16)
    d_rope[...] = q_acc[latent:].T.astype(BF16)


def attend(scale, qd, rope, bias, keys):
    rows = qd.shape[0]
    slots, part_len, width = keys[0].shape
    latent = width - rope.shape[1]
    tokens = len(keys) * slots * part_len
    outs = pl.pallas_call(
        functools.partial(attend_kernel, scale),
        out_shape=[
            jax.ShapeDtypeStruct((rows, 2 * latent), BF16),
            jax.ShapeDtypeStruct(rope.shape, BF16),
        ]
        + [jax.ShapeDtypeStruct(k.shape, BF16) for k in keys],
        in_specs=[VMEM] * (3 + len(keys)),
        out_specs=[VMEM] * (2 + len(keys)),
        scratch_shapes=[
            pltpu.VMEM((rows, width), BF16),
            pltpu.VMEM((2 * rows, latent), BF16),
            pltpu.VMEM((tokens, rows), F32),
            pltpu.VMEM((tokens, rows), F32),
            pltpu.VMEM((latent, rows), F32),
            pltpu.VMEM((width, rows), F32),
        ],
        compiler_params=params(56),
        name="attend",
    )(qd, rope, bias, *keys)
    return outs[0], outs[1], outs[2:]


def scatter_kernel(asked, got, out, acc):
    acc[...] = jnp.zeros_like(acc)
    for s in range(got.shape[0]):
        b = asked[s]
        acc[b] = acc[b] + got[s].astype(F32)
    out[...] = acc[...].astype(BF16)


def assemble_kernel(place, y0, y1, y2, y3, out):
    for k, y in enumerate((y0, y1, y2, y3)):
        out[:, place[k]] = y[...].astype(F32)


def local(q_nope, q_rope, cache, w_uk, w_uv, d_out, sel, slot_blocks):
    peers = lax.axis_size("seq")
    groups = lax.axis_size("grp")
    me = lax.axis_index("grp")
    queries, heads, nope = q_nope.shape
    rope = q_rope.shape[2]
    width = cache.shape[1]
    latent = width - rope
    value = d_out.shape[2]
    slot_total = slot_blocks.shape[1]
    per_peer = slot_total // peers
    own_blocks = cache.shape[0] // BLOCK_LEN
    part_len = BLOCK_LEN // groups
    rows = heads * queries
    scale = 1.0 / math.sqrt(nope + rope)

    asked = seq_swap(slot_blocks.reshape(peers, per_peer)).reshape(-1)
    pieces = cache.reshape(own_blocks * groups, part_len, width)
    mine = pieces[asked * groups + me]
    qn = q_nope.transpose(1, 0, 2)
    do = d_out.transpose(1, 0, 2)
    head_form = heads % peers == 0
    if head_form:
        tiles = latent // LANES
        n_rows = w_uk.shape[1] // latent
        uv_rows = w_uv.shape[1] // value
        uk = w_uk.reshape(heads, n_rows, tiles, LANES).transpose(0, 2, 1, 3)
        pack = jnp.concatenate(
            [uk.reshape(heads, n_rows * tiles, LANES), w_uv.reshape(heads, uv_rows, value), qn, do],
            axis=1,
        )
        pack = seq_swap(pack).reshape(peers, heads // peers, -1, LANES)
        sizes = (n_rows * tiles, uv_rows, queries, tiles, latent)
        lat = pl.pallas_call(
            functools.partial(expand_kernel, sizes),
            out_shape=jax.ShapeDtypeStruct((peers, heads // peers, queries, 2 * latent), BF16),
            in_specs=[VMEM],
            out_specs=VMEM,
            compiler_params=params(32),
            name="expand",
        )(pack)
        qd = seq_swap(lat).reshape(rows, 2 * latent)
    else:
        weight_k = lax.all_gather(w_uk, "seq", axis=1, tiled=True).reshape(heads, nope, latent)
        weight_v = lax.all_gather(w_uv, "seq", axis=1, tiled=True).reshape(heads, latent, value)
        q_lat = jnp.einsum("hqn,hnl->hql", qn, weight_k, preferred_element_type=F32).astype(BF16)
        d_olat = jnp.einsum("hqv,hlv->hql", do, weight_v, preferred_element_type=F32).astype(BF16)
        qd = jnp.concatenate([q_lat, d_olat], axis=-1).reshape(rows, 2 * latent)

    k0 = seq_swap(mine.reshape(peers, per_peer * part_len, width)).reshape(
        slot_total, part_len, width
    )
    k2 = grp_swap(k0, 2)
    k1 = grp_swap(k0, 1)
    k3 = grp_swap(k2, 1)

    chosen = jnp.any(
        sel[None, :, :] == jnp.arange(slot_total, dtype=jnp.int32)[:, None, None], axis=2
    )
    bias = jnp.where(chosen, 0.0, HIDDEN).astype(F32)
    bias = jnp.broadcast_to(bias[:, None, :], (slot_total, heads, queries)).reshape(
        slot_total, rows
    )
    rope_rows = q_rope.transpose(1, 0, 2).reshape(rows, rope)
    lat, d_rope, dk = attend(scale, qd, rope_rows, bias, (k0, k1, k2, k3))

    a2 = (dk[2].astype(F32) + grp_swap(dk[3], 1).astype(F32)).astype(BF16)
    a0 = (dk[0].astype(F32) + grp_swap(dk[1], 1).astype(F32)).astype(BF16)
    a0 = (a0.astype(F32) + grp_swap(a2, 2).astype(F32)).astype(BF16)
    got = seq_swap(a0.reshape(peers, per_peer * part_len, width)).reshape(
        slot_total, part_len, width
    )

    if head_form:
        lat = seq_swap(lat.reshape(peers, heads // peers, queries, 2 * latent))
        res = pl.pallas_call(
            functools.partial(reduce_kernel, sizes),
            out_shape=jax.ShapeDtypeStruct((peers, heads // peers, queries, value + nope), BF16),
            in_specs=[VMEM, VMEM],
            out_specs=VMEM,
            compiler_params=params(32),
            name="reduce",
        )(pack, lat)
        res = seq_swap(res).reshape(heads, queries, value + nope)
        attn_out, d_q_nope = res[:, :, :value], res[:, :, value:]
    else:
        lat = lat.reshape(heads, queries, 2 * latent)
        attn_out = jnp.einsum(
            "hql,hlv->hqv", lat[:, :, :latent], weight_v, preferred_element_type=F32
        ).astype(BF16)
        d_q_nope = jnp.einsum(
            "hql,hnl->hqn", lat[:, :, latent:], weight_k, preferred_element_type=F32
        ).astype(BF16)

    y0 = pl.pallas_call(
        scatter_kernel,
        out_shape=jax.ShapeDtypeStruct((own_blocks, part_len, width), BF16),
        in_specs=[SMEM, VMEM],
        out_specs=VMEM,
        scratch_shapes=[pltpu.VMEM((own_blocks, part_len, width), F32)],
        compiler_params=params(16),
        name="scatter",
    )(asked, got)
    y2 = grp_swap(y0, 2)
    y1 = grp_swap(y0, 1)
    y3 = grp_swap(y2, 1)
    place = jnp.bitwise_xor(me, jnp.arange(4, dtype=jnp.int32))
    d_cache = pl.pallas_call(
        assemble_kernel,
        out_shape=jax.ShapeDtypeStruct((own_blocks, groups, part_len, width), F32),
        in_specs=[SMEM, VMEM, VMEM, VMEM, VMEM],
        out_specs=VMEM,
        compiler_params=params(16),
        name="assemble",
    )(place, y0, y1, y2, y3).reshape(own_blocks * BLOCK_LEN, width)
    return (
        attn_out.transpose(1, 0, 2),
        d_q_nope.transpose(1, 0, 2),
        d_rope.reshape(heads, queries, rope).transpose(1, 0, 2),
        d_cache,
    )


def solution(mesh):
    return jax.shard_map(
        local,
        mesh=mesh,
        in_specs=(
            P("seq", "grp", None),
            P("seq", "grp", None),
            P("seq", None),
            P("grp", "seq"),
            P("grp", "seq"),
            P("seq", "grp", None),
            P("seq", None),
            P("seq", None),
        ),
        out_specs=(
            P("seq", "grp", None),
            P("seq", "grp", None),
            P("seq", "grp", None),
            P("seq", None),
        ),
        check_vma=False,
    )
```

```python
import functools
import math

import jax
import jax.numpy as jnp
from jax import lax
from jax.experimental import pallas as pl
from jax.experimental.pallas import tpu as pltpu
from jax.sharding import PartitionSpec as P

BLOCK_LEN = 64
LANES = 128
HIDDEN = -1e30
SPAN = 4
VMEM = pl.BlockSpec(memory_space=pltpu.VMEM)
SMEM = pl.BlockSpec(memory_space=pltpu.SMEM)
ANY = pl.BlockSpec(memory_space=pl.ANY)
F32 = jnp.float32
BF16 = jnp.bfloat16


def call(kernel, name, args, specs, outs, scratch=(), mib=32):
    return pl.pallas_call(
        kernel,
        out_shape=[jax.ShapeDtypeStruct(s, d) for s, d in outs],
        in_specs=specs,
        out_specs=[VMEM] * len(outs),
        scratch_shapes=list(scratch),
        compiler_params=pltpu.CompilerParams(vmem_limit_bytes=mib * 2**20),
        name=name,
    )(*args)


def nt(a, b):
    return lax.dot_general(a, b, (((1,), (1,)), ((), ())), preferred_element_type=F32)


def nn(a, b):
    return lax.dot_general(a, b, (((1,), (0,)), ((), ())), preferred_element_type=F32)


def swap(x, axis, bit):
    n = lax.axis_size(axis)
    return lax.ppermute(x, axis, [(i, i ^ bit) for i in range(n)])


def exchange(pieces):
    return [pieces[0]] + [swap(p, "seq", k) for k, p in enumerate(pieces) if k > 0]


def gather_kernel(count, ids, *refs):
    rows, cache, outs = refs[:count], refs[count], refs[count + 1 :]
    me, grp = ids[0], ids[1]
    depth, lanes = outs[0].shape
    per_peer = lanes // BLOCK_LEN
    part = pl.ds(pl.multiple_of(grp * depth, 16), depth)

    def block(k, j):
        b = rows[k][0, me * per_peer + j]
        tile = cache[part, pl.ds(pl.multiple_of((b >> 1) * LANES, LANES), LANES)]
        return jnp.where((b & 1) == 1, tile[:, BLOCK_LEN:], tile[:, :BLOCK_LEN])

    for k in range(count):
        for j in range(0, per_peer, 2):
            both = jnp.concatenate([block(k, j), block(k, j + 1)], axis=1)
            outs[k][:, j * BLOCK_LEN : (j + 2) * BLOCK_LEN] = both


def scatter_kernel(count, ids, *refs):
    rows, got, out, acc = refs[:count], refs[count : 2 * count], refs[2 * count], refs[2 * count + 1]
    me = ids[0]
    depth, lanes = got[0].shape
    per_peer = lanes // BLOCK_LEN
    acc[...] = jnp.zeros_like(acc)
    blank = jnp.zeros((depth, BLOCK_LEN), F32)
    for k in range(count):
        for j in range(per_peer):
            b = rows[k][0, me * per_peer + j]
            at = pl.ds(pl.multiple_of((b >> 1) * LANES, LANES), LANES)
            g = got[k][:, j * BLOCK_LEN : (j + 1) * BLOCK_LEN].astype(F32)
            low = jnp.concatenate([g, blank], axis=1)
            high = jnp.concatenate([blank, g], axis=1)
            acc[:, at] = acc[:, at] + jnp.where((b & 1) == 1, high, low)
    out[...] = acc[...].astype(BF16)


def assemble_kernel(ids, *refs):
    parts, out = refs[:-1], refs[-1]
    depth = parts[0].shape[0]
    for k, y in enumerate(parts):
        out[pl.ds(pl.multiple_of((ids[1] ^ k) * depth, 16), depth), :] = y[...].astype(F32)


def pack_kernel(span, ids, weight, vec, *refs):
    outs = refs[-lax.axis_size("seq") :]
    share = weight.shape[0] // span
    rows = weight.shape[1]
    for k, out in enumerate(outs):
        at = pl.ds(((ids[0] ^ k) & (span - 1)) * share, share)
        out[:, :rows] = weight[at]
        if k < span:
            out[:, rows:] = vec[at]


def expand_k_kernel(span, queries, ids, *refs):
    peers = lax.axis_size("seq")
    got, outs, whole = refs[:peers], refs[peers : peers + span], refs[peers + span]
    share, nope, latent = whole.shape
    n_rows = nope // peers
    tiles = latent // LANES
    for h in range(share):
        for k in range(peers):
            at = pl.ds(pl.multiple_of((ids[0] ^ k) * n_rows, 16), n_rows)
            for t in range(tiles):
                whole[h, at, t * LANES : (t + 1) * LANES] = got[k][h, t * n_rows : (t + 1) * n_rows]
        q = jnp.concatenate([got[k][h, n_rows * tiles :] for k in range(span)], axis=0)
        res = nn(q, whole[h]).astype(BF16)
        for k in range(span):
            outs[k][h] = res[k * queries : (k + 1) * queries]


def expand_v_kernel(span, queries, ids, *refs):
    peers = lax.axis_size("seq")
    got, outs, whole = refs[:peers], refs[peers : peers + span], refs[peers + span]
    share, latent, value = whole.shape
    l_rows = latent // peers
    for h in range(share):
        for k in range(peers):
            at = pl.ds(pl.multiple_of((ids[0] ^ k) * l_rows, 16), l_rows)
            whole[h, at, :] = got[k][h, :l_rows]
        d = jnp.concatenate([got[k][h, l_rows:] for k in range(span)], axis=0)
        res = nt(d, whole[h]).astype(BF16)
        for k in range(span):
            outs[k][h] = res[k * queries : (k + 1) * queries]


def reduce_kernel(span, queries, wk, wv, *refs):
    o, d, outs = refs[:span], refs[span : 2 * span], refs[2 * span :]
    value = wv.shape[2]
    for h in range(wk.shape[0]):
        attn = nn(jnp.concatenate([o[k][h] for k in range(span)], axis=0), wv[h]).astype(BF16)
        dqn = nt(jnp.concatenate([d[k][h] for k in range(span)], axis=0), wk[h]).astype(BF16)
        for k in range(span):
            outs[k][h, :, :value] = attn[k * queries : (k + 1) * queries]
            outs[k][h, :, value:] = dqn[k * queries : (k + 1) * queries]


def place_kernel(span, ids, *refs):
    got, attn, dqn = refs[:span], refs[span], refs[span + 1]
    value = attn.shape[2]
    share = got[0].shape[0]
    for k in range(span):
        at = pl.ds(((ids[0] ^ k) & (span - 1)) * share, share)
        attn[at] = got[k][:, :, :value]
        dqn[at] = got[k][:, :, value:]


def rope_at(ids, k, span, share):
    return pl.ds(((ids[0] ^ k) & (span - 1)) * share, share)


def forward_kernel(scale, span, per_peer, ids, sel, rope, *refs):
    q_lat, refs = refs[:span], refs[span:]
    keys, refs = (refs[:4], refs[4:8]), refs[8:]
    kts, pbs, refs = refs[:2], refs[2:4], refs[4:]
    o_out, o_full, qx, sc = refs[:span], refs[span], refs[span + 1], refs[span + 2]
    share, queries, latent = q_lat[0].shape
    rope_dim = rope.shape[2]
    width = latent + rope_dim
    span_rows = share * queries
    rows = span * span_rows
    slots = qx.shape[1] - width
    held, depth, lanes = keys[0][0].shape
    half = held * lanes

    picks = sel[...] ^ (ids[0] * per_peer)
    slot = lax.broadcasted_iota(jnp.int32, (queries, slots), 1)
    chosen = picks[:, 0:1] == slot
    for j in range(1, picks.shape[1]):
        chosen = chosen | (picks[:, j : j + 1] == slot)
    bias = jnp.where(chosen, 0.0, HIDDEN).astype(BF16)
    bias = jnp.broadcast_to(bias[None], (share, queries, slots)).reshape(span_rows, slots)
    for k in range(span):
        at = slice(k * span_rows, (k + 1) * span_rows)
        qx[at, :latent] = q_lat[k][...].reshape(span_rows, latent)
        tail = rope[rope_at(ids, k, span, share)].reshape(span_rows, rope_dim)
        qx[at, latent:] = jnp.concatenate([tail, bias], axis=1)
    for c in range(2):
        for k in range(4):
            at = pl.ds(pl.multiple_of((ids[1] ^ k) * depth, 16), depth)
            for i in range(held):
                kts[c][at, i * lanes : (i + 1) * lanes] = keys[c][k][i]
        place = lax.broadcasted_iota(jnp.int32, (slots, half), 0)
        token = lax.broadcasted_iota(jnp.int32, (slots, half), 1) + c * half
        kts[c][width:, :] = jnp.where(token // BLOCK_LEN == place, 1.0, 0.0).astype(BF16)

    scale2 = scale * math.log2(math.e)
    step = 512
    chunks = [(c, i) for c in range(2) for i in range(0, half, step)]
    top = jnp.full((rows, 1), -jnp.inf, F32)
    for n, (c, i) in enumerate(chunks):
        s = nn(qx[...], kts[c][:, i : i + step]) * scale2
        sc[:, n * step : (n + 1) * step] = s
        top = jnp.maximum(top, jnp.max(s, axis=1, keepdims=True))
    total = jnp.zeros((rows, 1), F32)
    for n in range(len(chunks)):
        e = jnp.exp2(sc[:, n * step : (n + 1) * step] - top)
        sc[:, n * step : (n + 1) * step] = e
        total = total + jnp.sum(e, axis=1, keepdims=True)
    inv = 1.0 / total
    for n, (c, i) in enumerate(chunks):
        pb = (sc[:, n * step : (n + 1) * step] * inv).astype(BF16)
        pbs[c][:, i : i + step] = pb
        part = nt(pb, kts[c][:latent, i : i + step])
        if n == 0:
            o_full[...] = part
        else:
            o_full[...] += part
    for k in range(span):
        o = o_full[k * span_rows : (k + 1) * span_rows].astype(BF16)
        o_out[k][...] = o.reshape(share, queries, latent)


def backward_kernel(scale, span, first, ids, rope, o_full, kt, pb, *refs):
    q_lat, refs = refs[:span], refs[span:]
    d_olat, refs = refs[:span], refs[span:]
    if not first:
        before, refs = refs[0], refs[1:]
    send, keep, refs = refs[0], refs[1], refs[2:]
    if first:
        dq, refs = refs[0], refs[1:]
    else:
        d_lat, d_rope, refs = refs[:span], refs[span], refs[span + 1 :]
    qf, do, flip, cat = refs[:4]
    if not first:
        dq = refs[4]
    share, queries, latent = q_lat[0].shape
    rope_dim = rope.shape[2]
    width = latent + rope_dim
    span_rows = share * queries
    rows = span * span_rows
    depth = width // 4
    for k in range(span):
        at = slice(k * span_rows, (k + 1) * span_rows)
        qf[at, :latent] = q_lat[k][...].reshape(span_rows, latent)
        qf[at, latent:] = rope[rope_at(ids, k, span, share)].reshape(span_rows, rope_dim)
        do[at, :] = d_olat[k][...].reshape(span_rows, latent)
    flip[:, :rows] = qf[...].T
    flip[:latent, rows:] = do[...].T
    flip[latent:, rows:] = jnp.zeros((rope_dim, rows), BF16)
    for k in range(4):
        at = pl.ds(pl.multiple_of((ids[1] ^ k) * depth, 16), depth)
        cat[k * depth : (k + 1) * depth] = flip[at, :]
    delta = jnp.sum(o_full[...] * do[...].astype(F32), axis=1, keepdims=True)
    step = 512
    for n, i in enumerate(range(0, pb.shape[1], step)):
        at = slice(i, i + step)
        p = pb[:, at]
        dp = nn(do[...], kt[:latent, at])
        ds = (p.astype(F32) * (dp - delta) * scale).astype(BF16)
        part = nt(ds, kt[:width, at])
        if n > 0:
            dq[...] += part
        elif first:
            dq[...] = part
        else:
            dq[...] = before[...] + part
        dk = nn(cat[...], jnp.concatenate([ds, p], axis=0)).astype(BF16)
        for k, ref in enumerate((keep, send, keep, send)):
            ref[k // 2, :, at] = dk[k * depth : (k + 1) * depth]
    if not first:
        for k in range(span):
            at = slice(k * span_rows, (k + 1) * span_rows)
            d_lat[k][...] = dq[at, :latent].astype(BF16).reshape(share, queries, latent)
            d_rope[rope_at(ids, k, span, share)] = (
                dq[at, latent:].astype(BF16).reshape(share, queries, rope_dim)
            )


def pair_kernel(keep, got, a0, *a2):
    total = keep[...].astype(F32) + got[...].astype(F32)
    a0[...] = total[0].astype(BF16)
    lanes = a2[0].shape[1]
    for i, a in enumerate(a2):
        a[...] = total[1, :, i * lanes : (i + 1) * lanes].astype(BF16)


def owner_kernel(a0, got, *outs):
    total = (a0[...].astype(F32) + got[...].astype(F32)).astype(BF16)
    lanes = outs[0].shape[1]
    for i, out in enumerate(outs):
        out[...] = total[:, i * lanes : (i + 1) * lanes]


def local(q_nope, q_rope, cache, w_uk, w_uv, d_out, sel, slot_blocks):
    peers = lax.axis_size("seq")
    groups = lax.axis_size("grp")
    queries, heads, nope = q_nope.shape
    rope = q_rope.shape[2]
    width = cache.shape[1]
    latent = width - rope
    value = d_out.shape[2]
    slots = slot_blocks.shape[1]
    per_peer = slots // peers
    if not (peers == 8 and groups == 4 and heads % SPAN == 0 and per_peer % 2 == 0):
        return local_general(q_nope, q_rope, cache, w_uk, w_uv, d_out, sel, slot_blocks)
    ids = jnp.stack([lax.axis_index("seq"), lax.axis_index("grp")]).astype(jnp.int32)
    tokens = cache.shape[0]
    depth = width // groups
    lanes = per_peer * BLOCK_LEN
    held = peers // 2
    half = held * lanes
    share = heads // SPAN
    rows = heads * queries
    scale = 1.0 / math.sqrt(nope + rope)

    asked = exchange([slot_blocks] * peers)
    mine = call(
        functools.partial(gather_kernel, peers),
        "gather",
        (ids, *asked, cache.T),
        [SMEM] * (1 + peers) + [VMEM],
        [((depth, lanes), BF16)] * peers,
    )
    arrived = exchange(mine)
    keys = []
    for c in range(2):
        k0 = jnp.stack(arrived[c * held : (c + 1) * held])
        k2 = swap(k0, "grp", 2)
        k1 = swap(k0, "grp", 1)
        k3 = swap(k2, "grp", 1)
        keys.append((k0, k1, k2, k3))

    n_rows = w_uk.shape[1] // latent
    l_rows = w_uv.shape[1] // value
    tiles = latent // LANES
    uk = w_uk.reshape(heads, n_rows, tiles, LANES).transpose(0, 2, 1, 3)
    uk = uk.reshape(heads, n_rows * tiles, LANES)
    uv = w_uv.reshape(heads, l_rows, value)

    def pieces(w_rows):
        return [
            ((share, w_rows + (queries if k < SPAN else 0), LANES), BF16) for k in range(peers)
        ]

    lat_shape = ((share, queries, latent), BF16)
    packed = call(
        functools.partial(pack_kernel, SPAN),
        "pack_k",
        (ids, uk, q_nope.transpose(1, 0, 2)),
        [SMEM, VMEM, VMEM],
        pieces(n_rows * tiles),
    )
    *q_lat, wk = call(
        functools.partial(expand_k_kernel, SPAN, queries),
        "expand_k",
        (ids, *exchange(packed)),
        [SMEM] + [VMEM] * peers,
        [lat_shape] * SPAN + [((share, nope, latent), BF16)],
    )
    packed = call(
        functools.partial(pack_kernel, SPAN),
        "pack_v",
        (ids, uv, d_out.transpose(1, 0, 2), wk),
        [SMEM, VMEM, VMEM, ANY],
        pieces(l_rows),
    )
    q_lat = exchange(q_lat)
    *d_olat, wv = call(
        functools.partial(expand_v_kernel, SPAN, queries),
        "expand_v",
        (ids, *exchange(packed)),
        [SMEM] + [VMEM] * peers,
        [lat_shape] * SPAN + [((share, latent, value), BF16)],
    )
    d_olat = exchange(d_olat)

    rope_rows = q_rope.transpose(1, 0, 2)
    kt0, kt1, pb0, pb1, *o_lat, o_full = call(
        functools.partial(forward_kernel, scale, SPAN, per_peer),
        "forward",
        (ids, sel, rope_rows, *q_lat, *keys[0], *keys[1]),
        [SMEM] + [VMEM] * (2 + SPAN + 8),
        [((width + slots, half), BF16)] * 2
        + [((rows, half), BF16)] * 2
        + [lat_shape] * SPAN
        + [((rows, latent), F32)],
        [pltpu.VMEM((rows, width + slots), BF16), pltpu.VMEM((rows, 2 * half), F32)],
        48,
    )
    o_lat = exchange(o_lat)

    def backward(kt, pb, before):
        first = before is None
        outs = [((2, depth, half), BF16)] * 2
        scratch = [
            pltpu.VMEM((rows, width), BF16),
            pltpu.VMEM((rows, latent), BF16),
            pltpu.VMEM((width, 2 * rows), BF16),
            pltpu.VMEM((width, 2 * rows), BF16),
        ]
        if first:
            outs = outs + [((rows, width), F32)]
        else:
            outs = outs + [lat_shape] * SPAN + [((heads, queries, rope), BF16)]
            scratch = scratch + [pltpu.VMEM((rows, width), F32)]
        args = (ids, rope_rows, o_full, kt, pb, *q_lat, *d_olat) + (() if first else (before,))
        return call(
            functools.partial(backward_kernel, scale, SPAN, first),
            "backward_far" if first else "backward_near",
            args,
            [SMEM] + [VMEM] * (len(args) - 1),
            outs,
            scratch,
            40,
        )

    def give(send, keep, splits):
        got = swap(send, "grp", 1)
        a0, *a2 = call(
            pair_kernel,
            "pair",
            (keep, got),
            [VMEM, VMEM],
            [((depth, half), BF16)] + [((depth, half // splits), BF16)] * splits,
        )
        out = []
        for i, a in enumerate(a2):
            size = half // splits
            out += call(
                owner_kernel,
                "owner",
                (a0[:, i * size : (i + 1) * size], swap(a, "grp", 2)),
                [VMEM, VMEM],
                [((depth, lanes), BF16)] * (size // lanes),
            )
        return out

    send, keep, dq = backward(kt1, pb1, None)
    far = give(send, keep, 2)
    send, keep, *rest = backward(kt0, pb0, dq)
    near = give(send, keep, 1)
    d_lat, d_rope = exchange(rest[:SPAN]), rest[SPAN]
    got = exchange(near + far)

    res = call(
        functools.partial(reduce_kernel, SPAN, queries),
        "reduce",
        (wk, wv, *o_lat, *d_lat),
        [VMEM] * (2 + 2 * SPAN),
        [((share, queries, value + nope), BF16)] * SPAN,
    )
    attn_out, d_q_nope = call(
        functools.partial(place_kernel, SPAN),
        "place",
        (ids, *exchange(res)),
        [SMEM] + [VMEM] * SPAN,
        [((heads, queries, value), BF16), ((heads, queries, nope), BF16)],
    )

    (y0,) = call(
        functools.partial(scatter_kernel, peers),
        "scatter",
        (ids, *asked, *got),
        [SMEM] * (1 + peers) + [VMEM] * peers,
        [((depth, tokens), BF16)],
        [pltpu.VMEM((depth, tokens), F32)],
    )
    y2 = swap(y0, "grp", 2)
    y1 = swap(y0, "grp", 1)
    y3 = swap(y2, "grp", 1)
    (d_cache,) = call(
        assemble_kernel,
        "assemble",
        (ids, y0, y1, y2, y3),
        [SMEM] + [VMEM] * 4,
        [((width, tokens), F32)],
    )
    return (
        attn_out.transpose(1, 0, 2),
        d_q_nope.transpose(1, 0, 2),
        d_rope.transpose(1, 0, 2),
        d_cache.T,
    )


def local_general(q_nope, q_rope, cache, w_uk, w_uv, d_out, sel, slot_blocks):
    peers = lax.axis_size("seq")
    queries, heads, nope = q_nope.shape
    rope = q_rope.shape[2]
    width = cache.shape[1]
    latent = width - rope
    value = d_out.shape[2]
    slot_total = slot_blocks.shape[1]
    per_peer = slot_total // peers
    own_blocks = cache.shape[0] // BLOCK_LEN
    scale = 1.0 / math.sqrt(nope + rope)
    gathered_k, gathered_v = (
        lax.all_gather(w_uk, "seq", axis=1, tiled=True),
        lax.all_gather(w_uv, "seq", axis=1, tiled=True),
    )
    weight_k = gathered_k.reshape(heads, nope, latent)
    weight_v = gathered_v.reshape(heads, latent, value)
    wanted = slot_blocks.reshape(peers, per_peer)
    asked = lax.all_to_all(wanted, "seq", split_axis=0, concat_axis=0, tiled=True)
    blocks = cache.reshape(own_blocks, BLOCK_LEN, width)
    arrived = lax.all_to_all(blocks[asked], "seq", split_axis=0, concat_axis=0, tiled=True)
    keys = arrived.reshape(slot_total * BLOCK_LEN, width)
    keys_lat = keys[:, :latent]
    q_lat = jnp.einsum("qhn,hnl->qhl", q_nope, weight_k, preferred_element_type=jnp.float32).astype(
        jnp.bfloat16
    )
    qfull = jnp.concatenate([q_lat, q_rope], axis=-1)
    chosen = jnp.any(
        sel[:, :, None] == jnp.arange(slot_total, dtype=jnp.int32)[None, None, :], axis=1
    )
    live = jnp.repeat(chosen, BLOCK_LEN, axis=1)[:, None, :]
    score = jnp.einsum("qhc,tc->qht", qfull, keys, preferred_element_type=jnp.float32) * scale
    score = jnp.where(live, score, -jnp.inf)
    prob = jax.nn.softmax(score, axis=-1)
    prob_low = prob.astype(jnp.bfloat16)
    olat = jnp.einsum("qht,tl->qhl", prob_low, keys_lat, preferred_element_type=jnp.float32).astype(
        jnp.bfloat16
    )
    attn_out = jnp.einsum(
        "qhl,hlv->qhv", olat, weight_v, preferred_element_type=jnp.float32
    ).astype(jnp.bfloat16)
    d_olat = jnp.einsum("qhv,hlv->qhl", d_out, weight_v, preferred_element_type=jnp.float32).astype(
        jnp.bfloat16
    )
    dprob = jnp.einsum("qhl,tl->qht", d_olat, keys_lat, preferred_element_type=jnp.float32)
    delta = jnp.sum(prob * dprob, axis=-1, keepdims=True)
    dscore = (prob * (dprob - delta) * scale).astype(jnp.bfloat16)
    dquery = jnp.einsum("qht,tc->qhc", dscore, keys, preferred_element_type=jnp.float32)
    d_q_rope = dquery[:, :, latent:].astype(jnp.bfloat16)
    d_qlat = dquery[:, :, :latent].astype(jnp.bfloat16)
    d_q_nope = jnp.einsum(
        "qhl,hnl->qhn", d_qlat, weight_k, preferred_element_type=jnp.float32
    ).astype(jnp.bfloat16)
    value_part = jnp.einsum("qht,qhl->tl", prob_low, d_olat, preferred_element_type=jnp.float32)
    dkeys = jnp.einsum("qht,qhc->tc", dscore, qfull, preferred_element_type=jnp.float32)
    dkeys = dkeys + jnp.pad(value_part, ((0, 0), (0, rope)))
    one_hot = (
        asked.reshape(-1)[:, None] == jnp.arange(own_blocks, dtype=jnp.int32)[None, :]
    ).astype(jnp.float32)
    returned = lax.all_to_all(
        dkeys.reshape(peers, per_peer, BLOCK_LEN * width).astype(jnp.bfloat16),
        "seq",
        split_axis=0,
        concat_axis=0,
        tiled=True,
    ).astype(jnp.float32)
    local_grad = jnp.dot(
        one_hot.T,
        returned.reshape(peers * per_peer, BLOCK_LEN * width),
        precision=lax.Precision.HIGHEST,
    )
    d_cache = (
        lax.psum(local_grad.astype(jnp.bfloat16), "grp")
        .astype(jnp.float32)
        .reshape(own_blocks * BLOCK_LEN, width)
    )
    return (attn_out, d_q_nope, d_q_rope, d_cache)


def solution(mesh):
    return jax.shard_map(
        local,
        mesh=mesh,
        in_specs=(
            P("seq", "grp", None),
            P("seq", "grp", None),
            P("seq", None),
            P("grp", "seq"),
            P("grp", "seq"),
            P("seq", "grp", None),
            P("seq", None),
            P("seq", None),
        ),
        out_specs=(
            P("seq", "grp", None),
            P("seq", "grp", None),
            P("seq", "grp", None),
            P("seq", None),
        ),
        check_vma=False,
    )
```

```python
import functools
import math

import jax
import jax.numpy as jnp
from jax import lax
from jax.experimental import pallas as pl
from jax.experimental.pallas import tpu as pltpu
from jax.sharding import PartitionSpec as P

BLOCK_LEN = 64
LANES = 128
HIDDEN = -1e30
VMEM = pl.BlockSpec(memory_space=pltpu.VMEM)
SMEM = pl.BlockSpec(memory_space=pltpu.SMEM)
F32 = jnp.float32
BF16 = jnp.bfloat16


def call(kernel, name, args, specs, outs, scratch=(), mib=32):
    return pl.pallas_call(
        kernel,
        out_shape=[jax.ShapeDtypeStruct(s, d) for s, d in outs],
        in_specs=specs,
        out_specs=[VMEM] * len(outs),
        scratch_shapes=list(scratch),
        compiler_params=pltpu.CompilerParams(vmem_limit_bytes=mib * 2**20),
        name=name,
    )(*args)


def nt(a, b):
    return lax.dot_general(a, b, (((1,), (1,)), ((), ())), preferred_element_type=F32)


def nn(a, b):
    return lax.dot_general(a, b, (((1,), (0,)), ((), ())), preferred_element_type=F32)


def swap(x, axis, bit):
    n = lax.axis_size(axis)
    return lax.ppermute(x, axis, [(i, i ^ bit) for i in range(n)])


def seq_swap(x):
    return lax.all_to_all(x, "seq", split_axis=0, concat_axis=0, tiled=True)


def exchange(pieces):
    return [pieces[0]] + [swap(p, "seq", k) for k, p in enumerate(pieces) if k > 0]


def gather_kernel(count, ids, rows, cache, *outs):
    me, grp = ids[0], ids[1]
    depth, lanes = outs[0].shape
    per_peer = lanes // BLOCK_LEN
    part = pl.ds(pl.multiple_of(grp * depth, 16), depth)

    def block(k, j):
        b = rows[k, me * per_peer + j]
        tile = cache[part, pl.ds(pl.multiple_of((b >> 1) * LANES, LANES), LANES)]
        return jnp.where((b & 1) == 1, tile[:, BLOCK_LEN:], tile[:, :BLOCK_LEN])

    for k in range(count):
        for j in range(0, per_peer, 2):
            both = jnp.concatenate([block(k, j), block(k, j + 1)], axis=1)
            outs[k][:, j * BLOCK_LEN : (j + 2) * BLOCK_LEN] = both


def scatter_kernel(count, ids, rows, *refs):
    got, out, acc = refs[:count], refs[count], refs[count + 1]
    me = ids[0]
    depth, lanes = got[0].shape
    per_peer = lanes // BLOCK_LEN
    acc[...] = jnp.zeros_like(acc)
    blank = jnp.zeros((depth, BLOCK_LEN), F32)
    for k in range(count):
        for j in range(per_peer):
            b = rows[k, me * per_peer + j]
            at = pl.ds(pl.multiple_of((b >> 1) * LANES, LANES), LANES)
            g = got[k][:, j * BLOCK_LEN : (j + 1) * BLOCK_LEN].astype(F32)
            low = jnp.concatenate([g, blank], axis=1)
            high = jnp.concatenate([blank, g], axis=1)
            acc[:, at] = acc[:, at] + jnp.where((b & 1) == 1, high, low)
    out[...] = acc[...].astype(BF16)


def assemble_kernel(ids, *refs):
    parts, out = refs[:-1], refs[-1]
    depth = parts[0].shape[0]
    for k, y in enumerate(parts):
        out[pl.ds(pl.multiple_of((ids[1] ^ k) * depth, 16), depth), :] = y[...].astype(F32)


def weight_k_of(pack, head, uk_rows, tiles):
    rows = uk_rows // tiles
    peers = pack.shape[0]
    cols = []
    for t in range(tiles):
        cols.append(
            jnp.concatenate(
                [pack[r, head, t * rows : (t + 1) * rows, :] for r in range(peers)], axis=0
            )
        )
    return jnp.concatenate(cols, axis=1)


def stacked(pack, head, start, rows):
    peers = pack.shape[0]
    return jnp.concatenate([pack[r, head, start : start + rows, :] for r in range(peers)], axis=0)


def expand_kernel(sizes, pack, out):
    uk_rows, uv_rows, queries, tiles, latent = sizes
    peers, heads = pack.shape[0], pack.shape[1]
    for h in range(heads):
        wk = weight_k_of(pack, h, uk_rows, tiles)
        wv = stacked(pack, h, uk_rows, uv_rows)
        qn = stacked(pack, h, uk_rows + uv_rows, queries)
        do = stacked(pack, h, uk_rows + uv_rows + queries, queries)
        q_lat = nn(qn, wk).astype(BF16)
        d_olat = nt(do, wv).astype(BF16)
        for r in range(peers):
            out[r, h, :, :latent] = q_lat[r * queries : (r + 1) * queries]
            out[r, h, :, latent:] = d_olat[r * queries : (r + 1) * queries]


def reduce_kernel(sizes, pack, o_lat, d_lat, out):
    uk_rows, uv_rows, queries, tiles, latent = sizes
    peers, heads = pack.shape[0], pack.shape[1]
    for h in range(heads):
        wk = weight_k_of(pack, h, uk_rows, tiles)
        wv = stacked(pack, h, uk_rows, uv_rows)
        o = jnp.concatenate([o_lat[r, h] for r in range(peers)], axis=0)
        d = jnp.concatenate([d_lat[r, h] for r in range(peers)], axis=0)
        attn = nn(o, wv).astype(BF16)
        dqn = nt(d, wk).astype(BF16)
        for r in range(peers):
            out[r, h, :, : attn.shape[1]] = attn[r * queries : (r + 1) * queries]
            out[r, h, :, attn.shape[1] :] = dqn[r * queries : (r + 1) * queries]


def far_or_near(grads, scale, do, cat, delta, kt, p, width):
    keep, send, at, depth = grads
    latent = do.shape[1]
    dp = nn(do[...], kt[:latent])
    ds = (p.astype(F32) * (dp - delta) * scale).astype(BF16)
    part = nt(ds, kt[:width])
    dk = nn(cat[...], jnp.concatenate([ds, p], axis=0)).astype(BF16)
    for k, ref in enumerate((keep, send, keep, send)):
        ref[k // 2, :, at] = dk[k * depth : (k + 1) * depth]
    return part


def first_kernel(scale, per_peer, ids, sel, rope, qd, *refs):
    keys, refs = (refs[:4], refs[4:8]), refs[8:]
    kt_near, pb_near, cat, o_lat, delta_out, keep, send, dq, refs = (*refs[:8], refs[8:])
    kt_far, pb_far, qx, do, sc, flip, o_full = refs
    rows, latent = do.shape
    heads, queries, rope_dim = rope.shape
    width = latent + rope_dim
    slots = qx.shape[1] - width
    held, depth, lanes = keys[0][0].shape
    half = held * lanes
    kts, pbs = (kt_near, kt_far), (pb_near, pb_far)

    picks = sel[...] ^ (ids[0] * per_peer)
    slot = lax.broadcasted_iota(jnp.int32, (queries, slots), 1)
    chosen = picks[:, 0:1] == slot
    for j in range(1, picks.shape[1]):
        chosen = chosen | (picks[:, j : j + 1] == slot)
    bias = jnp.where(chosen, 0.0, HIDDEN).astype(BF16)
    bias = jnp.broadcast_to(bias[None], (heads, queries, slots)).reshape(rows, slots)
    qx[:, :latent] = qd[:, :latent]
    qx[:, latent:] = jnp.concatenate([rope[...].reshape(rows, rope_dim), bias], axis=1)
    do[...] = qd[:, latent:]
    for c in range(2):
        for k in range(4):
            at = pl.ds(pl.multiple_of((ids[1] ^ k) * depth, 16), depth)
            for i in range(held):
                kts[c][at, i * lanes : (i + 1) * lanes] = keys[c][k][i]
        place = lax.broadcasted_iota(jnp.int32, (slots, half), 0)
        token = lax.broadcasted_iota(jnp.int32, (slots, half), 1) + c * half
        kts[c][width:, :] = jnp.where(token // BLOCK_LEN == place, 1.0, 0.0).astype(BF16)

    scale2 = scale * math.log2(math.e)
    step = 512
    chunks = [(c, i) for c in range(2) for i in range(0, half, step)]
    top = jnp.full((rows, 1), -jnp.inf, F32)
    for n, (c, i) in enumerate(chunks):
        s = nn(qx[...], kts[c][:, i : i + step]) * scale2
        sc[:, n * step : (n + 1) * step] = s
        top = jnp.maximum(top, jnp.max(s, axis=1, keepdims=True))
    total = jnp.zeros((rows, 1), F32)
    for n in range(len(chunks)):
        e = jnp.exp2(sc[:, n * step : (n + 1) * step] - top)
        sc[:, n * step : (n + 1) * step] = e
        total = total + jnp.sum(e, axis=1, keepdims=True)
    inv = 1.0 / total
    for n, (c, i) in enumerate(chunks):
        pb = (sc[:, n * step : (n + 1) * step] * inv).astype(BF16)
        pbs[c][:, i : i + step] = pb
        part = nt(pb, kts[c][:latent, i : i + step])
        if n == 0:
            o_full[...] = part
        else:
            o_full[...] += part
    o_lat[...] = o_full[...].astype(BF16)
    delta = jnp.sum(o_full[...] * do[...].astype(F32), axis=1, keepdims=True)
    delta_out[...] = delta

    flip[:, :rows] = qx[:, :width].T
    flip[:latent, rows:] = do[...].T
    flip[latent:, rows:] = jnp.zeros((rope_dim, rows), BF16)
    for k in range(4):
        at = pl.ds(pl.multiple_of((ids[1] ^ k) * depth, 16), depth)
        cat[k * depth : (k + 1) * depth] = flip[at, :]
    for i in range(0, half, step):
        at = slice(i, i + step)
        grads = (keep, send, at, depth)
        part = far_or_near(grads, scale, do, cat, delta, kt_far.at[:, at], pb_far[:, at], width)
        if i == 0:
            dq[...] = part
        else:
            dq[...] += part


def second_kernel(scale, qd, cat, delta, kt, pb, before, keep, send, d_lat, d_rope, do, dq):
    rows, latent = do.shape
    width = cat.shape[0]
    depth = width // 4
    do[...] = qd[:, latent:]
    step = 512
    dq[...] = before[...]
    for i in range(0, pb.shape[1], step):
        at = slice(i, i + step)
        grads = (keep, send, at, depth)
        dq[...] += far_or_near(
            grads, scale, do, cat, delta[...], kt.at[:, at], pb[:, at], width
        )
    d_lat[...] = dq[:, :latent].astype(BF16)
    d_rope[...] = dq[:, latent:].astype(BF16)


def pair_kernel(keep, got, a0, *a2):
    total = keep[...].astype(F32) + got[...].astype(F32)
    a0[...] = total[0].astype(BF16)
    lanes = a2[0].shape[1]
    for i, a in enumerate(a2):
        a[...] = total[1, :, i * lanes : (i + 1) * lanes].astype(BF16)


def owner_kernel(a0, got, *outs):
    total = (a0[...].astype(F32) + got[...].astype(F32)).astype(BF16)
    lanes = outs[0].shape[1]
    for i, out in enumerate(outs):
        out[...] = total[:, i * lanes : (i + 1) * lanes]


def local(q_nope, q_rope, cache, w_uk, w_uv, d_out, sel, slot_blocks):
    peers = lax.axis_size("seq")
    groups = lax.axis_size("grp")
    queries, heads, nope = q_nope.shape
    rope = q_rope.shape[2]
    width = cache.shape[1]
    latent = width - rope
    value = d_out.shape[2]
    slots = slot_blocks.shape[1]
    per_peer = slots // peers
    if not (peers == 8 and groups == 4 and heads % peers == 0 and per_peer % 2 == 0):
        return local_general(q_nope, q_rope, cache, w_uk, w_uv, d_out, sel, slot_blocks)
    ids = jnp.stack([lax.axis_index("seq"), lax.axis_index("grp")]).astype(jnp.int32)
    tokens = cache.shape[0]
    depth = width // groups
    lanes = per_peer * BLOCK_LEN
    held = peers // 2
    half = held * lanes
    share = heads // peers
    rows = heads * queries
    scale = 1.0 / math.sqrt(nope + rope)

    n_rows = w_uk.shape[1] // latent
    l_rows = w_uv.shape[1] // value
    tiles = latent // LANES
    uk = w_uk.reshape(heads, n_rows, tiles, LANES).transpose(0, 2, 1, 3)
    pack = jnp.concatenate(
        [
            uk.reshape(heads, n_rows * tiles, LANES),
            w_uv.reshape(heads, l_rows, value),
            q_nope.transpose(1, 0, 2),
            d_out.transpose(1, 0, 2),
        ],
        axis=1,
    )
    pack = seq_swap(pack).reshape(peers, share, -1, LANES)
    sizes = (n_rows * tiles, l_rows, queries, tiles, latent)
    (lat,) = call(
        functools.partial(expand_kernel, sizes),
        "expand",
        (pack,),
        [VMEM],
        [((peers, share, queries, 2 * latent), BF16)],
    )
    qd = seq_swap(lat).reshape(rows, 2 * latent)

    asked = slot_blocks
    for bit in (1, 2, 4):
        asked = jnp.concatenate([asked, swap(asked, "seq", bit)], axis=0)
    mine = call(
        functools.partial(gather_kernel, peers),
        "gather",
        (ids, asked, cache.T),
        [SMEM, SMEM, VMEM],
        [((depth, lanes), BF16)] * peers,
    )
    arrived = exchange(mine)
    keys = []
    for c in range(2):
        k0 = jnp.stack(arrived[c * held : (c + 1) * held])
        k2 = swap(k0, "grp", 2)
        k1 = swap(k0, "grp", 1)
        k3 = swap(k2, "grp", 1)
        keys += [k0, k1, k2, k3]

    rope_rows = q_rope.transpose(1, 0, 2)
    kt, pb, cat, o_lat, delta, keep, send, dq = call(
        functools.partial(first_kernel, scale, per_peer),
        "first",
        (ids, sel, rope_rows, qd, *keys),
        [SMEM] + [VMEM] * 11,
        [
            ((width + slots, half), BF16),
            ((rows, half), BF16),
            ((width, 2 * rows), BF16),
            ((rows, latent), BF16),
            ((rows, 1), F32),
            ((2, depth, half), BF16),
            ((2, depth, half), BF16),
            ((rows, width), F32),
        ],
        [
            pltpu.VMEM((width + slots, half), BF16),
            pltpu.VMEM((rows, half), BF16),
            pltpu.VMEM((rows, width + slots), BF16),
            pltpu.VMEM((rows, latent), BF16),
            pltpu.VMEM((rows, 2 * half), F32),
            pltpu.VMEM((width, 2 * rows), BF16),
            pltpu.VMEM((rows, latent), F32),
        ],
        56,
    )
    o_lat = seq_swap(o_lat.reshape(peers, share, queries, latent))

    def give(send, keep):
        got = swap(send, "grp", 1)
        a0, a2 = call(pair_kernel, "pair", (keep, got), [VMEM] * 2, [((depth, half), BF16)] * 2)
        return call(
            owner_kernel,
            "owner",
            (a0, swap(a2, "grp", 2)),
            [VMEM] * 2,
            [((depth, lanes), BF16)] * held,
        )

    far = give(send, keep)
    keep, send, d_lat, d_rope = call(
        functools.partial(second_kernel, scale),
        "second",
        (qd, cat, delta, kt, pb, dq),
        [VMEM] * 6,
        [
            ((2, depth, half), BF16),
            ((2, depth, half), BF16),
            ((rows, latent), BF16),
            ((rows, rope), BF16),
        ],
        [pltpu.VMEM((rows, latent), BF16), pltpu.VMEM((rows, width), F32)],
        56,
    )
    near = give(send, keep)
    d_lat = seq_swap(d_lat.reshape(peers, share, queries, latent))
    got = exchange(near + far)

    (res,) = call(
        functools.partial(reduce_kernel, sizes),
        "reduce",
        (pack, o_lat, d_lat),
        [VMEM] * 3,
        [((peers, share, queries, value + nope), BF16)],
    )
    res = seq_swap(res).reshape(heads, queries, value + nope)

    (y0,) = call(
        functools.partial(scatter_kernel, peers),
        "scatter",
        (ids, asked, *got),
        [SMEM, SMEM] + [VMEM] * peers,
        [((depth, tokens), BF16)],
        [pltpu.VMEM((depth, tokens), F32)],
    )
    y2 = swap(y0, "grp", 2)
    y1 = swap(y0, "grp", 1)
    y3 = swap(y2, "grp", 1)
    (d_cache,) = call(
        assemble_kernel,
        "assemble",
        (ids, y0, y1, y2, y3),
        [SMEM] + [VMEM] * 4,
        [((width, tokens), F32)],
    )
    return (
        res[:, :, :value].transpose(1, 0, 2),
        res[:, :, value:].transpose(1, 0, 2),
        d_rope.reshape(heads, queries, rope).transpose(1, 0, 2),
        d_cache.T,
    )


def local_general(q_nope, q_rope, cache, w_uk, w_uv, d_out, sel, slot_blocks):
    peers = lax.axis_size("seq")
    queries, heads, nope = q_nope.shape
    rope = q_rope.shape[2]
    width = cache.shape[1]
    latent = width - rope
    value = d_out.shape[2]
    slot_total = slot_blocks.shape[1]
    per_peer = slot_total // peers
    own_blocks = cache.shape[0] // BLOCK_LEN
    scale = 1.0 / math.sqrt(nope + rope)
    gathered_k, gathered_v = (
        lax.all_gather(w_uk, "seq", axis=1, tiled=True),
        lax.all_gather(w_uv, "seq", axis=1, tiled=True),
    )
    weight_k = gathered_k.reshape(heads, nope, latent)
    weight_v = gathered_v.reshape(heads, latent, value)
    wanted = slot_blocks.reshape(peers, per_peer)
    asked = lax.all_to_all(wanted, "seq", split_axis=0, concat_axis=0, tiled=True)
    blocks = cache.reshape(own_blocks, BLOCK_LEN, width)
    arrived = lax.all_to_all(blocks[asked], "seq", split_axis=0, concat_axis=0, tiled=True)
    keys = arrived.reshape(slot_total * BLOCK_LEN, width)
    keys_lat = keys[:, :latent]
    q_lat = jnp.einsum("qhn,hnl->qhl", q_nope, weight_k, preferred_element_type=jnp.float32).astype(
        jnp.bfloat16
    )
    qfull = jnp.concatenate([q_lat, q_rope], axis=-1)
    chosen = jnp.any(
        sel[:, :, None] == jnp.arange(slot_total, dtype=jnp.int32)[None, None, :], axis=1
    )
    live = jnp.repeat(chosen, BLOCK_LEN, axis=1)[:, None, :]
    score = jnp.einsum("qhc,tc->qht", qfull, keys, preferred_element_type=jnp.float32) * scale
    score = jnp.where(live, score, -jnp.inf)
    prob = jax.nn.softmax(score, axis=-1)
    prob_low = prob.astype(jnp.bfloat16)
    olat = jnp.einsum("qht,tl->qhl", prob_low, keys_lat, preferred_element_type=jnp.float32).astype(
        jnp.bfloat16
    )
    attn_out = jnp.einsum(
        "qhl,hlv->qhv", olat, weight_v, preferred_element_type=jnp.float32
    ).astype(jnp.bfloat16)
    d_olat = jnp.einsum("qhv,hlv->qhl", d_out, weight_v, preferred_element_type=jnp.float32).astype(
        jnp.bfloat16
    )
    dprob = jnp.einsum("qhl,tl->qht", d_olat, keys_lat, preferred_element_type=jnp.float32)
    delta = jnp.sum(prob * dprob, axis=-1, keepdims=True)
    dscore = (prob * (dprob - delta) * scale).astype(jnp.bfloat16)
    dquery = jnp.einsum("qht,tc->qhc", dscore, keys, preferred_element_type=jnp.float32)
    d_q_rope = dquery[:, :, latent:].astype(jnp.bfloat16)
    d_qlat = dquery[:, :, :latent].astype(jnp.bfloat16)
    d_q_nope = jnp.einsum(
        "qhl,hnl->qhn", d_qlat, weight_k, preferred_element_type=jnp.float32
    ).astype(jnp.bfloat16)
    value_part = jnp.einsum("qht,qhl->tl", prob_low, d_olat, preferred_element_type=jnp.float32)
    dkeys = jnp.einsum("qht,qhc->tc", dscore, qfull, preferred_element_type=jnp.float32)
    dkeys = dkeys + jnp.pad(value_part, ((0, 0), (0, rope)))
    one_hot = (
        asked.reshape(-1)[:, None] == jnp.arange(own_blocks, dtype=jnp.int32)[None, :]
    ).astype(jnp.float32)
    returned = lax.all_to_all(
        dkeys.reshape(peers, per_peer, BLOCK_LEN * width).astype(jnp.bfloat16),
        "seq",
        split_axis=0,
        concat_axis=0,
        tiled=True,
    ).astype(jnp.float32)
    local_grad = jnp.dot(
        one_hot.T,
        returned.reshape(peers * per_peer, BLOCK_LEN * width),
        precision=lax.Precision.HIGHEST,
    )
    d_cache = (
        lax.psum(local_grad.astype(jnp.bfloat16), "grp")
        .astype(jnp.float32)
        .reshape(own_blocks * BLOCK_LEN, width)
    )
    return (attn_out, d_q_nope, d_q_rope, d_cache)


def solution(mesh):
    return jax.shard_map(
        local,
        mesh=mesh,
        in_specs=(
            P("seq", "grp", None),
            P("seq", "grp", None),
            P("seq", None),
            P("grp", "seq"),
            P("grp", "seq"),
            P("seq", "grp", None),
            P("seq", None),
            P("seq", None),
        ),
        out_specs=(
            P("seq", "grp", None),
            P("seq", "grp", None),
            P("seq", "grp", None),
            P("seq", None),
        ),
        check_vma=False,
    )
```

```python
import functools
import math

import jax
import jax.numpy as jnp
from jax import lax
from jax.experimental import pallas as pl
from jax.experimental.pallas import tpu as pltpu
from jax.sharding import PartitionSpec as P

BLOCK_LEN = 64
LANES = 128
HIDDEN = -1e30
VMEM = pl.BlockSpec(memory_space=pltpu.VMEM)
SMEM = pl.BlockSpec(memory_space=pltpu.SMEM)
ANY = pl.BlockSpec(memory_space=pl.ANY)
F32 = jnp.float32
BF16 = jnp.bfloat16


def call(kernel, name, args, specs, outs, scratch=(), mib=32, tied=None):
    out_shape = [jax.ShapeDtypeStruct(s, d) for s, d in outs]
    out_specs = [VMEM] * len(outs)
    aliases = {}
    body = kernel
    if tied is not None:
        args, specs = (tied, *args), [ANY] + specs
        out_shape, out_specs = [jax.ShapeDtypeStruct(tied.shape, tied.dtype)] + out_shape, [ANY] + out_specs
        aliases = {0: 0}
        n_in = len(args)

        def body(*refs):
            kernel(*refs[1:n_in], *refs[n_in + 1 :])

    return pl.pallas_call(
        body,
        out_shape=out_shape,
        in_specs=specs,
        out_specs=out_specs,
        scratch_shapes=list(scratch),
        input_output_aliases=aliases,
        compiler_params=pltpu.CompilerParams(vmem_limit_bytes=mib * 2**20),
        name=name,
    )(*args)


def nt(a, b):
    return lax.dot_general(a, b, (((1,), (1,)), ((), ())), preferred_element_type=F32)


def nn(a, b):
    return lax.dot_general(a, b, (((1,), (0,)), ((), ())), preferred_element_type=F32)


def swap(x, axis, bit):
    n = lax.axis_size(axis)
    return lax.ppermute(x, axis, [(i, i ^ bit) for i in range(n)])


def seq_swap(x):
    return lax.all_to_all(x, "seq", split_axis=0, concat_axis=0, tiled=True)


def exchange(pieces):
    return [pieces[0]] + [swap(p, "seq", k) for k, p in enumerate(pieces) if k > 0]


def cut_kernel(ids, cache, out):
    depth = out.shape[0]
    out[...] = cache[pl.ds(pl.multiple_of(ids[1] * depth, 16), depth), :]


def gather_kernel(per_peer, ids, own, other, *refs):
    owners = len(refs) - 2
    caches, outs = refs[:owners], refs[owners:]
    lanes = per_peer * BLOCK_LEN

    def block(row, i, j):
        b = row[0, (ids[0] ^ (2 * i)) * per_peer + j]
        tile = caches[i][:, pl.ds(pl.multiple_of((b >> 1) * LANES, LANES), LANES)]
        return jnp.where((b & 1) == 1, tile[:, BLOCK_LEN:], tile[:, :BLOCK_LEN])

    for row, out in zip((other, own), outs):
        for i in range(owners):
            for j in range(0, per_peer, 2):
                both = jnp.concatenate([block(row, i, j), block(row, i, j + 1)], axis=1)
                at = i * lanes + j * BLOCK_LEN
                out[:, at : at + 2 * BLOCK_LEN] = both


def scatter_kernel(count, ids, rows, *refs):
    got, out, acc = refs[:count], refs[count], refs[count + 1]
    me = ids[0]
    depth, lanes = got[0].shape
    per_peer = lanes // BLOCK_LEN
    acc[...] = jnp.zeros_like(acc)
    blank = jnp.zeros((depth, BLOCK_LEN), F32)
    for k in range(count):
        for j in range(per_peer):
            b = rows[k, me * per_peer + j]
            at = pl.ds(pl.multiple_of((b >> 1) * LANES, LANES), LANES)
            g = got[k][:, j * BLOCK_LEN : (j + 1) * BLOCK_LEN].astype(F32)
            low = jnp.concatenate([g, blank], axis=1)
            high = jnp.concatenate([blank, g], axis=1)
            acc[:, at] = acc[:, at] + jnp.where((b & 1) == 1, high, low)
    out[...] = acc[...].astype(BF16)


def assemble_kernel(ids, *refs):
    parts, out = refs[:-1], refs[-1]
    depth = parts[0].shape[0]
    for k, y in enumerate(parts):
        out[pl.ds(pl.multiple_of((ids[1] ^ k) * depth, 16), depth), :] = y[...].astype(F32)


def weight_k_of(pack, head, uk_rows, tiles):
    rows = uk_rows // tiles
    peers = pack.shape[0]
    cols = []
    for t in range(tiles):
        cols.append(
            jnp.concatenate(
                [pack[r, head, t * rows : (t + 1) * rows, :] for r in range(peers)], axis=0
            )
        )
    return jnp.concatenate(cols, axis=1)


def stacked(pack, head, start, rows):
    peers = pack.shape[0]
    return jnp.concatenate([pack[r, head, start : start + rows, :] for r in range(peers)], axis=0)


def expand_kernel(sizes, pack, out):
    uk_rows, uv_rows, queries, tiles, latent = sizes
    peers, heads = pack.shape[0], pack.shape[1]
    for h in range(heads):
        wk = weight_k_of(pack, h, uk_rows, tiles)
        wv = stacked(pack, h, uk_rows, uv_rows)
        qn = stacked(pack, h, uk_rows + uv_rows, queries)
        do = stacked(pack, h, uk_rows + uv_rows + queries, queries)
        q_lat = nn(qn, wk).astype(BF16)
        d_olat = nt(do, wv).astype(BF16)
        for r in range(peers):
            out[r, h, :, :latent] = q_lat[r * queries : (r + 1) * queries]
            out[r, h, :, latent:] = d_olat[r * queries : (r + 1) * queries]


def reduce_kernel(sizes, pack, lat, out):
    uk_rows, uv_rows, queries, tiles, latent = sizes
    peers, heads = pack.shape[0], pack.shape[1]
    for h in range(heads):
        wk = weight_k_of(pack, h, uk_rows, tiles)
        wv = stacked(pack, h, uk_rows, uv_rows)
        both = jnp.concatenate([lat[r, h] for r in range(peers)], axis=0)
        attn = nn(both[:, :latent], wv).astype(BF16)
        dqn = nt(both[:, latent:], wk).astype(BF16)
        for r in range(peers):
            out[r, h, :, : attn.shape[1]] = attn[r * queries : (r + 1) * queries]
            out[r, h, :, attn.shape[1] :] = dqn[r * queries : (r + 1) * queries]


def far_or_near(grads, scale, do, cat, delta, kt, p, width):
    keep, send, at, depth = grads
    latent = do.shape[1]
    dp = nn(do[...], kt[:latent])
    ds = (p.astype(F32) * (dp - delta) * scale).astype(BF16)
    part = nt(ds, kt[:width])
    dk = nn(cat[...], jnp.concatenate([ds, p], axis=0)).astype(BF16)
    for k, ref in enumerate((keep, send, keep, send)):
        ref[k // 2, :, at] = dk[k * depth : (k + 1) * depth]
    return part


def first_kernel(scale, per_peer, ids, sel, rope, qd, *refs):
    keys, refs = (refs[:4], refs[4:8]), refs[8:]
    kt_near, pb_near, cat, o_lat, delta_out, keep, send, dq, refs = (*refs[:8], refs[8:])
    kt_far, pb_far, qx, do, sc, flip, o_full = refs
    rows, latent = do.shape
    heads, queries, rope_dim = rope.shape
    width = latent + rope_dim
    slots = qx.shape[1] - width
    depth, half = keys[0][0].shape
    held = 4
    lanes = half // held
    kts, pbs = (kt_near, kt_far), (pb_near, pb_far)

    picks = sel[...] ^ (ids[0] * per_peer)
    slot = lax.broadcasted_iota(jnp.int32, (queries, slots), 1)
    chosen = picks[:, 0:1] == slot
    for j in range(1, picks.shape[1]):
        chosen = chosen | (picks[:, j : j + 1] == slot)
    bias = jnp.where(chosen, 0.0, HIDDEN).astype(BF16)
    bias = jnp.broadcast_to(bias[None], (heads, queries, slots)).reshape(rows, slots)
    qx[:, :latent] = qd[:, :latent]
    qx[:, latent:] = jnp.concatenate([rope[...].reshape(rows, rope_dim), bias], axis=1)
    do[...] = qd[:, latent:]
    for c in range(2):
        for k in range(4):
            at = pl.ds(pl.multiple_of((ids[1] ^ k) * depth, 16), depth)
            for i in range(held):
                peer = c * held + i
                src = keys[peer % 2][k][:, (peer // 2) * lanes : (peer // 2 + 1) * lanes]
                kts[c][at, i * lanes : (i + 1) * lanes] = src
        place = lax.broadcasted_iota(jnp.int32, (slots, half), 0)
        token = lax.broadcasted_iota(jnp.int32, (slots, half), 1) + c * half
        kts[c][width:, :] = jnp.where(token // BLOCK_LEN == place, 1.0, 0.0).astype(BF16)

    scale2 = scale * math.log2(math.e)
    step = 512
    chunks = [(c, i) for c in range(2) for i in range(0, half, step)]
    top = jnp.full((rows, 1), -jnp.inf, F32)
    for n, (c, i) in enumerate(chunks):
        s = nn(qx[...], kts[c][:, i : i + step]) * scale2
        sc[:, n * step : (n + 1) * step] = s
        top = jnp.maximum(top, jnp.max(s, axis=1, keepdims=True))
    total = jnp.zeros((rows, 1), F32)
    for n in range(len(chunks)):
        e = jnp.exp2(sc[:, n * step : (n + 1) * step] - top)
        sc[:, n * step : (n + 1) * step] = e
        total = total + jnp.sum(e, axis=1, keepdims=True)
    inv = 1.0 / total
    for n, (c, i) in enumerate(chunks):
        pb = (sc[:, n * step : (n + 1) * step] * inv).astype(BF16)
        pbs[c][:, i : i + step] = pb
        part = nt(pb, kts[c][:latent, i : i + step])
        if n == 0:
            o_full[...] = part
        else:
            o_full[...] += part
    o_lat[...] = o_full[...].astype(BF16)
    delta = jnp.sum(o_full[...] * do[...].astype(F32), axis=1, keepdims=True)
    delta_out[...] = delta

    flip[:, :rows] = qx[:, :width].T
    flip[:latent, rows:] = do[...].T
    flip[latent:, rows:] = jnp.zeros((rope_dim, rows), BF16)
    for k in range(4):
        at = pl.ds(pl.multiple_of((ids[1] ^ k) * depth, 16), depth)
        cat[k * depth : (k + 1) * depth] = flip[at, :]
    for i in range(0, half, step):
        at = slice(i, i + step)
        grads = (keep, send, at, depth)
        part = far_or_near(grads, scale, do, cat, delta, kt_far.at[:, at], pb_far[:, at], width)
        if i == 0:
            dq[...] = part
        else:
            dq[...] += part


def second_kernel(scale, qd, cat, delta, kt, pb, o_lat, before, keep, send, lat, d_rope, do, dq):
    rows, latent = do.shape
    width = cat.shape[0]
    depth = width // 4
    do[...] = qd[:, latent:]
    step = 512
    dq[...] = before[...]
    for i in range(0, pb.shape[1], step):
        at = slice(i, i + step)
        grads = (keep, send, at, depth)
        dq[...] += far_or_near(
            grads, scale, do, cat, delta[...], kt.at[:, at], pb[:, at], width
        )
    lat[:, :latent] = o_lat[...]
    lat[:, latent:] = dq[:, :latent].astype(BF16)
    d_rope[...] = dq[:, latent:].astype(BF16)


def pair_kernel(keep, got, a0, *a2):
    total = keep[...].astype(F32) + got[...].astype(F32)
    a0[...] = total[0].astype(BF16)
    lanes = a2[0].shape[1]
    for i, a in enumerate(a2):
        a[...] = total[1, :, i * lanes : (i + 1) * lanes].astype(BF16)


def owner_kernel(a0, got, *outs):
    total = (a0[...].astype(F32) + got[...].astype(F32)).astype(BF16)
    lanes = outs[0].shape[1]
    for i, out in enumerate(outs):
        out[...] = total[:, i * lanes : (i + 1) * lanes]


def local(q_nope, q_rope, cache, w_uk, w_uv, d_out, sel, slot_blocks):
    peers = lax.axis_size("seq")
    groups = lax.axis_size("grp")
    queries, heads, nope = q_nope.shape
    rope = q_rope.shape[2]
    width = cache.shape[1]
    latent = width - rope
    value = d_out.shape[2]
    slots = slot_blocks.shape[1]
    per_peer = slots // peers
    if not (peers == 8 and groups == 4 and heads % peers == 0 and per_peer % 2 == 0):
        return local_general(q_nope, q_rope, cache, w_uk, w_uv, d_out, sel, slot_blocks)
    ids = jnp.stack([lax.axis_index("seq"), lax.axis_index("grp")]).astype(jnp.int32)
    tokens = cache.shape[0]
    depth = width // groups
    lanes = per_peer * BLOCK_LEN
    held = peers // 2
    half = held * lanes
    share = heads // peers
    rows = heads * queries
    scale = 1.0 / math.sqrt(nope + rope)

    n_rows = w_uk.shape[1] // latent
    l_rows = w_uv.shape[1] // value
    tiles = latent // LANES
    uk = w_uk.reshape(heads, n_rows, tiles, LANES).transpose(0, 2, 1, 3)
    pack = jnp.concatenate(
        [
            uk.reshape(heads, n_rows * tiles, LANES),
            w_uv.reshape(heads, l_rows, value),
            q_nope.transpose(1, 0, 2),
            d_out.transpose(1, 0, 2),
        ],
        axis=1,
    )
    pack = seq_swap(pack).reshape(peers, share, -1, LANES)
    sizes = (n_rows * tiles, l_rows, queries, tiles, latent)
    (lat,) = call(
        functools.partial(expand_kernel, sizes),
        "expand",
        (pack,),
        [VMEM],
        [((peers, share, queries, 2 * latent), BF16)],
    )
    qd = seq_swap(lat).reshape(rows, 2 * latent)

    row1 = swap(slot_blocks, "seq", 1)
    (c0,) = call(
        cut_kernel, "cut", (ids, cache.T), [SMEM, VMEM], [((depth, tokens), BF16)]
    )
    c2 = swap(c0, "seq", 4)
    c1 = swap(c0, "seq", 2)
    c3 = swap(c2, "seq", 2)
    away, k0 = call(
        functools.partial(gather_kernel, per_peer),
        "gather",
        (ids, slot_blocks, row1, c0, c1, c2, c3),
        [SMEM] * 3 + [VMEM] * 4,
        [((depth, half), BF16)] * 2,
    )
    keys = []
    for k in (k0, swap(away, "seq", 1)):
        k2 = swap(k, "grp", 2)
        keys += [k, swap(k, "grp", 1), k2, swap(k2, "grp", 1)]
    asked = jnp.concatenate([slot_blocks, row1], axis=0)
    for bit in (2, 4):
        asked = jnp.concatenate([asked, swap(asked, "seq", bit)], axis=0)

    rope_rows = q_rope.transpose(1, 0, 2)
    kt, pb, cat, o_lat, delta, keep, send, dq = call(
        functools.partial(first_kernel, scale, per_peer),
        "first",
        (ids, sel, rope_rows, qd, *keys),
        [SMEM] + [VMEM] * 11,
        [
            ((width + slots, half), BF16),
            ((rows, half), BF16),
            ((width, 2 * rows), BF16),
            ((rows, latent), BF16),
            ((rows, 1), F32),
            ((2, depth, half), BF16),
            ((2, depth, half), BF16),
            ((rows, width), F32),
        ],
        [
            pltpu.VMEM((width + slots, half), BF16),
            pltpu.VMEM((rows, half), BF16),
            pltpu.VMEM((rows, width + slots), BF16),
            pltpu.VMEM((rows, latent), BF16),
            pltpu.VMEM((rows, 2 * half), F32),
            pltpu.VMEM((width, 2 * rows), BF16),
            pltpu.VMEM((rows, latent), F32),
        ],
        40,
    )

    def pair(keep, send, tied=None):
        outs = [((depth, half), BF16)] * 2
        return call(pair_kernel, "pair", (keep, swap(send, "grp", 1)), [VMEM] * 2, outs, tied=tied)

    def owner(a0, a2, tied=None):
        outs = [((depth, lanes), BF16)] * held
        return call(owner_kernel, "owner", (a0, swap(a2, "grp", 2)), [VMEM] * 2, outs, tied=tied)

    far = (keep, send)
    keep, send, lat, d_rope = call(
        functools.partial(second_kernel, scale),
        "second",
        (qd, cat, delta, kt, pb, o_lat, dq),
        [VMEM] * 7,
        [
            ((2, depth, half), BF16),
            ((2, depth, half), BF16),
            ((rows, 2 * latent), BF16),
            ((rows, rope), BF16),
        ],
        [pltpu.VMEM((rows, latent), BF16), pltpu.VMEM((rows, width), F32)],
        28,
    )
    lat, *far = pair(*far, tied=lat)
    near = pair(keep, send)
    far = owner(*far)
    lat = seq_swap(lat.reshape(peers, share, queries, 2 * latent))
    (res,) = call(
        functools.partial(reduce_kernel, sizes),
        "reduce",
        (pack, lat),
        [VMEM] * 2,
        [((peers, share, queries, value + nope), BF16)],
    )
    res, *near = owner(*near, tied=res)
    got = exchange([*near, *far])
    res = seq_swap(res).reshape(heads, queries, value + nope)

    (y0,) = call(
        functools.partial(scatter_kernel, peers),
        "scatter",
        (ids, asked, *got),
        [SMEM, SMEM] + [VMEM] * peers,
        [((depth, tokens), BF16)],
        [pltpu.VMEM((depth, tokens), F32)],
    )
    y2 = swap(y0, "grp", 2)
    y1 = swap(y0, "grp", 1)
    y3 = swap(y2, "grp", 1)
    (d_cache,) = call(
        assemble_kernel,
        "assemble",
        (ids, y0, y1, y2, y3),
        [SMEM] + [VMEM] * 4,
        [((width, tokens), F32)],
    )
    return (
        res[:, :, :value].transpose(1, 0, 2),
        res[:, :, value:].transpose(1, 0, 2),
        d_rope.reshape(heads, queries, rope).transpose(1, 0, 2),
        d_cache.T,
    )


def local_general(q_nope, q_rope, cache, w_uk, w_uv, d_out, sel, slot_blocks):
    peers = lax.axis_size("seq")
    queries, heads, nope = q_nope.shape
    rope = q_rope.shape[2]
    width = cache.shape[1]
    latent = width - rope
    value = d_out.shape[2]
    slot_total = slot_blocks.shape[1]
    per_peer = slot_total // peers
    own_blocks = cache.shape[0] // BLOCK_LEN
    scale = 1.0 / math.sqrt(nope + rope)
    gathered_k, gathered_v = (
        lax.all_gather(w_uk, "seq", axis=1, tiled=True),
        lax.all_gather(w_uv, "seq", axis=1, tiled=True),
    )
    weight_k = gathered_k.reshape(heads, nope, latent)
    weight_v = gathered_v.reshape(heads, latent, value)
    wanted = slot_blocks.reshape(peers, per_peer)
    asked = lax.all_to_all(wanted, "seq", split_axis=0, concat_axis=0, tiled=True)
    blocks = cache.reshape(own_blocks, BLOCK_LEN, width)
    arrived = lax.all_to_all(blocks[asked], "seq", split_axis=0, concat_axis=0, tiled=True)
    keys = arrived.reshape(slot_total * BLOCK_LEN, width)
    keys_lat = keys[:, :latent]
    q_lat = jnp.einsum("qhn,hnl->qhl", q_nope, weight_k, preferred_element_type=jnp.float32).astype(
        jnp.bfloat16
    )
    qfull = jnp.concatenate([q_lat, q_rope], axis=-1)
    chosen = jnp.any(
        sel[:, :, None] == jnp.arange(slot_total, dtype=jnp.int32)[None, None, :], axis=1
    )
    live = jnp.repeat(chosen, BLOCK_LEN, axis=1)[:, None, :]
    score = jnp.einsum("qhc,tc->qht", qfull, keys, preferred_element_type=jnp.float32) * scale
    score = jnp.where(live, score, -jnp.inf)
    prob = jax.nn.softmax(score, axis=-1)
    prob_low = prob.astype(jnp.bfloat16)
    olat = jnp.einsum("qht,tl->qhl", prob_low, keys_lat, preferred_element_type=jnp.float32).astype(
        jnp.bfloat16
    )
    attn_out = jnp.einsum(
        "qhl,hlv->qhv", olat, weight_v, preferred_element_type=jnp.float32
    ).astype(jnp.bfloat16)
    d_olat = jnp.einsum("qhv,hlv->qhl", d_out, weight_v, preferred_element_type=jnp.float32).astype(
        jnp.bfloat16
    )
    dprob = jnp.einsum("qhl,tl->qht", d_olat, keys_lat, preferred_element_type=jnp.float32)
    delta = jnp.sum(prob * dprob, axis=-1, keepdims=True)
    dscore = (prob * (dprob - delta) * scale).astype(jnp.bfloat16)
    dquery = jnp.einsum("qht,tc->qhc", dscore, keys, preferred_element_type=jnp.float32)
    d_q_rope = dquery[:, :, latent:].astype(jnp.bfloat16)
    d_qlat = dquery[:, :, :latent].astype(jnp.bfloat16)
    d_q_nope = jnp.einsum(
        "qhl,hnl->qhn", d_qlat, weight_k, preferred_element_type=jnp.float32
    ).astype(jnp.bfloat16)
    value_part = jnp.einsum("qht,qhl->tl", prob_low, d_olat, preferred_element_type=jnp.float32)
    dkeys = jnp.einsum("qht,qhc->tc", dscore, qfull, preferred_element_type=jnp.float32)
    dkeys = dkeys + jnp.pad(value_part, ((0, 0), (0, rope)))
    one_hot = (
        asked.reshape(-1)[:, None] == jnp.arange(own_blocks, dtype=jnp.int32)[None, :]
    ).astype(jnp.float32)
    returned = lax.all_to_all(
        dkeys.reshape(peers, per_peer, BLOCK_LEN * width).astype(jnp.bfloat16),
        "seq",
        split_axis=0,
        concat_axis=0,
        tiled=True,
    ).astype(jnp.float32)
    local_grad = jnp.dot(
        one_hot.T,
        returned.reshape(peers * per_peer, BLOCK_LEN * width),
        precision=lax.Precision.HIGHEST,
    )
    d_cache = (
        lax.psum(local_grad.astype(jnp.bfloat16), "grp")
        .astype(jnp.float32)
        .reshape(own_blocks * BLOCK_LEN, width)
    )
    return (attn_out, d_q_nope, d_q_rope, d_cache)


def solution(mesh):
    return jax.shard_map(
        local,
        mesh=mesh,
        in_specs=(
            P("seq", "grp", None),
            P("seq", "grp", None),
            P("seq", None),
            P("grp", "seq"),
            P("grp", "seq"),
            P("seq", "grp", None),
            P("seq", None),
            P("seq", None),
        ),
        out_specs=(
            P("seq", "grp", None),
            P("seq", "grp", None),
            P("seq", "grp", None),
            P("seq", None),
        ),
        check_vma=False,
    )
```

```python
import functools
import math

import jax
import jax.numpy as jnp
from jax import lax
from jax.experimental import pallas as pl
from jax.experimental.pallas import tpu as pltpu
from jax.sharding import PartitionSpec as P

BLOCK_LEN = 64
LANES = 128
HIDDEN = -1e30
VMEM = pl.BlockSpec(memory_space=pltpu.VMEM)
SMEM = pl.BlockSpec(memory_space=pltpu.SMEM)
ANY = pl.BlockSpec(memory_space=pl.ANY)
F32 = jnp.float32
BF16 = jnp.bfloat16


def call(kernel, name, args, specs, outs, scratch=(), tied=None):
    out_shape = [jax.ShapeDtypeStruct(s, d) for s, d in outs]
    out_specs = [VMEM] * len(outs)
    aliases = {}
    body = kernel
    if tied is not None:
        args, specs = (tied, *args), [ANY] + specs
        out_shape, out_specs = [jax.ShapeDtypeStruct(tied.shape, tied.dtype)] + out_shape, [ANY] + out_specs
        aliases = {0: 0}
        n_in = len(args)

        def body(*refs):
            kernel(*refs[1:n_in], *refs[n_in + 1 :])

    return pl.pallas_call(
        body,
        out_shape=out_shape,
        in_specs=specs,
        out_specs=out_specs,
        scratch_shapes=list(scratch),
        input_output_aliases=aliases,
        compiler_params=pltpu.CompilerParams(vmem_limit_bytes=60 * 2**20),
        name=name,
    )(*args)


def nt(a, b):
    return lax.dot_general(a, b, (((1,), (1,)), ((), ())), preferred_element_type=F32)


def nn(a, b):
    return lax.dot_general(a, b, (((1,), (0,)), ((), ())), preferred_element_type=F32)


def swap(x, axis, bit):
    n = lax.axis_size(axis)
    return lax.ppermute(x, axis, [(i, i ^ bit) for i in range(n)])


def seq_swap(x):
    return lax.all_to_all(x, "seq", split_axis=0, concat_axis=0, tiled=True)


def exchange(pieces):
    return [pieces[0]] + [swap(p, "seq", k) for k, p in enumerate(pieces) if k > 0]


def copy_kernel(x, out):
    out[...] = x[...]


def cut_kernel(ids, cache, out):
    depth = out.shape[0]
    out[...] = cache[pl.ds(pl.multiple_of(ids[1] * depth, 16), depth), :]


def gather_kernel(per_peer, ids, own, other, *refs):
    owners = len(refs) - 2
    caches, outs = refs[:owners], refs[owners:]
    lanes = per_peer * BLOCK_LEN

    def block(row, i, j):
        b = row[0, (ids[0] ^ (2 * i)) * per_peer + j]
        tile = caches[i][:, pl.ds(pl.multiple_of((b >> 1) * LANES, LANES), LANES)]
        return jnp.where((b & 1) == 1, tile[:, BLOCK_LEN:], tile[:, :BLOCK_LEN])

    for row, out in zip((other, own), outs):
        for i in range(owners):
            for j in range(0, per_peer, 2):
                both = jnp.concatenate([block(row, i, j), block(row, i, j + 1)], axis=1)
                at = i * lanes + j * BLOCK_LEN
                out[:, at : at + 2 * BLOCK_LEN] = both


def scatter_kernel(count, ids, rows, *refs):
    got, out, acc = refs[:count], refs[count], refs[count + 1]
    me = ids[0]
    depth, lanes = got[0].shape
    per_peer = lanes // BLOCK_LEN
    acc[...] = jnp.zeros_like(acc)
    blank = jnp.zeros((depth, BLOCK_LEN), F32)
    for k in range(count):
        for j in range(per_peer):
            b = rows[k, me * per_peer + j]
            at = pl.ds(pl.multiple_of((b >> 1) * LANES, LANES), LANES)
            g = got[k][:, j * BLOCK_LEN : (j + 1) * BLOCK_LEN].astype(F32)
            low = jnp.concatenate([g, blank], axis=1)
            high = jnp.concatenate([blank, g], axis=1)
            acc[:, at] = acc[:, at] + jnp.where((b & 1) == 1, high, low)
    out[...] = acc[...].astype(BF16)


def assemble_kernel(ids, *refs):
    parts, out = refs[:-1], refs[-1]
    depth = parts[0].shape[0]
    for k, y in enumerate(parts):
        out[pl.ds(pl.multiple_of((ids[1] ^ k) * depth, 16), depth), :] = y[...].astype(F32)


def weight_k_of(pack, head, uk_rows, tiles):
    rows = uk_rows // tiles
    peers = pack.shape[0]
    cols = []
    for t in range(tiles):
        cols.append(
            jnp.concatenate(
                [pack[r, head, t * rows : (t + 1) * rows, :] for r in range(peers)], axis=0
            )
        )
    return jnp.concatenate(cols, axis=1)


def stacked(pack, head, start, rows):
    peers = pack.shape[0]
    return jnp.concatenate([pack[r, head, start : start + rows, :] for r in range(peers)], axis=0)


def expand_kernel(sizes, pack, out):
    uk_rows, uv_rows, queries, tiles, latent = sizes
    peers, heads = pack.shape[0], pack.shape[1]
    for h in range(heads):
        wk = weight_k_of(pack, h, uk_rows, tiles)
        wv = stacked(pack, h, uk_rows, uv_rows)
        qn = stacked(pack, h, uk_rows + uv_rows, queries)
        do = stacked(pack, h, uk_rows + uv_rows + queries, queries)
        q_lat = nn(qn, wk).astype(BF16)
        d_olat = nt(do, wv).astype(BF16)
        for r in range(peers):
            out[r, h, :, :latent] = q_lat[r * queries : (r + 1) * queries]
            out[r, h, :, latent:] = d_olat[r * queries : (r + 1) * queries]


def reduce_kernel(sizes, pack, lat, out):
    uk_rows, uv_rows, queries, tiles, latent = sizes
    peers, heads = pack.shape[0], pack.shape[1]
    for h in range(heads):
        wk = weight_k_of(pack, h, uk_rows, tiles)
        wv = stacked(pack, h, uk_rows, uv_rows)
        both = jnp.concatenate([lat[r, h] for r in range(peers)], axis=0)
        attn = nn(both[:, :latent], wv).astype(BF16)
        dqn = nt(both[:, latent:], wk).astype(BF16)
        for r in range(peers):
            out[r, h, :, : attn.shape[1]] = attn[r * queries : (r + 1) * queries]
            out[r, h, :, attn.shape[1] :] = dqn[r * queries : (r + 1) * queries]


def tokens_grad(grads, scale, do, cat, delta, kt, p, width):
    keep, send, at, depth = grads
    latent = do.shape[1]
    dp = nn(do[...], kt[:latent])
    ds = (p.astype(F32) * (dp - delta) * scale).astype(BF16)
    part = nt(ds, kt[:width])
    dk = nn(cat[...], jnp.concatenate([ds, p], axis=0)).astype(BF16)
    for k, ref in enumerate((keep, send, keep, send)):
        ref[k // 2, :, at] = dk[k * depth : (k + 1) * depth]
    return part


def attend_kernel(scale, per_peer, ids, sel, rope, qd, *refs):
    keys, refs = (refs[:4], refs[4:8]), refs[9:]
    keeps, sends, lat, d_rope, refs = (refs[0], refs[2]), (refs[1], refs[3]), refs[4], refs[5], refs[6:]
    kt_near, kt_far, pb_near, pb_far, qx, do, sc, flip, cat, o_full, dq = refs
    rows, latent = do.shape
    heads, queries, rope_dim = rope.shape
    width = latent + rope_dim
    slots = qx.shape[1] - width
    depth, half = keys[0][0].shape
    held = 4
    lanes = half // held
    kts, pbs = (kt_near, kt_far), (pb_near, pb_far)

    picks = sel[...] ^ (ids[0] * per_peer)
    slot = lax.broadcasted_iota(jnp.int32, (queries, slots), 1)
    chosen = picks[:, 0:1] == slot
    for j in range(1, picks.shape[1]):
        chosen = chosen | (picks[:, j : j + 1] == slot)
    bias = jnp.where(chosen, 0.0, HIDDEN).astype(BF16)
    bias = jnp.broadcast_to(bias[None], (heads, queries, slots)).reshape(rows, slots)
    qx[:, :latent] = qd[:, :latent]
    qx[:, latent:] = jnp.concatenate([rope[...].reshape(rows, rope_dim), bias], axis=1)
    do[...] = qd[:, latent:]
    for c in range(2):
        for k in range(4):
            at = pl.ds(pl.multiple_of((ids[1] ^ k) * depth, 16), depth)
            for i in range(held):
                peer = c * held + i
                src = keys[peer % 2][k][:, (peer // 2) * lanes : (peer // 2 + 1) * lanes]
                kts[c][at, i * lanes : (i + 1) * lanes] = src
        place = lax.broadcasted_iota(jnp.int32, (slots, half), 0)
        token = lax.broadcasted_iota(jnp.int32, (slots, half), 1) + c * half
        kts[c][width:, :] = jnp.where(token // BLOCK_LEN == place, 1.0, 0.0).astype(BF16)

    scale2 = scale * math.log2(math.e)
    step = 512
    chunks = [(c, i) for c in range(2) for i in range(0, half, step)]
    top = jnp.full((rows, 1), -jnp.inf, F32)
    for n, (c, i) in enumerate(chunks):
        s = nn(qx[...], kts[c][:, i : i + step]) * scale2
        sc[:, n * step : (n + 1) * step] = s
        top = jnp.maximum(top, jnp.max(s, axis=1, keepdims=True))
    total = jnp.zeros((rows, 1), F32)
    for n in range(len(chunks)):
        e = jnp.exp2(sc[:, n * step : (n + 1) * step] - top)
        sc[:, n * step : (n + 1) * step] = e
        total = total + jnp.sum(e, axis=1, keepdims=True)
    inv = 1.0 / total
    for n, (c, i) in enumerate(chunks):
        pb = (sc[:, n * step : (n + 1) * step] * inv).astype(BF16)
        pbs[c][:, i : i + step] = pb
        part = nt(pb, kts[c][:latent, i : i + step])
        if n == 0:
            o_full[...] = part
        else:
            o_full[...] += part
    lat[:, :latent] = o_full[...].astype(BF16)
    delta = jnp.sum(o_full[...] * do[...].astype(F32), axis=1, keepdims=True)

    flip[:, :rows] = qx[:, :width].T
    flip[:latent, rows:] = do[...].T
    flip[latent:, rows:] = jnp.zeros((rope_dim, rows), BF16)
    for k in range(4):
        at = pl.ds(pl.multiple_of((ids[1] ^ k) * depth, 16), depth)
        cat[k * depth : (k + 1) * depth] = flip[at, :]
    for n, (c, i) in enumerate([(c, i) for c in (1, 0) for i in range(0, half, step)]):
        at = slice(i, i + step)
        grads = (keeps[c], sends[c], at, depth)
        kt = kts[c].at[:, at]
        part = tokens_grad(grads, scale, do, cat, delta, kt, pbs[c][:, at], width)
        if n == 0:
            dq[...] = part
        else:
            dq[...] += part
    lat[:, latent:] = dq[:, :latent].astype(BF16)
    d_rope[...] = dq[:, latent:].astype(BF16)


def pair_kernel(keep, got, a0, *a2):
    total = keep[...].astype(F32) + got[...].astype(F32)
    a0[...] = total[0].astype(BF16)
    lanes = a2[0].shape[1]
    for i, a in enumerate(a2):
        a[...] = total[1, :, i * lanes : (i + 1) * lanes].astype(BF16)


def owner_kernel(a0, got, *outs):
    total = (a0[...].astype(F32) + got[...].astype(F32)).astype(BF16)
    lanes = outs[0].shape[1]
    for i, out in enumerate(outs):
        out[...] = total[:, i * lanes : (i + 1) * lanes]


def local(q_nope, q_rope, cache, w_uk, w_uv, d_out, sel, slot_blocks):
    peers = lax.axis_size("seq")
    groups = lax.axis_size("grp")
    queries, heads, nope = q_nope.shape
    rope = q_rope.shape[2]
    width = cache.shape[1]
    latent = width - rope
    value = d_out.shape[2]
    slots = slot_blocks.shape[1]
    per_peer = slots // peers
    if not (peers == 8 and groups == 4 and heads % peers == 0 and per_peer % 2 == 0):
        return local_general(q_nope, q_rope, cache, w_uk, w_uv, d_out, sel, slot_blocks)
    ids = jnp.stack([lax.axis_index("seq"), lax.axis_index("grp")]).astype(jnp.int32)
    tokens = cache.shape[0]
    depth = width // groups
    lanes = per_peer * BLOCK_LEN
    held = peers // 2
    half = held * lanes
    share = heads // peers
    rows = heads * queries
    scale = 1.0 / math.sqrt(nope + rope)

    row1 = swap(slot_blocks, "seq", 1)
    (c0,) = call(cut_kernel, "cut", (ids, cache.T), [SMEM, VMEM], [((depth, tokens), BF16)])

    n_rows = w_uk.shape[1] // latent
    l_rows = w_uv.shape[1] // value
    tiles = latent // LANES
    uk = w_uk.reshape(heads, n_rows, tiles, LANES).transpose(0, 2, 1, 3)
    pack = jnp.concatenate(
        [
            uk.reshape(heads, n_rows * tiles, LANES),
            w_uv.reshape(heads, l_rows, value),
            q_nope.transpose(1, 0, 2),
            d_out.transpose(1, 0, 2),
        ],
        axis=1,
    )
    pack, row1 = call(
        copy_kernel, "after", (row1,), [VMEM], [(row1.shape, jnp.int32)], tied=pack
    )
    pack = seq_swap(pack).reshape(peers, share, -1, LANES)
    sizes = (n_rows * tiles, l_rows, queries, tiles, latent)
    (lat,) = call(
        functools.partial(expand_kernel, sizes),
        "expand",
        (pack,),
        [VMEM],
        [((peers, share, queries, 2 * latent), BF16)],
    )
    qd = seq_swap(lat).reshape(rows, 2 * latent)

    c2 = swap(c0, "seq", 4)
    c1 = swap(c0, "seq", 2)
    c3 = swap(c2, "seq", 2)
    away, k0 = call(
        functools.partial(gather_kernel, per_peer),
        "gather",
        (ids, slot_blocks, row1, c0, c1, c2, c3),
        [SMEM] * 3 + [VMEM] * 4,
        [((depth, half), BF16)] * 2,
    )
    keys = []
    for k in (k0, swap(away, "seq", 1)):
        k2 = swap(k, "grp", 2)
        keys += [k, swap(k, "grp", 1), k2, swap(k2, "grp", 1)]
    asked = jnp.concatenate([slot_blocks, row1], axis=0)
    for bit in (2, 4):
        asked = jnp.concatenate([asked, swap(asked, "seq", bit)], axis=0)

    rope_rows = q_rope.transpose(1, 0, 2)
    near_keep, near_send, far_keep, far_send, lat, d_rope = call(
        functools.partial(attend_kernel, scale, per_peer),
        "attend",
        (ids, sel, rope_rows, qd, *keys, asked),
        [SMEM] + [VMEM] * 11 + [ANY],
        [((2, depth, half), BF16)] * 4 + [((rows, 2 * latent), BF16), ((rows, rope), BF16)],
        [pltpu.VMEM((width + slots, half), BF16)] * 2
        + [pltpu.VMEM((rows, half), BF16)] * 2
        + [
            pltpu.VMEM((rows, width + slots), BF16),
            pltpu.VMEM((rows, latent), BF16),
            pltpu.VMEM((rows, 2 * half), F32),
            pltpu.VMEM((width, 2 * rows), BF16),
            pltpu.VMEM((width, 2 * rows), BF16),
            pltpu.VMEM((rows, latent), F32),
            pltpu.VMEM((rows, width), F32),
        ],
    )

    def pair(keep, send, tied=None):
        outs = [((depth, half), BF16)] * 2
        return call(pair_kernel, "pair", (keep, swap(send, "grp", 1)), [VMEM] * 2, outs, tied=tied)

    def owner(a0, a2, tied=None):
        outs = [((depth, lanes), BF16)] * held
        return call(owner_kernel, "owner", (a0, swap(a2, "grp", 2)), [VMEM] * 2, outs, tied=tied)

    far = pair(far_keep, far_send)
    lat, *near = pair(near_keep, near_send, tied=lat)
    far = owner(*far)
    lat = seq_swap(lat.reshape(peers, share, queries, 2 * latent))
    (res,) = call(
        functools.partial(reduce_kernel, sizes),
        "reduce",
        (pack, lat),
        [VMEM] * 2,
        [((peers, share, queries, value + nope), BF16)],
    )
    res, *near = owner(*near, tied=res)
    got = exchange([*near, *far])
    res = seq_swap(res).reshape(heads, queries, value + nope)

    (y0,) = call(
        functools.partial(scatter_kernel, peers),
        "scatter",
        (ids, asked, *got),
        [SMEM, SMEM] + [VMEM] * peers,
        [((depth, tokens), BF16)],
        [pltpu.VMEM((depth, tokens), F32)],
    )
    y2 = swap(y0, "grp", 2)
    y1 = swap(y0, "grp", 1)
    y3 = swap(y2, "grp", 1)
    (d_cache,) = call(
        assemble_kernel,
        "assemble",
        (ids, y0, y1, y2, y3),
        [SMEM] + [VMEM] * 4,
        [((width, tokens), F32)],
    )
    return (
        res[:, :, :value].transpose(1, 0, 2),
        res[:, :, value:].transpose(1, 0, 2),
        d_rope.reshape(heads, queries, rope).transpose(1, 0, 2),
        d_cache.T,
    )


def local_general(q_nope, q_rope, cache, w_uk, w_uv, d_out, sel, slot_blocks):
    peers = lax.axis_size("seq")
    queries, heads, nope = q_nope.shape
    rope = q_rope.shape[2]
    width = cache.shape[1]
    latent = width - rope
    value = d_out.shape[2]
    slot_total = slot_blocks.shape[1]
    per_peer = slot_total // peers
    own_blocks = cache.shape[0] // BLOCK_LEN
    scale = 1.0 / math.sqrt(nope + rope)
    gathered_k, gathered_v = (
        lax.all_gather(w_uk, "seq", axis=1, tiled=True),
        lax.all_gather(w_uv, "seq", axis=1, tiled=True),
    )
    weight_k = gathered_k.reshape(heads, nope, latent)
    weight_v = gathered_v.reshape(heads, latent, value)
    wanted = slot_blocks.reshape(peers, per_peer)
    asked = lax.all_to_all(wanted, "seq", split_axis=0, concat_axis=0, tiled=True)
    blocks = cache.reshape(own_blocks, BLOCK_LEN, width)
    arrived = lax.all_to_all(blocks[asked], "seq", split_axis=0, concat_axis=0, tiled=True)
    keys = arrived.reshape(slot_total * BLOCK_LEN, width)
    keys_lat = keys[:, :latent]
    q_lat = jnp.einsum("qhn,hnl->qhl", q_nope, weight_k, preferred_element_type=jnp.float32).astype(
        jnp.bfloat16
    )
    qfull = jnp.concatenate([q_lat, q_rope], axis=-1)
    chosen = jnp.any(
        sel[:, :, None] == jnp.arange(slot_total, dtype=jnp.int32)[None, None, :], axis=1
    )
    live = jnp.repeat(chosen, BLOCK_LEN, axis=1)[:, None, :]
    score = jnp.einsum("qhc,tc->qht", qfull, keys, preferred_element_type=jnp.float32) * scale
    score = jnp.where(live, score, -jnp.inf)
    prob = jax.nn.softmax(score, axis=-1)
    prob_low = prob.astype(jnp.bfloat16)
    olat = jnp.einsum("qht,tl->qhl", prob_low, keys_lat, preferred_element_type=jnp.float32).astype(
        jnp.bfloat16
    )
    attn_out = jnp.einsum(
        "qhl,hlv->qhv", olat, weight_v, preferred_element_type=jnp.float32
    ).astype(jnp.bfloat16)
    d_olat = jnp.einsum("qhv,hlv->qhl", d_out, weight_v, preferred_element_type=jnp.float32).astype(
        jnp.bfloat16
    )
    dprob = jnp.einsum("qhl,tl->qht", d_olat, keys_lat, preferred_element_type=jnp.float32)
    delta = jnp.sum(prob * dprob, axis=-1, keepdims=True)
    dscore = (prob * (dprob - delta) * scale).astype(jnp.bfloat16)
    dquery = jnp.einsum("qht,tc->qhc", dscore, keys, preferred_element_type=jnp.float32)
    d_q_rope = dquery[:, :, latent:].astype(jnp.bfloat16)
    d_qlat = dquery[:, :, :latent].astype(jnp.bfloat16)
    d_q_nope = jnp.einsum(
        "qhl,hnl->qhn", d_qlat, weight_k, preferred_element_type=jnp.float32
    ).astype(jnp.bfloat16)
    value_part = jnp.einsum("qht,qhl->tl", prob_low, d_olat, preferred_element_type=jnp.float32)
    dkeys = jnp.einsum("qht,qhc->tc", dscore, qfull, preferred_element_type=jnp.float32)
    dkeys = dkeys + jnp.pad(value_part, ((0, 0), (0, rope)))
    one_hot = (
        asked.reshape(-1)[:, None] == jnp.arange(own_blocks, dtype=jnp.int32)[None, :]
    ).astype(jnp.float32)
    returned = lax.all_to_all(
        dkeys.reshape(peers, per_peer, BLOCK_LEN * width).astype(jnp.bfloat16),
        "seq",
        split_axis=0,
        concat_axis=0,
        tiled=True,
    ).astype(jnp.float32)
    local_grad = jnp.dot(
        one_hot.T,
        returned.reshape(peers * per_peer, BLOCK_LEN * width),
        precision=lax.Precision.HIGHEST,
    )
    d_cache = (
        lax.psum(local_grad.astype(jnp.bfloat16), "grp")
        .astype(jnp.float32)
        .reshape(own_blocks * BLOCK_LEN, width)
    )
    return (attn_out, d_q_nope, d_q_rope, d_cache)


def solution(mesh):
    return jax.shard_map(
        local,
        mesh=mesh,
        in_specs=(
            P("seq", "grp", None),
            P("seq", "grp", None),
            P("seq", None),
            P("grp", "seq"),
            P("grp", "seq"),
            P("seq", "grp", None),
            P("seq", None),
            P("seq", None),
        ),
        out_specs=(
            P("seq", "grp", None),
            P("seq", "grp", None),
            P("seq", "grp", None),
            P("seq", None),
        ),
        check_vma=False,
    )
```

```python
import functools
import math

import jax
import jax.numpy as jnp
from jax import lax
from jax.experimental import pallas as pl
from jax.experimental.pallas import tpu as pltpu
from jax.sharding import PartitionSpec as P

BLOCK_LEN = 64
LANES = 128
HIDDEN = -1e30
VMEM = pl.BlockSpec(memory_space=pltpu.VMEM)
SMEM = pl.BlockSpec(memory_space=pltpu.SMEM)
ANY = pl.BlockSpec(memory_space=pl.ANY)
F32 = jnp.float32
BF16 = jnp.bfloat16


def call(kernel, name, args, specs, outs, scratch=(), mib=16, tied=None):
    out_shape = [jax.ShapeDtypeStruct(s, d) for s, d in outs]
    out_specs = [VMEM] * len(outs)
    aliases = {}
    body = kernel
    if tied is not None:
        args, specs = (tied, *args), [ANY] + specs
        out_shape, out_specs = [jax.ShapeDtypeStruct(tied.shape, tied.dtype)] + out_shape, [ANY] + out_specs
        aliases = {0: 0}
        n_in = len(args)

        def body(*refs):
            kernel(*refs[1:n_in], *refs[n_in + 1 :])

    return pl.pallas_call(
        body,
        out_shape=out_shape,
        in_specs=specs,
        out_specs=out_specs,
        scratch_shapes=list(scratch),
        input_output_aliases=aliases,
        compiler_params=pltpu.CompilerParams(vmem_limit_bytes=mib * 2**20),
        name=name,
    )(*args)


def nt(a, b):
    return lax.dot_general(a, b, (((1,), (1,)), ((), ())), preferred_element_type=F32)


def nn(a, b):
    return lax.dot_general(a, b, (((1,), (0,)), ((), ())), preferred_element_type=F32)


def swap(x, axis, bit):
    n = lax.axis_size(axis)
    return lax.ppermute(x, axis, [(i, i ^ bit) for i in range(n)])


def seq_swap(x):
    return lax.all_to_all(x, "seq", split_axis=0, concat_axis=0, tiled=True)


def exchange(pieces):
    return [pieces[0]] + [swap(p, "seq", k) for k, p in enumerate(pieces) if k > 0]


def tie_kernel(*refs):
    pass


def cut_kernel(ids, cache, out):
    depth = out.shape[0]
    out[...] = cache[pl.ds(pl.multiple_of(ids[1] * depth, 16), depth), :]


def gather_kernel(per_peer, ids, own, other, *refs):
    owners = len(refs) - 2
    caches, outs = refs[:owners], refs[owners:]
    lanes = per_peer * BLOCK_LEN

    def block(row, i, j):
        b = row[0, (ids[0] ^ (2 * i)) * per_peer + j]
        tile = caches[i][:, pl.ds(pl.multiple_of((b >> 1) * LANES, LANES), LANES)]
        return jnp.where((b & 1) == 1, tile[:, BLOCK_LEN:], tile[:, :BLOCK_LEN])

    for row, out in zip((other, own), outs):
        for i in range(owners):
            for j in range(0, per_peer, 2):
                both = jnp.concatenate([block(row, i, j), block(row, i, j + 1)], axis=1)
                at = i * lanes + j * BLOCK_LEN
                out[:, at : at + 2 * BLOCK_LEN] = both


def scatter_kernel(count, ids, rows, *refs):
    got, out, acc = refs[:count], refs[count], refs[count + 1]
    me = ids[0]
    depth, lanes = got[0].shape
    per_peer = lanes // BLOCK_LEN
    acc[...] = jnp.zeros_like(acc)
    blank = jnp.zeros((depth, BLOCK_LEN), F32)
    for k in range(count):
        for j in range(per_peer):
            b = rows[k, me * per_peer + j]
            at = pl.ds(pl.multiple_of((b >> 1) * LANES, LANES), LANES)
            g = got[k][:, j * BLOCK_LEN : (j + 1) * BLOCK_LEN].astype(F32)
            low = jnp.concatenate([g, blank], axis=1)
            high = jnp.concatenate([blank, g], axis=1)
            acc[:, at] = acc[:, at] + jnp.where((b & 1) == 1, high, low)
    out[...] = acc[...].astype(BF16)


def assemble_kernel(ids, *refs):
    parts, out = refs[:-1], refs[-1]
    depth = parts[0].shape[0]
    for k, y in enumerate(parts):
        out[pl.ds(pl.multiple_of((ids[1] ^ k) * depth, 16), depth), :] = y[...].astype(F32)


def weight_k_of(pack, head, uk_rows, tiles):
    rows = uk_rows // tiles
    peers = pack.shape[0]
    cols = []
    for t in range(tiles):
        cols.append(
            jnp.concatenate(
                [pack[r, head, t * rows : (t + 1) * rows, :] for r in range(peers)], axis=0
            )
        )
    return jnp.concatenate(cols, axis=1)


def stacked(pack, head, start, rows):
    peers = pack.shape[0]
    return jnp.concatenate([pack[r, head, start : start + rows, :] for r in range(peers)], axis=0)


def expand_kernel(sizes, pack, out):
    uk_rows, uv_rows, queries, tiles, latent = sizes
    peers, heads = pack.shape[0], pack.shape[1]
    for h in range(heads):
        wk = weight_k_of(pack, h, uk_rows, tiles)
        wv = stacked(pack, h, uk_rows, uv_rows)
        qn = stacked(pack, h, uk_rows + uv_rows, queries)
        do = stacked(pack, h, uk_rows + uv_rows + queries, queries)
        q_lat = nn(qn, wk).astype(BF16)
        d_olat = nt(do, wv).astype(BF16)
        for r in range(peers):
            out[r, h, :, :latent] = q_lat[r * queries : (r + 1) * queries]
            out[r, h, :, latent:] = d_olat[r * queries : (r + 1) * queries]


def reduce_kernel(sizes, pack, lat, out):
    uk_rows, uv_rows, queries, tiles, latent = sizes
    peers, heads = pack.shape[0], pack.shape[1]
    for h in range(heads):
        wk = weight_k_of(pack, h, uk_rows, tiles)
        wv = stacked(pack, h, uk_rows, uv_rows)
        both = jnp.concatenate([lat[r, h] for r in range(peers)], axis=0)
        attn = nn(both[:, :latent], wv).astype(BF16)
        dqn = nt(both[:, latent:], wk).astype(BF16)
        for r in range(peers):
            out[r, h, :, : attn.shape[1]] = attn[r * queries : (r + 1) * queries]
            out[r, h, :, attn.shape[1] :] = dqn[r * queries : (r + 1) * queries]


def tokens_grad(grads, scale, do, cat, delta, kt, p, width):
    keep, send, at, depth = grads
    latent = do.shape[1]
    dp = nn(do[...], kt[:latent])
    ds = (p.astype(F32) * (dp - delta) * scale).astype(BF16)
    part = nt(ds, kt[:width])
    dk = nn(cat[...], jnp.concatenate([ds, p], axis=0)).astype(BF16)
    for k, ref in enumerate((keep, send, keep, send)):
        ref[k // 2, :, at] = dk[k * depth : (k + 1) * depth]
    return part


def attend_kernel(scale, per_peer, ids, sel, rope, qd, *refs):
    keys, refs = (refs[:4], refs[4:8]), refs[9:]
    keeps, sends, lat, d_rope, refs = (refs[0], refs[2]), (refs[1], refs[3]), refs[4], refs[5], refs[6:]
    kt_near, kt_far, pb_near, pb_far, qx, do, sc, flip, cat, o_full, dq = refs
    rows, latent = do.shape
    heads, queries, rope_dim = rope.shape
    width = latent + rope_dim
    slots = qx.shape[1] - width
    depth, half = keys[0][0].shape
    held = 4
    lanes = half // held
    kts, pbs = (kt_near, kt_far), (pb_near, pb_far)

    picks = sel[...] ^ (ids[0] * per_peer)
    slot = lax.broadcasted_iota(jnp.int32, (queries, slots), 1)
    chosen = picks[:, 0:1] == slot
    for j in range(1, picks.shape[1]):
        chosen = chosen | (picks[:, j : j + 1] == slot)
    bias = jnp.where(chosen, 0.0, HIDDEN).astype(BF16)
    bias = jnp.broadcast_to(bias[None], (heads, queries, slots)).reshape(rows, slots)
    qx[:, :latent] = qd[:, :latent]
    qx[:, latent:] = jnp.concatenate([rope[...].reshape(rows, rope_dim), bias], axis=1)
    do[...] = qd[:, latent:]
    for c in range(2):
        for k in range(4):
            at = pl.ds(pl.multiple_of((ids[1] ^ k) * depth, 16), depth)
            for i in range(held):
                peer = c * held + i
                src = keys[peer % 2][k][:, (peer // 2) * lanes : (peer // 2 + 1) * lanes]
                kts[c][at, i * lanes : (i + 1) * lanes] = src
        place = lax.broadcasted_iota(jnp.int32, (slots, half), 0)
        token = lax.broadcasted_iota(jnp.int32, (slots, half), 1) + c * half
        kts[c][width:, :] = jnp.where(token // BLOCK_LEN == place, 1.0, 0.0).astype(BF16)

    scale2 = scale * math.log2(math.e)
    step = 512
    chunks = [(c, i) for c in range(2) for i in range(0, half, step)]
    top = jnp.full((rows, 1), -jnp.inf, F32)
    for n, (c, i) in enumerate(chunks):
        s = nn(qx[...], kts[c][:, i : i + step]) * scale2
        sc[:, n * step : (n + 1) * step] = s
        top = jnp.maximum(top, jnp.max(s, axis=1, keepdims=True))
    total = jnp.zeros((rows, 1), F32)
    for n in range(len(chunks)):
        e = jnp.exp2(sc[:, n * step : (n + 1) * step] - top)
        sc[:, n * step : (n + 1) * step] = e
        total = total + jnp.sum(e, axis=1, keepdims=True)
    inv = 1.0 / total
    for n, (c, i) in enumerate(chunks):
        pb = (sc[:, n * step : (n + 1) * step] * inv).astype(BF16)
        pbs[c][:, i : i + step] = pb
        part = nt(pb, kts[c][:latent, i : i + step])
        if n == 0:
            o_full[...] = part
        else:
            o_full[...] += part
    lat[:, :latent] = o_full[...].astype(BF16)
    delta = jnp.sum(o_full[...] * do[...].astype(F32), axis=1, keepdims=True)

    flip[:, :rows] = qx[:, :width].T
    flip[:latent, rows:] = do[...].T
    flip[latent:, rows:] = jnp.zeros((rope_dim, rows), BF16)
    for k in range(4):
        at = pl.ds(pl.multiple_of((ids[1] ^ k) * depth, 16), depth)
        cat[k * depth : (k + 1) * depth] = flip[at, :]
    for n, (c, i) in enumerate([(c, i) for c in (1, 0) for i in range(0, half, step)]):
        at = slice(i, i + step)
        grads = (keeps[c], sends[c], at, depth)
        kt = kts[c].at[:, at]
        part = tokens_grad(grads, scale, do, cat, delta, kt, pbs[c][:, at], width)
        if n == 0:
            dq[...] = part
        else:
            dq[...] += part
    lat[:, latent:] = dq[:, :latent].astype(BF16)
    d_rope[...] = dq[:, latent:].astype(BF16)


def pair_kernel(keep, got, a0, *a2):
    total = keep[...].astype(F32) + got[...].astype(F32)
    a0[...] = total[0].astype(BF16)
    lanes = a2[0].shape[1]
    for i, a in enumerate(a2):
        a[...] = total[1, :, i * lanes : (i + 1) * lanes].astype(BF16)


def owner_kernel(a0, got, *outs):
    total = (a0[...].astype(F32) + got[...].astype(F32)).astype(BF16)
    lanes = outs[0].shape[1]
    for i, out in enumerate(outs):
        out[...] = total[:, i * lanes : (i + 1) * lanes]


def local(q_nope, q_rope, cache, w_uk, w_uv, d_out, sel, slot_blocks):
    peers = lax.axis_size("seq")
    groups = lax.axis_size("grp")
    queries, heads, nope = q_nope.shape
    rope = q_rope.shape[2]
    width = cache.shape[1]
    latent = width - rope
    value = d_out.shape[2]
    slots = slot_blocks.shape[1]
    per_peer = slots // peers
    if not (peers == 8 and groups == 4 and heads % peers == 0 and per_peer % 2 == 0):
        return local_general(q_nope, q_rope, cache, w_uk, w_uv, d_out, sel, slot_blocks)
    ids = jnp.stack([lax.axis_index("seq"), lax.axis_index("grp")]).astype(jnp.int32)
    tokens = cache.shape[0]
    depth = width // groups
    lanes = per_peer * BLOCK_LEN
    held = peers // 2
    half = held * lanes
    share = heads // peers
    rows = heads * queries
    scale = 1.0 / math.sqrt(nope + rope)

    row1 = swap(slot_blocks, "seq", 1)
    (c0,) = call(cut_kernel, "cut", (ids, cache.T), [SMEM, VMEM], [((depth, tokens), BF16)])
    c2 = swap(c0, "seq", 4)
    c1 = swap(c0, "seq", 2)
    asked = jnp.concatenate([slot_blocks, row1], axis=0)
    for bit in (2, 4):
        asked = jnp.concatenate([asked, swap(asked, "seq", bit)], axis=0)

    n_rows = w_uk.shape[1] // latent
    l_rows = w_uv.shape[1] // value
    tiles = latent // LANES
    uk = w_uk.reshape(heads, n_rows, tiles, LANES).transpose(0, 2, 1, 3)
    pack = jnp.concatenate(
        [
            uk.reshape(heads, n_rows * tiles, LANES),
            w_uv.reshape(heads, l_rows, value),
            q_nope.transpose(1, 0, 2),
            d_out.transpose(1, 0, 2),
        ],
        axis=1,
    )
    (pack,) = call(tie_kernel, "after", (c2, asked), [ANY] * 2, [], tied=pack)
    pack = seq_swap(pack).reshape(peers, share, -1, LANES)
    sizes = (n_rows * tiles, l_rows, queries, tiles, latent)
    (lat,) = call(
        functools.partial(expand_kernel, sizes),
        "expand",
        (pack,),
        [VMEM],
        [((peers, share, queries, 2 * latent), BF16)],
    )
    qd = seq_swap(lat).reshape(rows, 2 * latent)

    c3 = swap(c2, "seq", 2)
    away, k0 = call(
        functools.partial(gather_kernel, per_peer),
        "gather",
        (ids, slot_blocks, row1, c0, c1, c2, c3),
        [SMEM] * 3 + [VMEM] * 4,
        [((depth, half), BF16)] * 2,
    )
    keys = []
    for k in (k0, swap(away, "seq", 1)):
        k2 = swap(k, "grp", 2)
        keys += [k, swap(k, "grp", 1), k2, swap(k2, "grp", 1)]
    rope_rows = q_rope.transpose(1, 0, 2)
    near_keep, near_send, far_keep, far_send, lat, d_rope = call(
        functools.partial(attend_kernel, scale, per_peer),
        "attend",
        (ids, sel, rope_rows, qd, *keys, asked),
        [SMEM] + [VMEM] * 11 + [ANY],
        [((2, depth, half), BF16)] * 4 + [((rows, 2 * latent), BF16), ((rows, rope), BF16)],
        [pltpu.VMEM((width + slots, half), BF16)] * 2
        + [pltpu.VMEM((rows, half), BF16)] * 2
        + [
            pltpu.VMEM((rows, width + slots), BF16),
            pltpu.VMEM((rows, latent), BF16),
            pltpu.VMEM((rows, 2 * half), F32),
            pltpu.VMEM((width, 2 * rows), BF16),
            pltpu.VMEM((width, 2 * rows), BF16),
            pltpu.VMEM((rows, latent), F32),
            pltpu.VMEM((rows, width), F32),
        ],
        60,
    )

    def pair(keep, send, tied=None):
        outs = [((depth, half), BF16)] * 2
        return call(pair_kernel, "pair", (keep, swap(send, "grp", 1)), [VMEM] * 2, outs, tied=tied)


    def owner(a0, a2, tied=None):
        outs = [((depth, lanes), BF16)] * held
        return call(owner_kernel, "owner", (a0, swap(a2, "grp", 2)), [VMEM] * 2, outs, tied=tied)

    far = pair(far_keep, far_send)
    first, *near = pair(near_keep, near_send, tied=far[0])
    far = owner(first, far[1])
    lat = seq_swap(lat.reshape(peers, share, queries, 2 * latent))
    (res,) = call(
        functools.partial(reduce_kernel, sizes),
        "reduce",
        (pack, lat),
        [VMEM] * 2,
        [((peers, share, queries, value + nope), BF16)],
    )
    res, *near = owner(*near, tied=res)
    got = exchange([*near, *far])
    res = seq_swap(res).reshape(heads, queries, value + nope)

    (y0,) = call(
        functools.partial(scatter_kernel, peers),
        "scatter",
        (ids, asked, *got),
        [SMEM, SMEM] + [VMEM] * peers,
        [((depth, tokens), BF16)],
        [pltpu.VMEM((depth, tokens), F32)],
    )
    y2 = swap(y0, "grp", 2)
    y1 = swap(y0, "grp", 1)
    y3 = swap(y2, "grp", 1)
    (d_cache,) = call(
        assemble_kernel,
        "assemble",
        (ids, y0, y1, y2, y3),
        [SMEM] + [VMEM] * 4,
        [((width, tokens), F32)],
    )
    return (
        res[:, :, :value].transpose(1, 0, 2),
        res[:, :, value:].transpose(1, 0, 2),
        d_rope.reshape(heads, queries, rope).transpose(1, 0, 2),
        d_cache.T,
    )


def local_general(q_nope, q_rope, cache, w_uk, w_uv, d_out, sel, slot_blocks):
    peers = lax.axis_size("seq")
    queries, heads, nope = q_nope.shape
    rope = q_rope.shape[2]
    width = cache.shape[1]
    latent = width - rope
    value = d_out.shape[2]
    slot_total = slot_blocks.shape[1]
    per_peer = slot_total // peers
    own_blocks = cache.shape[0] // BLOCK_LEN
    scale = 1.0 / math.sqrt(nope + rope)
    gathered_k, gathered_v = (
        lax.all_gather(w_uk, "seq", axis=1, tiled=True),
        lax.all_gather(w_uv, "seq", axis=1, tiled=True),
    )
    weight_k = gathered_k.reshape(heads, nope, latent)
    weight_v = gathered_v.reshape(heads, latent, value)
    wanted = slot_blocks.reshape(peers, per_peer)
    asked = lax.all_to_all(wanted, "seq", split_axis=0, concat_axis=0, tiled=True)
    blocks = cache.reshape(own_blocks, BLOCK_LEN, width)
    arrived = lax.all_to_all(blocks[asked], "seq", split_axis=0, concat_axis=0, tiled=True)
    keys = arrived.reshape(slot_total * BLOCK_LEN, width)
    keys_lat = keys[:, :latent]
    q_lat = jnp.einsum("qhn,hnl->qhl", q_nope, weight_k, preferred_element_type=jnp.float32).astype(
        jnp.bfloat16
    )
    qfull = jnp.concatenate([q_lat, q_rope], axis=-1)
    chosen = jnp.any(
        sel[:, :, None] == jnp.arange(slot_total, dtype=jnp.int32)[None, None, :], axis=1
    )
    live = jnp.repeat(chosen, BLOCK_LEN, axis=1)[:, None, :]
    score = jnp.einsum("qhc,tc->qht", qfull, keys, preferred_element_type=jnp.float32) * scale
    score = jnp.where(live, score, -jnp.inf)
    prob = jax.nn.softmax(score, axis=-1)
    prob_low = prob.astype(jnp.bfloat16)
    olat = jnp.einsum("qht,tl->qhl", prob_low, keys_lat, preferred_element_type=jnp.float32).astype(
        jnp.bfloat16
    )
    attn_out = jnp.einsum(
        "qhl,hlv->qhv", olat, weight_v, preferred_element_type=jnp.float32
    ).astype(jnp.bfloat16)
    d_olat = jnp.einsum("qhv,hlv->qhl", d_out, weight_v, preferred_element_type=jnp.float32).astype(
        jnp.bfloat16
    )
    dprob = jnp.einsum("qhl,tl->qht", d_olat, keys_lat, preferred_element_type=jnp.float32)
    delta = jnp.sum(prob * dprob, axis=-1, keepdims=True)
    dscore = (prob * (dprob - delta) * scale).astype(jnp.bfloat16)
    dquery = jnp.einsum("qht,tc->qhc", dscore, keys, preferred_element_type=jnp.float32)
    d_q_rope = dquery[:, :, latent:].astype(jnp.bfloat16)
    d_qlat = dquery[:, :, :latent].astype(jnp.bfloat16)
    d_q_nope = jnp.einsum(
        "qhl,hnl->qhn", d_qlat, weight_k, preferred_element_type=jnp.float32
    ).astype(jnp.bfloat16)
    value_part = jnp.einsum("qht,qhl->tl", prob_low, d_olat, preferred_element_type=jnp.float32)
    dkeys = jnp.einsum("qht,qhc->tc", dscore, qfull, preferred_element_type=jnp.float32)
    dkeys = dkeys + jnp.pad(value_part, ((0, 0), (0, rope)))
    one_hot = (
        asked.reshape(-1)[:, None] == jnp.arange(own_blocks, dtype=jnp.int32)[None, :]
    ).astype(jnp.float32)
    returned = lax.all_to_all(
        dkeys.reshape(peers, per_peer, BLOCK_LEN * width).astype(jnp.bfloat16),
        "seq",
        split_axis=0,
        concat_axis=0,
        tiled=True,
    ).astype(jnp.float32)
    local_grad = jnp.dot(
        one_hot.T,
        returned.reshape(peers * per_peer, BLOCK_LEN * width),
        precision=lax.Precision.HIGHEST,
    )
    d_cache = (
        lax.psum(local_grad.astype(jnp.bfloat16), "grp")
        .astype(jnp.float32)
        .reshape(own_blocks * BLOCK_LEN, width)
    )
    return (attn_out, d_q_nope, d_q_rope, d_cache)


def solution(mesh):
    return jax.shard_map(
        local,
        mesh=mesh,
        in_specs=(
            P("seq", "grp", None),
            P("seq", "grp", None),
            P("seq", None),
            P("grp", "seq"),
            P("grp", "seq"),
            P("seq", "grp", None),
            P("seq", None),
            P("seq", None),
        ),
        out_specs=(
            P("seq", "grp", None),
            P("seq", "grp", None),
            P("seq", "grp", None),
            P("seq", None),
        ),
        check_vma=False,
    )
```

```python
import functools
import math

import jax
import jax.numpy as jnp
from jax import lax
from jax.experimental import pallas as pl
from jax.experimental.pallas import tpu as pltpu
from jax.sharding import PartitionSpec as P

BLOCK_LEN = 64
LANES = 128
HIDDEN = -1e30
VMEM = pl.BlockSpec(memory_space=pltpu.VMEM)
SMEM = pl.BlockSpec(memory_space=pltpu.SMEM)
ANY = pl.BlockSpec(memory_space=pl.ANY)
F32 = jnp.float32
BF16 = jnp.bfloat16


def call(kernel, name, args, specs, outs, scratch=(), mib=16, tied=None):
    out_shape = [jax.ShapeDtypeStruct(s, d) for s, d in outs]
    out_specs = [VMEM] * len(outs)
    aliases = {}
    body = kernel
    if tied is not None:
        args, specs = (tied, *args), [ANY] + specs
        out_shape, out_specs = [jax.ShapeDtypeStruct(tied.shape, tied.dtype)] + out_shape, [ANY] + out_specs
        aliases = {0: 0}
        n_in = len(args)

        def body(*refs):
            kernel(*refs[1:n_in], *refs[n_in + 1 :])

    return pl.pallas_call(
        body,
        out_shape=out_shape,
        in_specs=specs,
        out_specs=out_specs,
        scratch_shapes=list(scratch),
        input_output_aliases=aliases,
        compiler_params=pltpu.CompilerParams(vmem_limit_bytes=mib * 2**20),
        name=name,
    )(*args)


def nt(a, b):
    return lax.dot_general(a, b, (((1,), (1,)), ((), ())), preferred_element_type=F32)


def nn(a, b):
    return lax.dot_general(a, b, (((1,), (0,)), ((), ())), preferred_element_type=F32)


def swap(x, axis, bit):
    n = lax.axis_size(axis)
    return lax.ppermute(x, axis, [(i, i ^ bit) for i in range(n)])


def seq_swap(x):
    return lax.all_to_all(x, "seq", split_axis=0, concat_axis=0, tiled=True)


def exchange(pieces):
    return [pieces[0]] + [swap(p, "seq", k) for k, p in enumerate(pieces) if k > 0]


def tie_kernel(*refs):
    pass


def cut_kernel(ids, cache, out):
    depth = out.shape[0]
    out[...] = cache[pl.ds(pl.multiple_of(ids[1] * depth, 16), depth), :]


def gather_kernel(per_peer, ids, own, other, *refs):
    owners = len(refs) - 3
    caches, outs = refs[:owners], refs[owners + 1 :]
    lanes = per_peer * BLOCK_LEN

    def block(row, i, j):
        b = row[0, (ids[0] ^ (2 * i)) * per_peer + j]
        tile = caches[i][:, pl.ds(pl.multiple_of((b >> 1) * LANES, LANES), LANES)]
        return jnp.where((b & 1) == 1, tile[:, BLOCK_LEN:], tile[:, :BLOCK_LEN])

    for row, out in zip((other, own), outs):
        for i in range(owners):
            for j in range(0, per_peer, 2):
                both = jnp.concatenate([block(row, i, j), block(row, i, j + 1)], axis=1)
                at = i * lanes + j * BLOCK_LEN
                out[:, at : at + 2 * BLOCK_LEN] = both


def scatter_kernel(count, ids, rows, *refs):
    got, out, acc = refs[:count], refs[count], refs[count + 1]
    me = ids[0]
    depth, lanes = got[0].shape
    per_peer = lanes // BLOCK_LEN
    acc[...] = jnp.zeros_like(acc)
    blank = jnp.zeros((depth, BLOCK_LEN), F32)
    for k in range(count):
        for j in range(per_peer):
            b = rows[k, me * per_peer + j]
            at = pl.ds(pl.multiple_of((b >> 1) * LANES, LANES), LANES)
            g = got[k][:, j * BLOCK_LEN : (j + 1) * BLOCK_LEN].astype(F32)
            low = jnp.concatenate([g, blank], axis=1)
            high = jnp.concatenate([blank, g], axis=1)
            acc[:, at] = acc[:, at] + jnp.where((b & 1) == 1, high, low)
    out[...] = acc[...].astype(BF16)


def assemble_kernel(ids, *refs):
    parts, out = refs[:-1], refs[-1]
    depth = parts[0].shape[0]
    for k, y in enumerate(parts):
        out[pl.ds(pl.multiple_of((ids[1] ^ k) * depth, 16), depth), :] = y[...].astype(F32)


def weight_k_of(pack, head, uk_rows, tiles):
    rows = uk_rows // tiles
    peers = pack.shape[0]
    cols = []
    for t in range(tiles):
        cols.append(
            jnp.concatenate(
                [pack[r, head, t * rows : (t + 1) * rows, :] for r in range(peers)], axis=0
            )
        )
    return jnp.concatenate(cols, axis=1)


def stacked(pack, head, start, rows):
    peers = pack.shape[0]
    return jnp.concatenate([pack[r, head, start : start + rows, :] for r in range(peers)], axis=0)


def expand_kernel(sizes, pack, away, asked, out):
    uk_rows, uv_rows, queries, tiles, latent = sizes
    peers, heads = pack.shape[0], pack.shape[1]
    for h in range(heads):
        wk = weight_k_of(pack, h, uk_rows, tiles)
        wv = stacked(pack, h, uk_rows, uv_rows)
        qn = stacked(pack, h, uk_rows + uv_rows, queries)
        do = stacked(pack, h, uk_rows + uv_rows + queries, queries)
        q_lat = nn(qn, wk).astype(BF16)
        d_olat = nt(do, wv).astype(BF16)
        for r in range(peers):
            out[r, h, :, :latent] = q_lat[r * queries : (r + 1) * queries]
            out[r, h, :, latent:] = d_olat[r * queries : (r + 1) * queries]


def reduce_kernel(sizes, pack, lat, out):
    uk_rows, uv_rows, queries, tiles, latent = sizes
    peers, heads = pack.shape[0], pack.shape[1]
    for h in range(heads):
        wk = weight_k_of(pack, h, uk_rows, tiles)
        wv = stacked(pack, h, uk_rows, uv_rows)
        both = jnp.concatenate([lat[r, h] for r in range(peers)], axis=0)
        attn = nn(both[:, :latent], wv).astype(BF16)
        dqn = nt(both[:, latent:], wk).astype(BF16)
        for r in range(peers):
            out[r, h, :, : attn.shape[1]] = attn[r * queries : (r + 1) * queries]
            out[r, h, :, attn.shape[1] :] = dqn[r * queries : (r + 1) * queries]


def tokens_grad(grads, scale, do, cat, delta, kt, p, width):
    keep, send, at, depth = grads
    latent = do.shape[1]
    dp = nn(do[...], kt[:latent])
    ds = (p.astype(F32) * (dp - delta) * scale).astype(BF16)
    part = nt(ds, kt[:width])
    dk = nn(cat[...], jnp.concatenate([ds, p], axis=0)).astype(BF16)
    for k, ref in enumerate((keep, send, keep, send)):
        ref[k // 2, :, at] = dk[k * depth : (k + 1) * depth]
    return part


def attend_kernel(scale, per_peer, ids, sel, rope, qd, *refs):
    keys, refs = (refs[:4], refs[4:8]), refs[8:]
    keeps, sends, lat, d_rope, refs = (refs[0], refs[2]), (refs[1], refs[3]), refs[4], refs[5], refs[6:]
    kt_near, kt_far, pb_near, pb_far, qx, do, sc, flip, cat, o_full, dq = refs
    rows, latent = do.shape
    heads, queries, rope_dim = rope.shape
    width = latent + rope_dim
    slots = qx.shape[1] - width
    depth, half = keys[0][0].shape
    held = 4
    lanes = half // held
    kts, pbs = (kt_near, kt_far), (pb_near, pb_far)

    picks = sel[...] ^ (ids[0] * per_peer)
    slot = lax.broadcasted_iota(jnp.int32, (queries, slots), 1)
    chosen = picks[:, 0:1] == slot
    for j in range(1, picks.shape[1]):
        chosen = chosen | (picks[:, j : j + 1] == slot)
    bias = jnp.where(chosen, 0.0, HIDDEN).astype(BF16)
    bias = jnp.broadcast_to(bias[None], (heads, queries, slots)).reshape(rows, slots)
    qx[:, :latent] = qd[:, :latent]
    qx[:, latent:] = jnp.concatenate([rope[...].reshape(rows, rope_dim), bias], axis=1)
    do[...] = qd[:, latent:]
    for c in range(2):
        for k in range(4):
            at = pl.ds(pl.multiple_of((ids[1] ^ k) * depth, 16), depth)
            for i in range(held):
                peer = c * held + i
                src = keys[peer % 2][k][:, (peer // 2) * lanes : (peer // 2 + 1) * lanes]
                kts[c][at, i * lanes : (i + 1) * lanes] = src
        place = lax.broadcasted_iota(jnp.int32, (slots, half), 0)
        token = lax.broadcasted_iota(jnp.int32, (slots, half), 1) + c * half
        kts[c][width:, :] = jnp.where(token // BLOCK_LEN == place, 1.0, 0.0).astype(BF16)

    scale2 = scale * math.log2(math.e)
    step = 512
    chunks = [(c, i) for c in range(2) for i in range(0, half, step)]
    top = jnp.full((rows, 1), -jnp.inf, F32)
    for n, (c, i) in enumerate(chunks):
        s = nn(qx[...], kts[c][:, i : i + step]) * scale2
        sc[:, n * step : (n + 1) * step] = s
        top = jnp.maximum(top, jnp.max(s, axis=1, keepdims=True))
    total = jnp.zeros((rows, 1), F32)
    for n in range(len(chunks)):
        e = jnp.exp2(sc[:, n * step : (n + 1) * step] - top)
        sc[:, n * step : (n + 1) * step] = e
        total = total + jnp.sum(e, axis=1, keepdims=True)
    inv = 1.0 / total
    for n, (c, i) in enumerate(chunks):
        pb = (sc[:, n * step : (n + 1) * step] * inv).astype(BF16)
        pbs[c][:, i : i + step] = pb
        part = nt(pb, kts[c][:latent, i : i + step])
        if n == 0:
            o_full[...] = part
        else:
            o_full[...] += part
    lat[:, :latent] = o_full[...].astype(BF16)
    delta = jnp.sum(o_full[...] * do[...].astype(F32), axis=1, keepdims=True)

    flip[:, :rows] = qx[:, :width].T
    flip[:latent, rows:] = do[...].T
    flip[latent:, rows:] = jnp.zeros((rope_dim, rows), BF16)
    for k in range(4):
        at = pl.ds(pl.multiple_of((ids[1] ^ k) * depth, 16), depth)
        cat[k * depth : (k + 1) * depth] = flip[at, :]
    for n, (c, i) in enumerate([(c, i) for c in (1, 0) for i in range(0, half, step)]):
        at = slice(i, i + step)
        grads = (keeps[c], sends[c], at, depth)
        kt = kts[c].at[:, at]
        part = tokens_grad(grads, scale, do, cat, delta, kt, pbs[c][:, at], width)
        if n == 0:
            dq[...] = part
        else:
            dq[...] += part
    lat[:, latent:] = dq[:, :latent].astype(BF16)
    d_rope[...] = dq[:, latent:].astype(BF16)


def pair_kernel(keep, got, a0, *a2):
    total = keep[...].astype(F32) + got[...].astype(F32)
    a0[...] = total[0].astype(BF16)
    lanes = a2[0].shape[1]
    for i, a in enumerate(a2):
        a[...] = total[1, :, i * lanes : (i + 1) * lanes].astype(BF16)


def owner_kernel(a0, got, *outs):
    total = (a0[...].astype(F32) + got[...].astype(F32)).astype(BF16)
    lanes = outs[0].shape[1]
    for i, out in enumerate(outs):
        out[...] = total[:, i * lanes : (i + 1) * lanes]


def local(q_nope, q_rope, cache, w_uk, w_uv, d_out, sel, slot_blocks):
    peers = lax.axis_size("seq")
    groups = lax.axis_size("grp")
    queries, heads, nope = q_nope.shape
    rope = q_rope.shape[2]
    width = cache.shape[1]
    latent = width - rope
    value = d_out.shape[2]
    slots = slot_blocks.shape[1]
    per_peer = slots // peers
    if not (peers == 8 and groups == 4 and heads % peers == 0 and per_peer % 2 == 0):
        return local_general(q_nope, q_rope, cache, w_uk, w_uv, d_out, sel, slot_blocks)
    ids = jnp.stack([lax.axis_index("seq"), lax.axis_index("grp")]).astype(jnp.int32)
    tokens = cache.shape[0]
    depth = width // groups
    lanes = per_peer * BLOCK_LEN
    held = peers // 2
    half = held * lanes
    share = heads // peers
    rows = heads * queries
    scale = 1.0 / math.sqrt(nope + rope)

    row1 = swap(slot_blocks, "seq", 1)
    (c0,) = call(cut_kernel, "cut", (ids, cache.T), [SMEM, VMEM], [((depth, tokens), BF16)])
    c2 = swap(c0, "seq", 4)
    c1 = swap(c0, "seq", 2)
    asked_y = jnp.concatenate([slot_blocks, row1], axis=0)
    asked_z = jnp.concatenate([asked_y, swap(asked_y, "seq", 2)], axis=0)
    asked = jnp.concatenate([asked_z, swap(asked_z, "seq", 4)], axis=0)

    n_rows = w_uk.shape[1] // latent
    l_rows = w_uv.shape[1] // value
    tiles = latent // LANES
    uk = w_uk.reshape(heads, n_rows, tiles, LANES).transpose(0, 2, 1, 3)
    pack = jnp.concatenate(
        [
            uk.reshape(heads, n_rows * tiles, LANES),
            w_uv.reshape(heads, l_rows, value),
            q_nope.transpose(1, 0, 2),
            d_out.transpose(1, 0, 2),
        ],
        axis=1,
    )
    (pack,) = call(tie_kernel, "after", (c2,), [ANY], [], tied=pack)
    pack = seq_swap(pack).reshape(peers, share, -1, LANES)
    c3 = swap(c2, "seq", 2)
    away, k0 = call(
        functools.partial(gather_kernel, per_peer),
        "gather",
        (ids, slot_blocks, row1, c0, c1, c2, c3, asked_z),
        [SMEM] * 3 + [VMEM] * 4 + [ANY],
        [((depth, half), BF16)] * 2,
    )
    sizes = (n_rows * tiles, l_rows, queries, tiles, latent)
    (lat,) = call(
        functools.partial(expand_kernel, sizes),
        "expand",
        (pack, away, asked),
        [VMEM, ANY, ANY],
        [((peers, share, queries, 2 * latent), BF16)],
    )
    qd = seq_swap(lat).reshape(rows, 2 * latent)

    keys = []
    for k in (k0, swap(away, "seq", 1)):
        k2 = swap(k, "grp", 2)
        keys += [k, swap(k, "grp", 1), k2, swap(k2, "grp", 1)]
    rope_rows = q_rope.transpose(1, 0, 2)
    near_keep, near_send, far_keep, far_send, lat, d_rope = call(
        functools.partial(attend_kernel, scale, per_peer),
        "attend",
        (ids, sel, rope_rows, qd, *keys),
        [SMEM] + [VMEM] * 11,
        [((2, depth, half), BF16)] * 4 + [((rows, 2 * latent), BF16), ((rows, rope), BF16)],
        [pltpu.VMEM((width + slots, half), BF16)] * 2
        + [pltpu.VMEM((rows, half), BF16)] * 2
        + [
            pltpu.VMEM((rows, width + slots), BF16),
            pltpu.VMEM((rows, latent), BF16),
            pltpu.VMEM((rows, 2 * half), F32),
            pltpu.VMEM((width, 2 * rows), BF16),
            pltpu.VMEM((width, 2 * rows), BF16),
            pltpu.VMEM((rows, latent), F32),
            pltpu.VMEM((rows, width), F32),
        ],
        60,
    )

    def pair(keep, send, tied=None):
        outs = [((depth, half), BF16)] * 2
        return call(pair_kernel, "pair", (keep, swap(send, "grp", 1)), [VMEM] * 2, outs, tied=tied)


    def owner(a0, a2, tied=None):
        outs = [((depth, lanes), BF16)] * held
        return call(owner_kernel, "owner", (a0, swap(a2, "grp", 2)), [VMEM] * 2, outs, tied=tied)

    far = pair(far_keep, far_send)
    first, *near = pair(near_keep, near_send, tied=far[0])
    far = owner(first, far[1])
    lat = seq_swap(lat.reshape(peers, share, queries, 2 * latent))
    (res,) = call(
        functools.partial(reduce_kernel, sizes),
        "reduce",
        (pack, lat),
        [VMEM] * 2,
        [((peers, share, queries, value + nope), BF16)],
    )
    near = owner(*near)
    (res,) = call(tie_kernel, "after", (near[0],), [ANY], [], tied=res)
    got = exchange([*near, *far])
    res = seq_swap(res).reshape(heads, queries, value + nope)

    (y0,) = call(
        functools.partial(scatter_kernel, peers),
        "scatter",
        (ids, asked, *got),
        [SMEM, SMEM] + [VMEM] * peers,
        [((depth, tokens), BF16)],
        [pltpu.VMEM((depth, tokens), F32)],
    )
    y2 = swap(y0, "grp", 2)
    y1 = swap(y0, "grp", 1)
    y3 = swap(y2, "grp", 1)
    (d_cache,) = call(
        assemble_kernel,
        "assemble",
        (ids, y0, y1, y2, y3),
        [SMEM] + [VMEM] * 4,
        [((width, tokens), F32)],
    )
    return (
        res[:, :, :value].transpose(1, 0, 2),
        res[:, :, value:].transpose(1, 0, 2),
        d_rope.reshape(heads, queries, rope).transpose(1, 0, 2),
        d_cache.T,
    )


def local_general(q_nope, q_rope, cache, w_uk, w_uv, d_out, sel, slot_blocks):
    peers = lax.axis_size("seq")
    queries, heads, nope = q_nope.shape
    rope = q_rope.shape[2]
    width = cache.shape[1]
    latent = width - rope
    value = d_out.shape[2]
    slot_total = slot_blocks.shape[1]
    per_peer = slot_total // peers
    own_blocks = cache.shape[0] // BLOCK_LEN
    scale = 1.0 / math.sqrt(nope + rope)
    gathered_k, gathered_v = (
        lax.all_gather(w_uk, "seq", axis=1, tiled=True),
        lax.all_gather(w_uv, "seq", axis=1, tiled=True),
    )
    weight_k = gathered_k.reshape(heads, nope, latent)
    weight_v = gathered_v.reshape(heads, latent, value)
    wanted = slot_blocks.reshape(peers, per_peer)
    asked = lax.all_to_all(wanted, "seq", split_axis=0, concat_axis=0, tiled=True)
    blocks = cache.reshape(own_blocks, BLOCK_LEN, width)
    arrived = lax.all_to_all(blocks[asked], "seq", split_axis=0, concat_axis=0, tiled=True)
    keys = arrived.reshape(slot_total * BLOCK_LEN, width)
    keys_lat = keys[:, :latent]
    q_lat = jnp.einsum("qhn,hnl->qhl", q_nope, weight_k, preferred_element_type=jnp.float32).astype(
        jnp.bfloat16
    )
    qfull = jnp.concatenate([q_lat, q_rope], axis=-1)
    chosen = jnp.any(
        sel[:, :, None] == jnp.arange(slot_total, dtype=jnp.int32)[None, None, :], axis=1
    )
    live = jnp.repeat(chosen, BLOCK_LEN, axis=1)[:, None, :]
    score = jnp.einsum("qhc,tc->qht", qfull, keys, preferred_element_type=jnp.float32) * scale
    score = jnp.where(live, score, -jnp.inf)
    prob = jax.nn.softmax(score, axis=-1)
    prob_low = prob.astype(jnp.bfloat16)
    olat = jnp.einsum("qht,tl->qhl", prob_low, keys_lat, preferred_element_type=jnp.float32).astype(
        jnp.bfloat16
    )
    attn_out = jnp.einsum(
        "qhl,hlv->qhv", olat, weight_v, preferred_element_type=jnp.float32
    ).astype(jnp.bfloat16)
    d_olat = jnp.einsum("qhv,hlv->qhl", d_out, weight_v, preferred_element_type=jnp.float32).astype(
        jnp.bfloat16
    )
    dprob = jnp.einsum("qhl,tl->qht", d_olat, keys_lat, preferred_element_type=jnp.float32)
    delta = jnp.sum(prob * dprob, axis=-1, keepdims=True)
    dscore = (prob * (dprob - delta) * scale).astype(jnp.bfloat16)
    dquery = jnp.einsum("qht,tc->qhc", dscore, keys, preferred_element_type=jnp.float32)
    d_q_rope = dquery[:, :, latent:].astype(jnp.bfloat16)
    d_qlat = dquery[:, :, :latent].astype(jnp.bfloat16)
    d_q_nope = jnp.einsum(
        "qhl,hnl->qhn", d_qlat, weight_k, preferred_element_type=jnp.float32
    ).astype(jnp.bfloat16)
    value_part = jnp.einsum("qht,qhl->tl", prob_low, d_olat, preferred_element_type=jnp.float32)
    dkeys = jnp.einsum("qht,qhc->tc", dscore, qfull, preferred_element_type=jnp.float32)
    dkeys = dkeys + jnp.pad(value_part, ((0, 0), (0, rope)))
    one_hot = (
        asked.reshape(-1)[:, None] == jnp.arange(own_blocks, dtype=jnp.int32)[None, :]
    ).astype(jnp.float32)
    returned = lax.all_to_all(
        dkeys.reshape(peers, per_peer, BLOCK_LEN * width).astype(jnp.bfloat16),
        "seq",
        split_axis=0,
        concat_axis=0,
        tiled=True,
    ).astype(jnp.float32)
    local_grad = jnp.dot(
        one_hot.T,
        returned.reshape(peers * per_peer, BLOCK_LEN * width),
        precision=lax.Precision.HIGHEST,
    )
    d_cache = (
        lax.psum(local_grad.astype(jnp.bfloat16), "grp")
        .astype(jnp.float32)
        .reshape(own_blocks * BLOCK_LEN, width)
    )
    return (attn_out, d_q_nope, d_q_rope, d_cache)


def solution(mesh):
    return jax.shard_map(
        local,
        mesh=mesh,
        in_specs=(
            P("seq", "grp", None),
            P("seq", "grp", None),
            P("seq", None),
            P("grp", "seq"),
            P("grp", "seq"),
            P("seq", "grp", None),
            P("seq", None),
            P("seq", None),
        ),
        out_specs=(
            P("seq", "grp", None),
            P("seq", "grp", None),
            P("seq", "grp", None),
            P("seq", None),
        ),
        check_vma=False,
    )
```

```python
import functools
import math

import jax
import jax.numpy as jnp
from jax import lax
from jax.experimental import pallas as pl
from jax.experimental.pallas import tpu as pltpu
from jax.sharding import PartitionSpec as P

BLOCK_LEN = 64
LANES = 128
HIDDEN = -1e30
VMEM = pl.BlockSpec(memory_space=pltpu.VMEM)
SMEM = pl.BlockSpec(memory_space=pltpu.SMEM)
ANY = pl.BlockSpec(memory_space=pl.ANY)
F32 = jnp.float32
BF16 = jnp.bfloat16


def call(kernel, name, args, specs, outs, scratch=(), mib=16, tied=None):
    out_shape = [jax.ShapeDtypeStruct(s, d) for s, d in outs]
    out_specs = [VMEM] * len(outs)
    aliases = {}
    body = kernel
    if tied is not None:
        args, specs = (tied, *args), [ANY] + specs
        out_shape, out_specs = [jax.ShapeDtypeStruct(tied.shape, tied.dtype)] + out_shape, [ANY] + out_specs
        aliases = {0: 0}
        n_in = len(args)

        def body(*refs):
            kernel(*refs[1:n_in], *refs[n_in + 1 :])

    return pl.pallas_call(
        body,
        out_shape=out_shape,
        in_specs=specs,
        out_specs=out_specs,
        scratch_shapes=list(scratch),
        input_output_aliases=aliases,
        compiler_params=pltpu.CompilerParams(vmem_limit_bytes=mib * 2**20),
        name=name,
    )(*args)


def nt(a, b):
    return lax.dot_general(a, b, (((1,), (1,)), ((), ())), preferred_element_type=F32)


def nn(a, b):
    return lax.dot_general(a, b, (((1,), (0,)), ((), ())), preferred_element_type=F32)


def swap(x, axis, bit):
    n = lax.axis_size(axis)
    return lax.ppermute(x, axis, [(i, i ^ bit) for i in range(n)])


def seq_swap(x):
    return lax.all_to_all(x, "seq", split_axis=0, concat_axis=0, tiled=True)


def tie_kernel(*refs):
    pass


def cut_kernel(ids, cache, out):
    depth = out.shape[0]
    out[...] = cache[pl.ds(pl.multiple_of(ids[1] * depth, 16), depth), :]


def gather_kernel(per_peer, ids, own, other, *refs):
    owners = len(refs) - 2
    caches, outs = refs[:owners], refs[owners:]
    lanes = per_peer * BLOCK_LEN

    def block(row, i, j):
        b = row[0, (ids[0] ^ (2 * i)) * per_peer + j]
        tile = caches[i][:, pl.ds(pl.multiple_of((b >> 1) * LANES, LANES), LANES)]
        return jnp.where((b & 1) == 1, tile[:, BLOCK_LEN:], tile[:, :BLOCK_LEN])

    for row, out in zip((other, own), outs):
        for i in range(owners):
            for j in range(0, per_peer, 2):
                both = jnp.concatenate([block(row, i, j), block(row, i, j + 1)], axis=1)
                at = i * lanes + j * BLOCK_LEN
                out[:, at : at + 2 * BLOCK_LEN] = both


def scatter_kernel(per_peer, pieces, ids, rows, *refs):
    got, out, acc = refs[:-2], refs[-2], refs[-1]
    me = ids[0]
    depth = out.shape[0]
    acc[...] = jnp.zeros_like(acc)
    blank = jnp.zeros((depth, BLOCK_LEN), F32)
    for k, (ref, place) in enumerate(pieces):
        for j in range(per_peer):
            b = rows[k, me * per_peer + j]
            at = pl.ds(pl.multiple_of((b >> 1) * LANES, LANES), LANES)
            start = (place * per_peer + j) * BLOCK_LEN
            g = got[ref][:, start : start + BLOCK_LEN].astype(F32)
            low = jnp.concatenate([g, blank], axis=1)
            high = jnp.concatenate([blank, g], axis=1)
            acc[:, at] = acc[:, at] + jnp.where((b & 1) == 1, high, low)
    out[...] = acc[...].astype(BF16)


def assemble_kernel(ids, *refs):
    parts, out = refs[:-1], refs[-1]
    depth = parts[0].shape[0]
    for k, y in enumerate(parts):
        out[pl.ds(pl.multiple_of((ids[1] ^ k) * depth, 16), depth), :] = y[...].astype(F32)


def weight_k_of(pack, head, uk_rows, tiles):
    rows = uk_rows // tiles
    peers = pack.shape[0]
    cols = []
    for t in range(tiles):
        cols.append(
            jnp.concatenate(
                [pack[r, head, t * rows : (t + 1) * rows, :] for r in range(peers)], axis=0
            )
        )
    return jnp.concatenate(cols, axis=1)


def stacked(pack, head, start, rows):
    peers = pack.shape[0]
    return jnp.concatenate([pack[r, head, start : start + rows, :] for r in range(peers)], axis=0)


def expand_kernel(sizes, pack, asked, out):
    uk_rows, uv_rows, queries, tiles, latent = sizes
    peers, heads = pack.shape[0], pack.shape[1]
    for h in range(heads):
        wk = weight_k_of(pack, h, uk_rows, tiles)
        wv = stacked(pack, h, uk_rows, uv_rows)
        qn = stacked(pack, h, uk_rows + uv_rows, queries)
        do = stacked(pack, h, uk_rows + uv_rows + queries, queries)
        q_lat = nn(qn, wk).astype(BF16)
        d_olat = nt(do, wv).astype(BF16)
        for r in range(peers):
            out[r, h, :, :latent] = q_lat[r * queries : (r + 1) * queries]
            out[r, h, :, latent:] = d_olat[r * queries : (r + 1) * queries]


def reduce_kernel(sizes, pack, lat, out):
    uk_rows, uv_rows, queries, tiles, latent = sizes
    peers, heads = pack.shape[0], pack.shape[1]
    for h in range(heads):
        wk = weight_k_of(pack, h, uk_rows, tiles)
        wv = stacked(pack, h, uk_rows, uv_rows)
        both = jnp.concatenate([lat[r, h] for r in range(peers)], axis=0)
        attn = nn(both[:, :latent], wv).astype(BF16)
        dqn = nt(both[:, latent:], wk).astype(BF16)
        for r in range(peers):
            out[r, h, :, : attn.shape[1]] = attn[r * queries : (r + 1) * queries]
            out[r, h, :, attn.shape[1] :] = dqn[r * queries : (r + 1) * queries]


def tokens_grad(grads, scale, do, cat, delta, kt, p, width):
    keep, send, at, depth = grads
    latent = do.shape[1]
    dp = nn(do[...], kt[:latent])
    ds = (p.astype(F32) * (dp - delta) * scale).astype(BF16)
    part = nt(ds, kt[:width])
    dk = nn(cat[...], jnp.concatenate([ds, p], axis=0)).astype(BF16)
    for k, ref in enumerate((keep, send, keep, send)):
        ref[k // 2, :, at] = dk[k * depth : (k + 1) * depth]
    return part


def attend_kernel(scale, per_peer, ids, sel, rope, qd, *refs):
    keys, refs = (refs[:4], refs[4:8]), refs[8:]
    keeps, sends, lat, d_rope, refs = (refs[0], refs[2]), (refs[1], refs[3]), refs[4], refs[5], refs[6:]
    kt_near, kt_far, pb_near, pb_far, qx, do, sc, flip, cat, o_full, dq = refs
    rows, latent = do.shape
    heads, queries, rope_dim = rope.shape
    width = latent + rope_dim
    slots = qx.shape[1] - width
    depth, half = keys[0][0].shape
    held = 4
    lanes = half // held
    kts, pbs = (kt_near, kt_far), (pb_near, pb_far)

    picks = sel[...] ^ (ids[0] * per_peer)
    slot = lax.broadcasted_iota(jnp.int32, (queries, slots), 1)
    chosen = picks[:, 0:1] == slot
    for j in range(1, picks.shape[1]):
        chosen = chosen | (picks[:, j : j + 1] == slot)
    bias = jnp.where(chosen, 0.0, HIDDEN).astype(BF16)
    bias = jnp.broadcast_to(bias[None], (heads, queries, slots)).reshape(rows, slots)
    qx[:, :latent] = qd[:, :latent]
    qx[:, latent:] = jnp.concatenate([rope[...].reshape(rows, rope_dim), bias], axis=1)
    do[...] = qd[:, latent:]
    for c in range(2):
        for k in range(4):
            at = pl.ds(pl.multiple_of((ids[1] ^ k) * depth, 16), depth)
            for i in range(held):
                peer = c * held + i
                src = keys[peer % 2][k][:, (peer // 2) * lanes : (peer // 2 + 1) * lanes]
                kts[c][at, i * lanes : (i + 1) * lanes] = src
        place = lax.broadcasted_iota(jnp.int32, (slots, half), 0)
        token = lax.broadcasted_iota(jnp.int32, (slots, half), 1) + c * half
        kts[c][width:, :] = jnp.where(token // BLOCK_LEN == place, 1.0, 0.0).astype(BF16)

    scale2 = scale * math.log2(math.e)
    step = 512
    chunks = [(c, i) for c in range(2) for i in range(0, half, step)]
    top = jnp.full((rows, 1), -jnp.inf, F32)
    total = jnp.zeros((rows, 1), F32)
    tops = []
    for n, (c, i) in enumerate(chunks):
        s = nn(qx[...], kts[c][:, i : i + step]) * scale2
        high = jnp.maximum(top, jnp.max(s, axis=1, keepdims=True))
        e = jnp.exp2(s - high)
        sc[:, n * step : (n + 1) * step] = e
        total = total * jnp.exp2(top - high) + jnp.sum(e, axis=1, keepdims=True)
        top = high
        tops.append(high)
    inv = 1.0 / total
    for n, (c, i) in enumerate(chunks):
        pb = (sc[:, n * step : (n + 1) * step] * (jnp.exp2(tops[n] - top) * inv)).astype(BF16)
        pbs[c][:, i : i + step] = pb
        part = nt(pb, kts[c][:latent, i : i + step])
        if n == 0:
            o_full[...] = part
        else:
            o_full[...] += part
    lat[:, :latent] = o_full[...].astype(BF16)
    delta = jnp.sum(o_full[...] * do[...].astype(F32), axis=1, keepdims=True)

    flip[:, :rows] = qx[:, :width].T
    flip[:latent, rows:] = do[...].T
    flip[latent:, rows:] = jnp.zeros((rope_dim, rows), BF16)
    for k in range(4):
        at = pl.ds(pl.multiple_of((ids[1] ^ k) * depth, 16), depth)
        cat[k * depth : (k + 1) * depth] = flip[at, :]
    for n, (c, i) in enumerate([(c, i) for c in (1, 0) for i in range(0, half, step)]):
        at = slice(i, i + step)
        grads = (keeps[c], sends[c], at, depth)
        kt = kts[c].at[:, at]
        part = tokens_grad(grads, scale, do, cat, delta, kt, pbs[c][:, at], width)
        if n == 0:
            dq[...] = part
        else:
            dq[...] += part
    lat[:, latent:] = dq[:, :latent].astype(BF16)
    d_rope[...] = dq[:, latent:].astype(BF16)


def pair_kernel(keep, got, a0, *a2):
    total = keep[...].astype(F32) + got[...].astype(F32)
    a0[...] = total[0].astype(BF16)
    lanes = a2[0].shape[1]
    for i, a in enumerate(a2):
        a[...] = total[1, :, i * lanes : (i + 1) * lanes].astype(BF16)


def owner_kernel(order, a0, got, *outs):
    total = (a0[...].astype(F32) + got[...].astype(F32)).astype(BF16)
    for places, out in zip(order, outs):
        lanes = out.shape[1] // len(places)
        for i, p in enumerate(places):
            out[:, i * lanes : (i + 1) * lanes] = total[:, p * lanes : (p + 1) * lanes]


def local(q_nope, q_rope, cache, w_uk, w_uv, d_out, sel, slot_blocks):
    peers = lax.axis_size("seq")
    groups = lax.axis_size("grp")
    queries, heads, nope = q_nope.shape
    rope = q_rope.shape[2]
    width = cache.shape[1]
    latent = width - rope
    value = d_out.shape[2]
    slots = slot_blocks.shape[1]
    per_peer = slots // peers
    if not (peers == 8 and groups == 4 and heads % peers == 0 and per_peer % 2 == 0):
        return local_general(q_nope, q_rope, cache, w_uk, w_uv, d_out, sel, slot_blocks)
    ids = jnp.stack([lax.axis_index("seq"), lax.axis_index("grp")]).astype(jnp.int32)
    tokens = cache.shape[0]
    depth = width // groups
    lanes = per_peer * BLOCK_LEN
    held = peers // 2
    half = held * lanes
    share = heads // peers
    rows = heads * queries
    scale = 1.0 / math.sqrt(nope + rope)

    row1 = swap(slot_blocks, "seq", 1)
    (c0,) = call(cut_kernel, "cut", (ids, cache.T), [SMEM, VMEM], [((depth, tokens), BF16)])
    c2 = swap(c0, "seq", 4)
    c1 = swap(c0, "seq", 2)
    asked_y = jnp.concatenate([slot_blocks, row1], axis=0)

    c3 = swap(c2, "seq", 2)
    away, k0 = call(
        functools.partial(gather_kernel, per_peer),
        "gather",
        (ids, slot_blocks, row1, c0, c1, c2, c3),
        [SMEM] * 3 + [VMEM] * 4,
        [((depth, half), BF16)] * 2,
    )
    n_rows = w_uk.shape[1] // latent
    l_rows = w_uv.shape[1] // value
    tiles = latent // LANES
    uk = w_uk.reshape(heads, n_rows, tiles, LANES).transpose(0, 2, 1, 3)
    pack = jnp.concatenate(
        [
            uk.reshape(heads, n_rows * tiles, LANES),
            w_uv.reshape(heads, l_rows, value),
            q_nope.transpose(1, 0, 2),
            d_out.transpose(1, 0, 2),
        ],
        axis=1,
    )
    (pack,) = call(tie_kernel, "after", (away,), [ANY], [], tied=pack)
    (asked_y,) = call(tie_kernel, "after", (away,), [ANY], [], tied=asked_y)
    asked = jnp.concatenate([asked_y] + [swap(asked_y, "seq", bit) for bit in (2, 4, 6)], axis=0)
    pack = seq_swap(pack).reshape(peers, share, -1, LANES)
    sizes = (n_rows * tiles, l_rows, queries, tiles, latent)
    (lat,) = call(
        functools.partial(expand_kernel, sizes),
        "expand",
        (pack, asked),
        [VMEM, ANY],
        [((peers, share, queries, 2 * latent), BF16)],
    )
    qd = seq_swap(lat).reshape(rows, 2 * latent)

    keys = []
    for k in (k0, swap(away, "seq", 1)):
        k2 = swap(k, "grp", 2)
        keys += [k, swap(k, "grp", 1), k2, swap(k2, "grp", 1)]
    rope_rows = q_rope.transpose(1, 0, 2)
    near_keep, near_send, far_keep, far_send, lat, d_rope = call(
        functools.partial(attend_kernel, scale, per_peer),
        "attend",
        (ids, sel, rope_rows, qd, *keys),
        [SMEM] + [VMEM] * 11,
        [((2, depth, half), BF16)] * 4 + [((rows, 2 * latent), BF16), ((rows, rope), BF16)],
        [pltpu.VMEM((width + slots, half), BF16)] * 2
        + [pltpu.VMEM((rows, half), BF16)] * 2
        + [
            pltpu.VMEM((rows, width + slots), BF16),
            pltpu.VMEM((rows, latent), BF16),
            pltpu.VMEM((rows, 2 * half), F32),
            pltpu.VMEM((width, 2 * rows), BF16),
            pltpu.VMEM((width, 2 * rows), BF16),
            pltpu.VMEM((rows, latent), F32),
            pltpu.VMEM((rows, width), F32),
        ],
        60,
    )

    def pair(keep, send, tied=None):
        outs = [((depth, half), BF16)] * 2
        return call(pair_kernel, "pair", (keep, swap(send, "grp", 1)), [VMEM] * 2, outs, tied=tied)


    def owner(a0, a2, order):
        outs = [((depth, lanes * len(places)), BF16) for places in order]
        kernel = functools.partial(owner_kernel, order)
        return call(kernel, "owner", (a0, swap(a2, "grp", 2)), [VMEM] * 2, outs)

    far = pair(far_keep, far_send)
    first, *near = pair(near_keep, near_send, tied=far[0])
    far = owner(first, far[1], [(0,), (1,), (2,), (3,)])
    lat = seq_swap(lat.reshape(peers, share, queries, 2 * latent))
    (res,) = call(
        functools.partial(reduce_kernel, sizes),
        "reduce",
        (pack, lat),
        [VMEM] * 2,
        [((peers, share, queries, value + nope), BF16)],
    )
    own, over_y, over_z = owner(*near, [(0,), (1, 3), (2,)])
    from_y = swap(over_y, "seq", 1)
    over_z = jnp.concatenate([over_z, from_y[:, lanes:]], axis=1)
    (over_z,) = call(tie_kernel, "after", (res,), [ANY], [], tied=over_z)
    from_z = swap(over_z, "seq", 2)
    got = [own, from_y, from_z] + [swap(p, "seq", 4 + i) for i, p in enumerate(far)]
    res = seq_swap(res).reshape(heads, queries, value + nope)

    (y0,) = call(
        functools.partial(
            scatter_kernel,
            per_peer,
            [(0, 0), (1, 0), (2, 0), (2, 1), (3, 0), (4, 0), (5, 0), (6, 0)],
        ),
        "scatter",
        (ids, asked, *got),
        [SMEM, SMEM] + [VMEM] * len(got),
        [((depth, tokens), BF16)],
        [pltpu.VMEM((depth, tokens), F32)],
    )
    y2 = swap(y0, "grp", 2)
    y1 = swap(y0, "grp", 1)
    y3 = swap(y2, "grp", 1)
    (d_cache,) = call(
        assemble_kernel,
        "assemble",
        (ids, y0, y1, y2, y3),
        [SMEM] + [VMEM] * 4,
        [((width, tokens), F32)],
    )
    return (
        res[:, :, :value].transpose(1, 0, 2),
        res[:, :, value:].transpose(1, 0, 2),
        d_rope.reshape(heads, queries, rope).transpose(1, 0, 2),
        d_cache.T,
    )


def local_general(q_nope, q_rope, cache, w_uk, w_uv, d_out, sel, slot_blocks):
    peers = lax.axis_size("seq")
    queries, heads, nope = q_nope.shape
    rope = q_rope.shape[2]
    width = cache.shape[1]
    latent = width - rope
    value = d_out.shape[2]
    slot_total = slot_blocks.shape[1]
    per_peer = slot_total // peers
    own_blocks = cache.shape[0] // BLOCK_LEN
    scale = 1.0 / math.sqrt(nope + rope)
    gathered_k, gathered_v = (
        lax.all_gather(w_uk, "seq", axis=1, tiled=True),
        lax.all_gather(w_uv, "seq", axis=1, tiled=True),
    )
    weight_k = gathered_k.reshape(heads, nope, latent)
    weight_v = gathered_v.reshape(heads, latent, value)
    wanted = slot_blocks.reshape(peers, per_peer)
    asked = lax.all_to_all(wanted, "seq", split_axis=0, concat_axis=0, tiled=True)
    blocks = cache.reshape(own_blocks, BLOCK_LEN, width)
    arrived = lax.all_to_all(blocks[asked], "seq", split_axis=0, concat_axis=0, tiled=True)
    keys = arrived.reshape(slot_total * BLOCK_LEN, width)
    keys_lat = keys[:, :latent]
    q_lat = jnp.einsum("qhn,hnl->qhl", q_nope, weight_k, preferred_element_type=jnp.float32).astype(
        jnp.bfloat16
    )
    qfull = jnp.concatenate([q_lat, q_rope], axis=-1)
    chosen = jnp.any(
        sel[:, :, None] == jnp.arange(slot_total, dtype=jnp.int32)[None, None, :], axis=1
    )
    live = jnp.repeat(chosen, BLOCK_LEN, axis=1)[:, None, :]
    score = jnp.einsum("qhc,tc->qht", qfull, keys, preferred_element_type=jnp.float32) * scale
    score = jnp.where(live, score, -jnp.inf)
    prob = jax.nn.softmax(score, axis=-1)
    prob_low = prob.astype(jnp.bfloat16)
    olat = jnp.einsum("qht,tl->qhl", prob_low, keys_lat, preferred_element_type=jnp.float32).astype(
        jnp.bfloat16
    )
    attn_out = jnp.einsum(
        "qhl,hlv->qhv", olat, weight_v, preferred_element_type=jnp.float32
    ).astype(jnp.bfloat16)
    d_olat = jnp.einsum("qhv,hlv->qhl", d_out, weight_v, preferred_element_type=jnp.float32).astype(
        jnp.bfloat16
    )
    dprob = jnp.einsum("qhl,tl->qht", d_olat, keys_lat, preferred_element_type=jnp.float32)
    delta = jnp.sum(prob * dprob, axis=-1, keepdims=True)
    dscore = (prob * (dprob - delta) * scale).astype(jnp.bfloat16)
    dquery = jnp.einsum("qht,tc->qhc", dscore, keys, preferred_element_type=jnp.float32)
    d_q_rope = dquery[:, :, latent:].astype(jnp.bfloat16)
    d_qlat = dquery[:, :, :latent].astype(jnp.bfloat16)
    d_q_nope = jnp.einsum(
        "qhl,hnl->qhn", d_qlat, weight_k, preferred_element_type=jnp.float32
    ).astype(jnp.bfloat16)
    value_part = jnp.einsum("qht,qhl->tl", prob_low, d_olat, preferred_element_type=jnp.float32)
    dkeys = jnp.einsum("qht,qhc->tc", dscore, qfull, preferred_element_type=jnp.float32)
    dkeys = dkeys + jnp.pad(value_part, ((0, 0), (0, rope)))
    one_hot = (
        asked.reshape(-1)[:, None] == jnp.arange(own_blocks, dtype=jnp.int32)[None, :]
    ).astype(jnp.float32)
    returned = lax.all_to_all(
        dkeys.reshape(peers, per_peer, BLOCK_LEN * width).astype(jnp.bfloat16),
        "seq",
        split_axis=0,
        concat_axis=0,
        tiled=True,
    ).astype(jnp.float32)
    local_grad = jnp.dot(
        one_hot.T,
        returned.reshape(peers * per_peer, BLOCK_LEN * width),
        precision=lax.Precision.HIGHEST,
    )
    d_cache = (
        lax.psum(local_grad.astype(jnp.bfloat16), "grp")
        .astype(jnp.float32)
        .reshape(own_blocks * BLOCK_LEN, width)
    )
    return (attn_out, d_q_nope, d_q_rope, d_cache)


def solution(mesh):
    return jax.shard_map(
        local,
        mesh=mesh,
        in_specs=(
            P("seq", "grp", None),
            P("seq", "grp", None),
            P("seq", None),
            P("grp", "seq"),
            P("grp", "seq"),
            P("seq", "grp", None),
            P("seq", None),
            P("seq", None),
        ),
        out_specs=(
            P("seq", "grp", None),
            P("seq", "grp", None),
            P("seq", "grp", None),
            P("seq", None),
        ),
        check_vma=False,
    )
```

```python
import functools
import math

import jax
import jax.numpy as jnp
from jax import lax
from jax.experimental import pallas as pl
from jax.experimental.pallas import tpu as pltpu
from jax.sharding import PartitionSpec as P

BLOCK_LEN = 64
LANES = 128
HIDDEN = -1e30
VMEM = pl.BlockSpec(memory_space=pltpu.VMEM)
SMEM = pl.BlockSpec(memory_space=pltpu.SMEM)
ANY = pl.BlockSpec(memory_space=pl.ANY)
F32 = jnp.float32
BF16 = jnp.bfloat16


def call(kernel, name, args, specs, outs, scratch=(), mib=32, tied=None):
    out_shape = [jax.ShapeDtypeStruct(s, d) for s, d in outs]
    out_specs = [VMEM] * len(outs)
    aliases = {}
    body = kernel
    if tied is not None:
        args, specs = (tied, *args), [ANY] + specs
        out_shape, out_specs = [jax.ShapeDtypeStruct(tied.shape, tied.dtype)] + out_shape, [ANY] + out_specs
        aliases = {0: 0}
        n_in = len(args)

        def body(*refs):
            kernel(*refs[1:n_in], *refs[n_in + 1 :])

    return pl.pallas_call(
        body,
        out_shape=out_shape,
        in_specs=specs,
        out_specs=out_specs,
        scratch_shapes=list(scratch),
        input_output_aliases=aliases,
        compiler_params=pltpu.CompilerParams(vmem_limit_bytes=mib * 2**20),
        name=name,
    )(*args)


def nt(a, b):
    return lax.dot_general(a, b, (((1,), (1,)), ((), ())), preferred_element_type=F32)


def nn(a, b):
    return lax.dot_general(a, b, (((1,), (0,)), ((), ())), preferred_element_type=F32)


def swap(x, axis, bit):
    n = lax.axis_size(axis)
    return lax.ppermute(x, axis, [(i, i ^ bit) for i in range(n)])


def seq_swap(x):
    return lax.all_to_all(x, "seq", split_axis=0, concat_axis=0, tiled=True)


def tie_kernel(*refs):
    pass


def cut_kernel(ids, cache, out):
    depth = out.shape[0]
    out[...] = cache[pl.ds(pl.multiple_of(ids[1] * depth, 16), depth), :]


def gather_kernel(per_peer, ids, own, other, *refs):
    owners = len(refs) - 2
    caches, outs = refs[:owners], refs[owners:]
    lanes = per_peer * BLOCK_LEN

    def block(row, i, j):
        b = row[0, (ids[0] ^ (2 * i)) * per_peer + j]
        tile = caches[i][:, pl.ds(pl.multiple_of((b >> 1) * LANES, LANES), LANES)]
        return jnp.where((b & 1) == 1, tile[:, BLOCK_LEN:], tile[:, :BLOCK_LEN])

    for row, out in zip((other, own), outs):
        for i in range(owners):
            for j in range(0, per_peer, 2):
                both = jnp.concatenate([block(row, i, j), block(row, i, j + 1)], axis=1)
                at = i * lanes + j * BLOCK_LEN
                out[:, at : at + 2 * BLOCK_LEN] = both


def scatter_kernel(per_peer, pieces, ids, rows, *refs):
    got, out, acc = refs[:-2], refs[-2], refs[-1]
    me = ids[0]
    depth = out.shape[0]
    acc[...] = jnp.zeros_like(acc)
    blank = jnp.zeros((depth, BLOCK_LEN), F32)
    for k, (ref, place) in enumerate(pieces):
        for j in range(per_peer):
            b = rows[k, me * per_peer + j]
            at = pl.ds(pl.multiple_of((b >> 1) * LANES, LANES), LANES)
            start = (place * per_peer + j) * BLOCK_LEN
            g = got[ref][:, start : start + BLOCK_LEN].astype(F32)
            low = jnp.concatenate([g, blank], axis=1)
            high = jnp.concatenate([blank, g], axis=1)
            acc[:, at] = acc[:, at] + jnp.where((b & 1) == 1, high, low)
    out[...] = acc[...].astype(BF16)


def assemble_kernel(ids, *refs):
    parts, out = refs[:-1], refs[-1]
    depth = parts[0].shape[0]
    for k, y in enumerate(parts):
        out[pl.ds(pl.multiple_of((ids[1] ^ k) * depth, 16), depth), :] = y[...].astype(F32)


def weight_k_of(pack, head, uk_rows, tiles):
    rows = uk_rows // tiles
    peers = pack.shape[0]
    cols = []
    for t in range(tiles):
        cols.append(
            jnp.concatenate(
                [pack[r, head, t * rows : (t + 1) * rows, :] for r in range(peers)], axis=0
            )
        )
    return jnp.concatenate(cols, axis=1)


def stacked(pack, head, start, rows):
    peers = pack.shape[0]
    return jnp.concatenate([pack[r, head, start : start + rows, :] for r in range(peers)], axis=0)


def expand_kernel(sizes, pack, away, over_x, out):
    uk_rows, uv_rows, queries, tiles, latent = sizes
    peers, heads = pack.shape[0], pack.shape[1]
    for h in range(heads):
        wk = weight_k_of(pack, h, uk_rows, tiles)
        wv = stacked(pack, h, uk_rows, uv_rows)
        qn = stacked(pack, h, uk_rows + uv_rows, queries)
        do = stacked(pack, h, uk_rows + uv_rows + queries, queries)
        q_lat = nn(qn, wk).astype(BF16)
        d_olat = nt(do, wv).astype(BF16)
        for r in range(peers):
            out[r, h, :, :latent] = q_lat[r * queries : (r + 1) * queries]
            out[r, h, :, latent:] = d_olat[r * queries : (r + 1) * queries]


def reduce_kernel(sizes, pack, lat, out):
    uk_rows, uv_rows, queries, tiles, latent = sizes
    peers, heads = pack.shape[0], pack.shape[1]
    for h in range(heads):
        wk = weight_k_of(pack, h, uk_rows, tiles)
        wv = stacked(pack, h, uk_rows, uv_rows)
        both = jnp.concatenate([lat[r, h] for r in range(peers)], axis=0)
        attn = nn(both[:, :latent], wv).astype(BF16)
        dqn = nt(both[:, latent:], wk).astype(BF16)
        for r in range(peers):
            out[r, h, :, : attn.shape[1]] = attn[r * queries : (r + 1) * queries]
            out[r, h, :, attn.shape[1] :] = dqn[r * queries : (r + 1) * queries]


def tokens_grad(grads, scale, do, cat, delta, kt, p, width):
    keep, send, at, depth = grads
    latent = do.shape[1]
    dp = nn(do[...], kt[:latent])
    ds = (p.astype(F32) * (dp - delta) * scale).astype(BF16)
    part = nt(ds, kt[:width])
    dk = nn(cat[...], jnp.concatenate([ds, p], axis=0)).astype(BF16)
    for k, ref in enumerate((keep, send, keep, send)):
        ref[k // 2, :, at] = dk[k * depth : (k + 1) * depth]
    return part


def attend_kernel(scale, per_peer, ids, sel, rope, qd, *refs):
    keys, refs = (refs[:4], refs[4:8]), refs[8:]
    keeps, sends, lat, d_rope, refs = (refs[0], refs[2]), (refs[1], refs[3]), refs[4], refs[5], refs[6:]
    kt_near, kt_far, pb_near, pb_far, qx, do, sc, flip, cat, o_full, dq = refs
    rows, latent = do.shape
    heads, queries, rope_dim = rope.shape
    width = latent + rope_dim
    slots = qx.shape[1] - width
    depth, half = keys[0][0].shape
    held = 4
    lanes = half // held
    kts, pbs = (kt_near, kt_far), (pb_near, pb_far)

    picks = sel[...] ^ (ids[0] * per_peer)
    slot = lax.broadcasted_iota(jnp.int32, (queries, slots), 1)
    chosen = picks[:, 0:1] == slot
    for j in range(1, picks.shape[1]):
        chosen = chosen | (picks[:, j : j + 1] == slot)
    bias = jnp.where(chosen, 0.0, HIDDEN).astype(BF16)
    bias = jnp.broadcast_to(bias[None], (heads, queries, slots)).reshape(rows, slots)
    qx[:, :latent] = qd[:, :latent]
    qx[:, latent:] = jnp.concatenate([rope[...].reshape(rows, rope_dim), bias], axis=1)
    do[...] = qd[:, latent:]
    for c in range(2):
        for k in range(4):
            at = pl.ds(pl.multiple_of((ids[1] ^ k) * depth, 16), depth)
            for i in range(held):
                peer = c * held + i
                src = keys[peer % 2][k][:, (peer // 2) * lanes : (peer // 2 + 1) * lanes]
                kts[c][at, i * lanes : (i + 1) * lanes] = src
        place = lax.broadcasted_iota(jnp.int32, (slots, half), 0)
        token = lax.broadcasted_iota(jnp.int32, (slots, half), 1) + c * half
        kts[c][width:, :] = jnp.where(token // BLOCK_LEN == place, 1.0, 0.0).astype(BF16)

    scale2 = scale * math.log2(math.e)
    step = 512
    chunks = [(c, i) for c in range(2) for i in range(0, half, step)]
    top = jnp.full((rows, 1), -jnp.inf, F32)
    total = jnp.zeros((rows, 1), F32)
    tops = []
    for n, (c, i) in enumerate(chunks):
        s = nn(qx[...], kts[c][:, i : i + step]) * scale2
        high = jnp.maximum(top, jnp.max(s, axis=1, keepdims=True))
        e = jnp.exp2(s - high)
        sc[:, n * step : (n + 1) * step] = e
        total = total * jnp.exp2(top - high) + jnp.sum(e, axis=1, keepdims=True)
        top = high
        tops.append(high)
    inv = 1.0 / total
    for n, (c, i) in enumerate(chunks):
        pb = (sc[:, n * step : (n + 1) * step] * (jnp.exp2(tops[n] - top) * inv)).astype(BF16)
        pbs[c][:, i : i + step] = pb
        part = nt(pb, kts[c][:latent, i : i + step])
        if n == 0:
            o_full[...] = part
        else:
            o_full[...] += part
    lat[:, :latent] = o_full[...].astype(BF16)
    delta = jnp.sum(o_full[...] * do[...].astype(F32), axis=1, keepdims=True)

    flip[:, :rows] = qx[:, :width].T
    flip[:latent, rows:] = do[...].T
    flip[latent:, rows:] = jnp.zeros((rope_dim, rows), BF16)
    for k in range(4):
        at = pl.ds(pl.multiple_of((ids[1] ^ k) * depth, 16), depth)
        cat[k * depth : (k + 1) * depth] = flip[at, :]
    for n, (c, i) in enumerate([(c, i) for c in (1, 0) for i in range(0, half, step)]):
        at = slice(i, i + step)
        grads = (keeps[c], sends[c], at, depth)
        kt = kts[c].at[:, at]
        part = tokens_grad(grads, scale, do, cat, delta, kt, pbs[c][:, at], width)
        if n == 0:
            dq[...] = part
        else:
            dq[...] += part
    lat[:, latent:] = dq[:, :latent].astype(BF16)
    d_rope[...] = dq[:, latent:].astype(BF16)


def pair_kernel(keep, got, a0, *a2):
    total = keep[...].astype(F32) + got[...].astype(F32)
    a0[...] = total[0].astype(BF16)
    lanes = a2[0].shape[1]
    for i, a in enumerate(a2):
        a[...] = total[1, :, i * lanes : (i + 1) * lanes].astype(BF16)


def owner_kernel(order, a0, got, *outs):
    total = (a0[...].astype(F32) + got[...].astype(F32)).astype(BF16)
    for places, out in zip(order, outs):
        lanes = out.shape[1] // len(places)
        for i, p in enumerate(places):
            out[:, i * lanes : (i + 1) * lanes] = total[:, p * lanes : (p + 1) * lanes]


def local(q_nope, q_rope, cache, w_uk, w_uv, d_out, sel, slot_blocks):
    peers = lax.axis_size("seq")
    groups = lax.axis_size("grp")
    queries, heads, nope = q_nope.shape
    rope = q_rope.shape[2]
    width = cache.shape[1]
    latent = width - rope
    value = d_out.shape[2]
    slots = slot_blocks.shape[1]
    per_peer = slots // peers
    if not (peers == 8 and groups == 4 and heads % peers == 0 and per_peer % 2 == 0):
        return local_general(q_nope, q_rope, cache, w_uk, w_uv, d_out, sel, slot_blocks)
    ids = jnp.stack([lax.axis_index("seq"), lax.axis_index("grp")]).astype(jnp.int32)
    tokens = cache.shape[0]
    depth = width // groups
    lanes = per_peer * BLOCK_LEN
    held = peers // 2
    half = held * lanes
    share = heads // peers
    rows = heads * queries
    scale = 1.0 / math.sqrt(nope + rope)

    row1 = swap(slot_blocks, "seq", 1)
    (c0,) = call(cut_kernel, "cut", (ids, cache.T), [SMEM, VMEM], [((depth, tokens), BF16)])
    c2 = swap(c0, "seq", 4)
    c1 = swap(c0, "seq", 2)
    asked_y = jnp.concatenate([slot_blocks, row1], axis=0)
    asked = jnp.concatenate([asked_y] + [swap(asked_y, "seq", bit) for bit in (2, 4, 6)], axis=0)

    c3 = swap(c2, "seq", 2)
    away, k0 = call(
        functools.partial(gather_kernel, per_peer),
        "gather",
        (ids, slot_blocks, row1, c0, c1, c2, c3),
        [SMEM] * 3 + [VMEM] * 4,
        [((depth, half), BF16)] * 2,
    )
    k_away, k0_x = swap(away, "seq", 1), swap(k0, "grp", 2)

    n_rows = w_uk.shape[1] // latent
    l_rows = w_uv.shape[1] // value
    tiles = latent // LANES
    uk = w_uk.reshape(heads, n_rows, tiles, LANES).transpose(0, 2, 1, 3)
    pack = jnp.concatenate(
        [
            uk.reshape(heads, n_rows * tiles, LANES),
            w_uv.reshape(heads, l_rows, value),
            q_nope.transpose(1, 0, 2),
            d_out.transpose(1, 0, 2),
        ],
        axis=1,
    )
    (pack,) = call(tie_kernel, "after", (c1, c3, asked), [ANY] * 3, [], tied=pack)
    pack = seq_swap(pack).reshape(peers, share, -1, LANES)
    sizes = (n_rows * tiles, l_rows, queries, tiles, latent)
    (lat,) = call(
        functools.partial(expand_kernel, sizes),
        "expand",
        (pack, k_away, k0_x),
        [VMEM, ANY, ANY],
        [((peers, share, queries, 2 * latent), BF16)],
    )
    qd = seq_swap(lat).reshape(rows, 2 * latent)

    keys = []
    for k, k2 in ((k0, k0_x), (k_away, swap(k_away, "grp", 2))):
        keys += [k, swap(k, "grp", 1), k2, swap(k2, "grp", 1)]
    rope_rows = q_rope.transpose(1, 0, 2)
    near_keep, near_send, far_keep, far_send, lat, d_rope = call(
        functools.partial(attend_kernel, scale, per_peer),
        "attend",
        (ids, sel, rope_rows, qd, *keys),
        [SMEM] + [VMEM] * 11,
        [((2, depth, half), BF16)] * 4 + [((rows, 2 * latent), BF16), ((rows, rope), BF16)],
        [pltpu.VMEM((width + slots, half), BF16)] * 2
        + [pltpu.VMEM((rows, half), BF16)] * 2
        + [
            pltpu.VMEM((rows, width + slots), BF16),
            pltpu.VMEM((rows, latent), BF16),
            pltpu.VMEM((rows, 2 * half), F32),
            pltpu.VMEM((width, 2 * rows), BF16),
            pltpu.VMEM((width, 2 * rows), BF16),
            pltpu.VMEM((rows, latent), F32),
            pltpu.VMEM((rows, width), F32),
        ],
        50,
    )

    def pair(keep, send, tied=None):
        outs = [((depth, half), BF16)] * 2
        return call(pair_kernel, "pair", (keep, swap(send, "grp", 1)), [VMEM] * 2, outs, tied=tied)


    def owner(a0, a2, order, tied=None):
        outs = [((depth, lanes * len(places)), BF16) for places in order]
        kernel = functools.partial(owner_kernel, order)
        return call(kernel, "owner", (a0, swap(a2, "grp", 2)), [VMEM] * 2, outs, tied=tied)

    far = pair(far_keep, far_send)
    first, *near = pair(near_keep, near_send, tied=far[0])
    held_a2, *far = owner(first, far[1], [(0,), (1,), (2,), (3,)], tied=near[1])
    lat = seq_swap(lat.reshape(peers, share, queries, 2 * latent))
    (res,) = call(
        functools.partial(reduce_kernel, sizes),
        "reduce",
        (pack, lat),
        [VMEM] * 2,
        [((peers, share, queries, value + nope), BF16)],
    )
    own, over_y, over_z = owner(near[0], held_a2, [(0,), (1, 3), (2,)])
    from_y = swap(over_y, "seq", 1)
    over_z = jnp.concatenate([over_z, from_y[:, lanes:]], axis=1)
    (over_z,) = call(tie_kernel, "after", (res,), [ANY], [], tied=over_z)
    from_z = swap(over_z, "seq", 2)
    got = [own, from_y, from_z] + [swap(p, "seq", 4 + i) for i, p in enumerate(far)]
    res = seq_swap(res).reshape(heads, queries, value + nope)

    (y0,) = call(
        functools.partial(
            scatter_kernel,
            per_peer,
            [(0, 0), (1, 0), (2, 0), (2, 1), (3, 0), (4, 0), (5, 0), (6, 0)],
        ),
        "scatter",
        (ids, asked, *got),
        [SMEM, SMEM] + [VMEM] * len(got),
        [((depth, tokens), BF16)],
        [pltpu.VMEM((depth, tokens), F32)],
    )
    y2 = swap(y0, "grp", 2)
    y1 = swap(y0, "grp", 1)
    y3 = swap(y2, "grp", 1)
    (d_cache,) = call(
        assemble_kernel,
        "assemble",
        (ids, y0, y1, y2, y3),
        [SMEM] + [VMEM] * 4,
        [((width, tokens), F32)],
    )
    return (
        res[:, :, :value].transpose(1, 0, 2),
        res[:, :, value:].transpose(1, 0, 2),
        d_rope.reshape(heads, queries, rope).transpose(1, 0, 2),
        d_cache.T,
    )


def local_general(q_nope, q_rope, cache, w_uk, w_uv, d_out, sel, slot_blocks):
    peers = lax.axis_size("seq")
    queries, heads, nope = q_nope.shape
    rope = q_rope.shape[2]
    width = cache.shape[1]
    latent = width - rope
    value = d_out.shape[2]
    slot_total = slot_blocks.shape[1]
    per_peer = slot_total // peers
    own_blocks = cache.shape[0] // BLOCK_LEN
    scale = 1.0 / math.sqrt(nope + rope)
    gathered_k, gathered_v = (
        lax.all_gather(w_uk, "seq", axis=1, tiled=True),
        lax.all_gather(w_uv, "seq", axis=1, tiled=True),
    )
    weight_k = gathered_k.reshape(heads, nope, latent)
    weight_v = gathered_v.reshape(heads, latent, value)
    wanted = slot_blocks.reshape(peers, per_peer)
    asked = lax.all_to_all(wanted, "seq", split_axis=0, concat_axis=0, tiled=True)
    blocks = cache.reshape(own_blocks, BLOCK_LEN, width)
    arrived = lax.all_to_all(blocks[asked], "seq", split_axis=0, concat_axis=0, tiled=True)
    keys = arrived.reshape(slot_total * BLOCK_LEN, width)
    keys_lat = keys[:, :latent]
    q_lat = jnp.einsum("qhn,hnl->qhl", q_nope, weight_k, preferred_element_type=jnp.float32).astype(
        jnp.bfloat16
    )
    qfull = jnp.concatenate([q_lat, q_rope], axis=-1)
    chosen = jnp.any(
        sel[:, :, None] == jnp.arange(slot_total, dtype=jnp.int32)[None, None, :], axis=1
    )
    live = jnp.repeat(chosen, BLOCK_LEN, axis=1)[:, None, :]
    score = jnp.einsum("qhc,tc->qht", qfull, keys, preferred_element_type=jnp.float32) * scale
    score = jnp.where(live, score, -jnp.inf)
    prob = jax.nn.softmax(score, axis=-1)
    prob_low = prob.astype(jnp.bfloat16)
    olat = jnp.einsum("qht,tl->qhl", prob_low, keys_lat, preferred_element_type=jnp.float32).astype(
        jnp.bfloat16
    )
    attn_out = jnp.einsum(
        "qhl,hlv->qhv", olat, weight_v, preferred_element_type=jnp.float32
    ).astype(jnp.bfloat16)
    d_olat = jnp.einsum("qhv,hlv->qhl", d_out, weight_v, preferred_element_type=jnp.float32).astype(
        jnp.bfloat16
    )
    dprob = jnp.einsum("qhl,tl->qht", d_olat, keys_lat, preferred_element_type=jnp.float32)
    delta = jnp.sum(prob * dprob, axis=-1, keepdims=True)
    dscore = (prob * (dprob - delta) * scale).astype(jnp.bfloat16)
    dquery = jnp.einsum("qht,tc->qhc", dscore, keys, preferred_element_type=jnp.float32)
    d_q_rope = dquery[:, :, latent:].astype(jnp.bfloat16)
    d_qlat = dquery[:, :, :latent].astype(jnp.bfloat16)
    d_q_nope = jnp.einsum(
        "qhl,hnl->qhn", d_qlat, weight_k, preferred_element_type=jnp.float32
    ).astype(jnp.bfloat16)
    value_part = jnp.einsum("qht,qhl->tl", prob_low, d_olat, preferred_element_type=jnp.float32)
    dkeys = jnp.einsum("qht,qhc->tc", dscore, qfull, preferred_element_type=jnp.float32)
    dkeys = dkeys + jnp.pad(value_part, ((0, 0), (0, rope)))
    one_hot = (
        asked.reshape(-1)[:, None] == jnp.arange(own_blocks, dtype=jnp.int32)[None, :]
    ).astype(jnp.float32)
    returned = lax.all_to_all(
        dkeys.reshape(peers, per_peer, BLOCK_LEN * width).astype(jnp.bfloat16),
        "seq",
        split_axis=0,
        concat_axis=0,
        tiled=True,
    ).astype(jnp.float32)
    local_grad = jnp.dot(
        one_hot.T,
        returned.reshape(peers * per_peer, BLOCK_LEN * width),
        precision=lax.Precision.HIGHEST,
    )
    d_cache = (
        lax.psum(local_grad.astype(jnp.bfloat16), "grp")
        .astype(jnp.float32)
        .reshape(own_blocks * BLOCK_LEN, width)
    )
    return (attn_out, d_q_nope, d_q_rope, d_cache)


def solution(mesh):
    return jax.shard_map(
        local,
        mesh=mesh,
        in_specs=(
            P("seq", "grp", None),
            P("seq", "grp", None),
            P("seq", None),
            P("grp", "seq"),
            P("grp", "seq"),
            P("seq", "grp", None),
            P("seq", None),
            P("seq", None),
        ),
        out_specs=(
            P("seq", "grp", None),
            P("seq", "grp", None),
            P("seq", "grp", None),
            P("seq", None),
        ),
        check_vma=False,
    )
```

```python
import functools
import math

import jax
import jax.numpy as jnp
from jax import lax
from jax.experimental import pallas as pl
from jax.experimental.pallas import tpu as pltpu
from jax.sharding import PartitionSpec as P

BLOCK_LEN = 64
LANES = 128
HIDDEN = -1e30
VMEM = pl.BlockSpec(memory_space=pltpu.VMEM)
SMEM = pl.BlockSpec(memory_space=pltpu.SMEM)
ANY = pl.BlockSpec(memory_space=pl.ANY)
F32 = jnp.float32
BF16 = jnp.bfloat16


def call(kernel, name, args, specs, outs, scratch=(), mib=32, tied=None):
    out_shape = [jax.ShapeDtypeStruct(s, d) for s, d in outs]
    out_specs = [VMEM] * len(outs)
    aliases = {}
    body = kernel
    if tied is not None:
        args, specs = (tied, *args), [ANY] + specs
        out_shape, out_specs = [jax.ShapeDtypeStruct(tied.shape, tied.dtype)] + out_shape, [ANY] + out_specs
        aliases = {0: 0}
        n_in = len(args)

        def body(*refs):
            kernel(*refs[1:n_in], *refs[n_in + 1 :])

    return pl.pallas_call(
        body,
        out_shape=out_shape,
        in_specs=specs,
        out_specs=out_specs,
        scratch_shapes=list(scratch),
        input_output_aliases=aliases,
        compiler_params=pltpu.CompilerParams(vmem_limit_bytes=mib * 2**20),
        name=name,
    )(*args)


def nt(a, b):
    return lax.dot_general(a, b, (((1,), (1,)), ((), ())), preferred_element_type=F32)


def nn(a, b):
    return lax.dot_general(a, b, (((1,), (0,)), ((), ())), preferred_element_type=F32)


def swap(x, axis, bit):
    n = lax.axis_size(axis)
    return lax.ppermute(x, axis, [(i, i ^ bit) for i in range(n)])


def seq_swap(x):
    return lax.all_to_all(x, "seq", split_axis=0, concat_axis=0, tiled=True)


def tie_kernel(*refs):
    pass


def cut_kernel(ids, cache, out):
    depth = out.shape[0]
    out[...] = cache[pl.ds(pl.multiple_of(ids[1] * depth, 16), depth), :]


def gather_kernel(per_peer, ids, own, other, *refs):
    owners = len(refs) - 2
    caches, outs = refs[:owners], refs[owners:]
    lanes = per_peer * BLOCK_LEN

    def block(row, i, j):
        b = row[0, (ids[0] ^ (2 * i)) * per_peer + j]
        tile = caches[i][:, pl.ds(pl.multiple_of((b >> 1) * LANES, LANES), LANES)]
        return jnp.where((b & 1) == 1, tile[:, BLOCK_LEN:], tile[:, :BLOCK_LEN])

    for row, out in zip((other, own), outs):
        for i in range(owners):
            for j in range(0, per_peer, 2):
                both = jnp.concatenate([block(row, i, j), block(row, i, j + 1)], axis=1)
                at = i * lanes + j * BLOCK_LEN
                out[:, at : at + 2 * BLOCK_LEN] = both


def scatter_kernel(per_peer, ids, rows, *refs):
    got, out, acc = refs[:-2], refs[-2], refs[-1]
    me = ids[0]
    depth = out.shape[0]
    acc[...] = jnp.zeros_like(acc)
    blank = jnp.zeros((depth, BLOCK_LEN), F32)
    for k, piece in enumerate(got):
        for j in range(per_peer):
            b = rows[k, me * per_peer + j]
            at = pl.ds(pl.multiple_of((b >> 1) * LANES, LANES), LANES)
            g = piece[:, j * BLOCK_LEN : (j + 1) * BLOCK_LEN].astype(F32)
            low = jnp.concatenate([g, blank], axis=1)
            high = jnp.concatenate([blank, g], axis=1)
            acc[:, at] = acc[:, at] + jnp.where((b & 1) == 1, high, low)
    out[...] = acc[...].astype(BF16)


def assemble_kernel(ids, *refs):
    parts, out = refs[:-1], refs[-1]
    depth = parts[0].shape[0]
    for k, y in enumerate(parts):
        out[pl.ds(pl.multiple_of((ids[1] ^ k) * depth, 16), depth), :] = y[...].astype(F32)


def weight_k_of(pack, head, uk_rows, tiles):
    rows = uk_rows // tiles
    peers = pack.shape[0]
    cols = []
    for t in range(tiles):
        cols.append(
            jnp.concatenate(
                [pack[r, head, t * rows : (t + 1) * rows, :] for r in range(peers)], axis=0
            )
        )
    return jnp.concatenate(cols, axis=1)


def stacked(pack, head, start, rows):
    peers = pack.shape[0]
    return jnp.concatenate([pack[r, head, start : start + rows, :] for r in range(peers)], axis=0)


def expand_kernel(sizes, pack, away, over_x, out):
    uk_rows, uv_rows, queries, tiles, latent = sizes
    peers, heads = pack.shape[0], pack.shape[1]
    for h in range(heads):
        wk = weight_k_of(pack, h, uk_rows, tiles)
        wv = stacked(pack, h, uk_rows, uv_rows)
        qn = stacked(pack, h, uk_rows + uv_rows, queries)
        do = stacked(pack, h, uk_rows + uv_rows + queries, queries)
        q_lat = nn(qn, wk).astype(BF16)
        d_olat = nt(do, wv).astype(BF16)
        for r in range(peers):
            out[r, h, :, :latent] = q_lat[r * queries : (r + 1) * queries]
            out[r, h, :, latent:] = d_olat[r * queries : (r + 1) * queries]


def reduce_kernel(sizes, pack, lat, out):
    uk_rows, uv_rows, queries, tiles, latent = sizes
    peers, heads = pack.shape[0], pack.shape[1]
    for h in range(heads):
        wk = weight_k_of(pack, h, uk_rows, tiles)
        wv = stacked(pack, h, uk_rows, uv_rows)
        both = jnp.concatenate([lat[r, h] for r in range(peers)], axis=0)
        attn = nn(both[:, :latent], wv).astype(BF16)
        dqn = nt(both[:, latent:], wk).astype(BF16)
        for r in range(peers):
            out[r, h, :, : attn.shape[1]] = attn[r * queries : (r + 1) * queries]
            out[r, h, :, attn.shape[1] :] = dqn[r * queries : (r + 1) * queries]


def tokens_grad(grads, scale, do, cat, delta, kt, p, width):
    keep, send, at, depth = grads
    latent = do.shape[1]
    dp = nn(do[...], kt[:latent])
    ds = (p.astype(F32) * (dp - delta) * scale).astype(BF16)
    part = nt(ds, kt[:width])
    dk = nn(cat[...], jnp.concatenate([ds, p], axis=0)).astype(BF16)
    for k, ref in enumerate((keep, send, keep, send)):
        ref[k // 2, :, at] = dk[k * depth : (k + 1) * depth]
    return part


def attend_kernel(scale, per_peer, ids, sel, rope, qd, *refs):
    keys, refs = (refs[:4], refs[4:8]), refs[8:]
    keeps, sends, lat, d_rope, refs = (refs[0], refs[2]), (refs[1], refs[3]), refs[4], refs[5], refs[6:]
    kt_near, kt_far, pb_near, pb_far, qx, do, sc, flip, cat, o_full, dq = refs
    rows, latent = do.shape
    heads, queries, rope_dim = rope.shape
    width = latent + rope_dim
    slots = qx.shape[1] - width
    depth, half = keys[0][0].shape
    kts, pbs = (kt_near, kt_far), (pb_near, pb_far)

    picks = sel[...] ^ (ids[0] * per_peer)
    slot = lax.broadcasted_iota(jnp.int32, (queries, slots), 1)
    chosen = picks[:, 0:1] == slot
    for j in range(1, picks.shape[1]):
        chosen = chosen | (picks[:, j : j + 1] == slot)
    bias = jnp.where(chosen, 0.0, HIDDEN).astype(BF16)
    bias = jnp.broadcast_to(bias[None], (heads, queries, slots)).reshape(rows, slots)
    qx[:, :latent] = qd[:, :latent]
    qx[:, latent:] = jnp.concatenate([rope[...].reshape(rows, rope_dim), bias], axis=1)
    do[...] = qd[:, latent:]
    for c in range(2):
        for k in range(4):
            at = pl.ds(pl.multiple_of((ids[1] ^ k) * depth, 16), depth)
            kts[c][at, :] = keys[c][k][...]
        place = lax.broadcasted_iota(jnp.int32, (slots, half), 0)
        block = lax.broadcasted_iota(jnp.int32, (slots, half), 1) // BLOCK_LEN
        block = block + (block // per_peer + c) * per_peer
        kts[c][width:, :] = jnp.where(block == place, 1.0, 0.0).astype(BF16)

    scale2 = scale * math.log2(math.e)
    step = 512
    chunks = [(c, i) for c in range(2) for i in range(0, half, step)]
    top = jnp.full((rows, 1), -jnp.inf, F32)
    total = jnp.zeros((rows, 1), F32)
    tops = []
    for n, (c, i) in enumerate(chunks):
        s = nn(qx[...], kts[c][:, i : i + step]) * scale2
        high = jnp.maximum(top, jnp.max(s, axis=1, keepdims=True))
        e = jnp.exp2(s - high)
        sc[:, n * step : (n + 1) * step] = e
        total = total * jnp.exp2(top - high) + jnp.sum(e, axis=1, keepdims=True)
        top = high
        tops.append(high)
    inv = 1.0 / total
    for n, (c, i) in enumerate(chunks):
        pb = (sc[:, n * step : (n + 1) * step] * (jnp.exp2(tops[n] - top) * inv)).astype(BF16)
        pbs[c][:, i : i + step] = pb
        part = nt(pb, kts[c][:latent, i : i + step])
        if n == 0:
            o_full[...] = part
        else:
            o_full[...] += part
    lat[:, :latent] = o_full[...].astype(BF16)
    delta = jnp.sum(o_full[...] * do[...].astype(F32), axis=1, keepdims=True)

    flip[:, :rows] = qx[:, :width].T
    flip[:latent, rows:] = do[...].T
    flip[latent:, rows:] = jnp.zeros((rope_dim, rows), BF16)
    for k in range(4):
        at = pl.ds(pl.multiple_of((ids[1] ^ k) * depth, 16), depth)
        cat[k * depth : (k + 1) * depth] = flip[at, :]
    for n, (c, i) in enumerate([(c, i) for c in (1, 0) for i in range(0, half, step)]):
        at = slice(i, i + step)
        grads = (keeps[c], sends[c], at, depth)
        kt = kts[c].at[:, at]
        part = tokens_grad(grads, scale, do, cat, delta, kt, pbs[c][:, at], width)
        if n == 0:
            dq[...] = part
        else:
            dq[...] += part
    lat[:, latent:] = dq[:, :latent].astype(BF16)
    d_rope[...] = dq[:, latent:].astype(BF16)


def pair_kernel(keep, got, a0, *a2):
    total = keep[...].astype(F32) + got[...].astype(F32)
    a0[...] = total[0].astype(BF16)
    lanes = a2[0].shape[1]
    for i, a in enumerate(a2):
        a[...] = total[1, :, i * lanes : (i + 1) * lanes].astype(BF16)


def owner_kernel(a0, got, *outs):
    total = (a0[...].astype(F32) + got[...].astype(F32)).astype(BF16)
    lanes = outs[0].shape[1]
    for i, out in enumerate(outs):
        out[...] = total[:, i * lanes : (i + 1) * lanes]


def local(q_nope, q_rope, cache, w_uk, w_uv, d_out, sel, slot_blocks):
    peers = lax.axis_size("seq")
    groups = lax.axis_size("grp")
    queries, heads, nope = q_nope.shape
    rope = q_rope.shape[2]
    width = cache.shape[1]
    latent = width - rope
    value = d_out.shape[2]
    slots = slot_blocks.shape[1]
    per_peer = slots // peers
    if not (peers == 8 and groups == 4 and heads % peers == 0 and per_peer % 2 == 0):
        return local_general(q_nope, q_rope, cache, w_uk, w_uv, d_out, sel, slot_blocks)
    ids = jnp.stack([lax.axis_index("seq"), lax.axis_index("grp")]).astype(jnp.int32)
    tokens = cache.shape[0]
    depth = width // groups
    lanes = per_peer * BLOCK_LEN
    held = peers // 2
    half = held * lanes
    share = heads // peers
    rows = heads * queries
    scale = 1.0 / math.sqrt(nope + rope)

    row1 = swap(slot_blocks, "seq", 1)
    (c0,) = call(cut_kernel, "cut", (ids, cache.T), [SMEM, VMEM], [((depth, tokens), BF16)])
    asked_y = jnp.concatenate([slot_blocks, row1], axis=0)
    asked = jnp.concatenate([asked_y] + [swap(asked_y, "seq", bit) for bit in (2, 4, 6)], axis=0)
    c2 = swap(c0, "seq", 4)
    c1 = swap(c0, "seq", 2)

    (c2,) = call(tie_kernel, "after", (asked,), [ANY], [], tied=c2)
    c3 = swap(c2, "seq", 2)
    away, k0 = call(
        functools.partial(gather_kernel, per_peer),
        "gather",
        (ids, slot_blocks, row1, c0, c1, c2, c3),
        [SMEM] * 3 + [VMEM] * 4,
        [((depth, half), BF16)] * 2,
    )
    k_away, k0_x = swap(away, "seq", 1), swap(k0, "grp", 2)

    n_rows = w_uk.shape[1] // latent
    l_rows = w_uv.shape[1] // value
    tiles = latent // LANES
    uk = w_uk.reshape(heads, n_rows, tiles, LANES).transpose(0, 2, 1, 3)
    pack = jnp.concatenate(
        [
            uk.reshape(heads, n_rows * tiles, LANES),
            w_uv.reshape(heads, l_rows, value),
            q_nope.transpose(1, 0, 2),
            d_out.transpose(1, 0, 2),
        ],
        axis=1,
    )
    (pack,) = call(tie_kernel, "after", (c1, c3), [ANY] * 2, [], tied=pack)
    pack = seq_swap(pack).reshape(peers, share, -1, LANES)
    sizes = (n_rows * tiles, l_rows, queries, tiles, latent)
    (lat,) = call(
        functools.partial(expand_kernel, sizes),
        "expand",
        (pack, k_away, k0_x),
        [VMEM, ANY, ANY],
        [((peers, share, queries, 2 * latent), BF16)],
    )
    qd = seq_swap(lat).reshape(rows, 2 * latent)

    keys = []
    for k, k2 in ((k0, k0_x), (k_away, swap(k_away, "grp", 2))):
        keys += [k, swap(k, "grp", 1), k2, swap(k2, "grp", 1)]
    rope_rows = q_rope.transpose(1, 0, 2)
    near_keep, near_send, far_keep, far_send, lat, d_rope = call(
        functools.partial(attend_kernel, scale, per_peer),
        "attend",
        (ids, sel, rope_rows, qd, *keys),
        [SMEM] + [VMEM] * 11,
        [((2, depth, half), BF16)] * 4 + [((rows, 2 * latent), BF16), ((rows, rope), BF16)],
        [pltpu.VMEM((width + slots, half), BF16)] * 2
        + [pltpu.VMEM((rows, half), BF16)] * 2
        + [
            pltpu.VMEM((rows, width + slots), BF16),
            pltpu.VMEM((rows, latent), BF16),
            pltpu.VMEM((rows, 2 * half), F32),
            pltpu.VMEM((width, 2 * rows), BF16),
            pltpu.VMEM((width, 2 * rows), BF16),
            pltpu.VMEM((rows, latent), F32),
            pltpu.VMEM((rows, width), F32),
        ],
        60,
    )

    def pair(keep, send, tied=None):
        outs = [((depth, half), BF16)] * 2
        return call(pair_kernel, "pair", (keep, swap(send, "grp", 1)), [VMEM] * 2, outs, tied=tied)


    def owner(a0, a2):
        outs = [((depth, lanes), BF16)] * held
        return call(owner_kernel, "owner", (a0, swap(a2, "grp", 2)), [VMEM] * 2, outs)

    far = pair(far_keep, far_send)
    first, *near = pair(near_keep, near_send, tied=far[0])
    far = owner(first, far[1])
    lat = seq_swap(lat.reshape(peers, share, queries, 2 * latent))
    (res,) = call(
        functools.partial(reduce_kernel, sizes),
        "reduce",
        (pack, lat),
        [VMEM] * 2,
        [((peers, share, queries, value + nope), BF16)],
    )
    near = owner(*near)
    got = [near[0]]
    for k in range(1, peers):
        got.append(swap((far if k % 2 else near)[k // 2], "seq", k))
    res = seq_swap(res).reshape(heads, queries, value + nope)

    (y0,) = call(
        functools.partial(scatter_kernel, per_peer),
        "scatter",
        (ids, asked, *got),
        [SMEM, SMEM] + [VMEM] * len(got),
        [((depth, tokens), BF16)],
        [pltpu.VMEM((depth, tokens), F32)],
    )
    y2 = swap(y0, "grp", 2)
    y1 = swap(y0, "grp", 1)
    y3 = swap(y2, "grp", 1)
    (d_cache,) = call(
        assemble_kernel,
        "assemble",
        (ids, y0, y1, y2, y3),
        [SMEM] + [VMEM] * 4,
        [((width, tokens), F32)],
    )
    return (
        res[:, :, :value].transpose(1, 0, 2),
        res[:, :, value:].transpose(1, 0, 2),
        d_rope.reshape(heads, queries, rope).transpose(1, 0, 2),
        d_cache.T,
    )


def local_general(q_nope, q_rope, cache, w_uk, w_uv, d_out, sel, slot_blocks):
    peers = lax.axis_size("seq")
    queries, heads, nope = q_nope.shape
    rope = q_rope.shape[2]
    width = cache.shape[1]
    latent = width - rope
    value = d_out.shape[2]
    slot_total = slot_blocks.shape[1]
    per_peer = slot_total // peers
    own_blocks = cache.shape[0] // BLOCK_LEN
    scale = 1.0 / math.sqrt(nope + rope)
    gathered_k, gathered_v = (
        lax.all_gather(w_uk, "seq", axis=1, tiled=True),
        lax.all_gather(w_uv, "seq", axis=1, tiled=True),
    )
    weight_k = gathered_k.reshape(heads, nope, latent)
    weight_v = gathered_v.reshape(heads, latent, value)
    wanted = slot_blocks.reshape(peers, per_peer)
    asked = lax.all_to_all(wanted, "seq", split_axis=0, concat_axis=0, tiled=True)
    blocks = cache.reshape(own_blocks, BLOCK_LEN, width)
    arrived = lax.all_to_all(blocks[asked], "seq", split_axis=0, concat_axis=0, tiled=True)
    keys = arrived.reshape(slot_total * BLOCK_LEN, width)
    keys_lat = keys[:, :latent]
    q_lat = jnp.einsum("qhn,hnl->qhl", q_nope, weight_k, preferred_element_type=jnp.float32).astype(
        jnp.bfloat16
    )
    qfull = jnp.concatenate([q_lat, q_rope], axis=-1)
    chosen = jnp.any(
        sel[:, :, None] == jnp.arange(slot_total, dtype=jnp.int32)[None, None, :], axis=1
    )
    live = jnp.repeat(chosen, BLOCK_LEN, axis=1)[:, None, :]
    score = jnp.einsum("qhc,tc->qht", qfull, keys, preferred_element_type=jnp.float32) * scale
    score = jnp.where(live, score, -jnp.inf)
    prob = jax.nn.softmax(score, axis=-1)
    prob_low = prob.astype(jnp.bfloat16)
    olat = jnp.einsum("qht,tl->qhl", prob_low, keys_lat, preferred_element_type=jnp.float32).astype(
        jnp.bfloat16
    )
    attn_out = jnp.einsum(
        "qhl,hlv->qhv", olat, weight_v, preferred_element_type=jnp.float32
    ).astype(jnp.bfloat16)
    d_olat = jnp.einsum("qhv,hlv->qhl", d_out, weight_v, preferred_element_type=jnp.float32).astype(
        jnp.bfloat16
    )
    dprob = jnp.einsum("qhl,tl->qht", d_olat, keys_lat, preferred_element_type=jnp.float32)
    delta = jnp.sum(prob * dprob, axis=-1, keepdims=True)
    dscore = (prob * (dprob - delta) * scale).astype(jnp.bfloat16)
    dquery = jnp.einsum("qht,tc->qhc", dscore, keys, preferred_element_type=jnp.float32)
    d_q_rope = dquery[:, :, latent:].astype(jnp.bfloat16)
    d_qlat = dquery[:, :, :latent].astype(jnp.bfloat16)
    d_q_nope = jnp.einsum(
        "qhl,hnl->qhn", d_qlat, weight_k, preferred_element_type=jnp.float32
    ).astype(jnp.bfloat16)
    value_part = jnp.einsum("qht,qhl->tl", prob_low, d_olat, preferred_element_type=jnp.float32)
    dkeys = jnp.einsum("qht,qhc->tc", dscore, qfull, preferred_element_type=jnp.float32)
    dkeys = dkeys + jnp.pad(value_part, ((0, 0), (0, rope)))
    one_hot = (
        asked.reshape(-1)[:, None] == jnp.arange(own_blocks, dtype=jnp.int32)[None, :]
    ).astype(jnp.float32)
    returned = lax.all_to_all(
        dkeys.reshape(peers, per_peer, BLOCK_LEN * width).astype(jnp.bfloat16),
        "seq",
        split_axis=0,
        concat_axis=0,
        tiled=True,
    ).astype(jnp.float32)
    local_grad = jnp.dot(
        one_hot.T,
        returned.reshape(peers * per_peer, BLOCK_LEN * width),
        precision=lax.Precision.HIGHEST,
    )
    d_cache = (
        lax.psum(local_grad.astype(jnp.bfloat16), "grp")
        .astype(jnp.float32)
        .reshape(own_blocks * BLOCK_LEN, width)
    )
    return (attn_out, d_q_nope, d_q_rope, d_cache)


def solution(mesh):
    return jax.shard_map(
        local,
        mesh=mesh,
        in_specs=(
            P("seq", "grp", None),
            P("seq", "grp", None),
            P("seq", None),
            P("grp", "seq"),
            P("grp", "seq"),
            P("seq", "grp", None),
            P("seq", None),
            P("seq", None),
        ),
        out_specs=(
            P("seq", "grp", None),
            P("seq", "grp", None),
            P("seq", "grp", None),
            P("seq", None),
        ),
        check_vma=False,
    )
```

```python
import functools
import math

import jax
import jax.numpy as jnp
from jax import lax
from jax.experimental import pallas as pl
from jax.experimental.pallas import tpu as pltpu
from jax.sharding import PartitionSpec as P

BLOCK_LEN = 64
LANES = 128
HIDDEN = -1e30
VMEM = pl.BlockSpec(memory_space=pltpu.VMEM)
SMEM = pl.BlockSpec(memory_space=pltpu.SMEM)
ANY = pl.BlockSpec(memory_space=pl.ANY)
F32 = jnp.float32
BF16 = jnp.bfloat16


def call(kernel, name, args, specs, outs, scratch=(), mib=32, tied=None):
    out_shape = [jax.ShapeDtypeStruct(s, d) for s, d in outs]
    out_specs = [VMEM] * len(outs)
    aliases = {}
    body = kernel
    if tied is not None:
        args, specs = (tied, *args), [ANY] + specs
        out_shape, out_specs = [jax.ShapeDtypeStruct(tied.shape, tied.dtype)] + out_shape, [ANY] + out_specs
        aliases = {0: 0}
        n_in = len(args)

        def body(*refs):
            kernel(*refs[1:n_in], *refs[n_in + 1 :])

    return pl.pallas_call(
        body,
        out_shape=out_shape,
        in_specs=specs,
        out_specs=out_specs,
        scratch_shapes=list(scratch),
        input_output_aliases=aliases,
        compiler_params=pltpu.CompilerParams(vmem_limit_bytes=mib * 2**20),
        name=name,
    )(*args)


def nt(a, b):
    return lax.dot_general(a, b, (((1,), (1,)), ((), ())), preferred_element_type=F32)


def nn(a, b):
    return lax.dot_general(a, b, (((1,), (0,)), ((), ())), preferred_element_type=F32)


def swap(x, axis, bit):
    n = lax.axis_size(axis)
    return lax.ppermute(x, axis, [(i, i ^ bit) for i in range(n)])


def seq_swap(x):
    return lax.all_to_all(x, "seq", split_axis=0, concat_axis=0, tiled=True)


def tie_kernel(*refs):
    pass


def cut_kernel(ids, cache, out):
    depth = out.shape[0]
    out[...] = cache[pl.ds(pl.multiple_of(ids[1] * depth, 16), depth), :]


def gather_kernel(per_peer, ids, own, other, *refs):
    owners = len(refs) - 2
    caches, outs = refs[:owners], refs[owners:]
    lanes = per_peer * BLOCK_LEN

    def block(row, i, j):
        b = row[0, (ids[0] ^ (2 * i)) * per_peer + j]
        tile = caches[i][:, pl.ds(pl.multiple_of((b >> 1) * LANES, LANES), LANES)]
        return jnp.where((b & 1) == 1, tile[:, BLOCK_LEN:], tile[:, :BLOCK_LEN])

    for row, out in zip((other, own), outs):
        for i in range(owners):
            for j in range(0, per_peer, 2):
                both = jnp.concatenate([block(row, i, j), block(row, i, j + 1)], axis=1)
                at = i * lanes + j * BLOCK_LEN
                out[:, at : at + 2 * BLOCK_LEN] = both


def scatter_kernel(per_peer, ids, rows, *refs):
    got, out, acc = refs[:-2], refs[-2], refs[-1]
    me = ids[0]
    depth = out.shape[0]
    acc[...] = jnp.zeros_like(acc)
    blank = jnp.zeros((depth, BLOCK_LEN), F32)
    for k, piece in enumerate(got):
        for j in range(per_peer):
            b = rows[k, me * per_peer + j]
            at = pl.ds(pl.multiple_of((b >> 1) * LANES, LANES), LANES)
            g = piece[:, j * BLOCK_LEN : (j + 1) * BLOCK_LEN].astype(F32)
            low = jnp.concatenate([g, blank], axis=1)
            high = jnp.concatenate([blank, g], axis=1)
            acc[:, at] = acc[:, at] + jnp.where((b & 1) == 1, high, low)
    out[...] = acc[...].astype(BF16)


def assemble_kernel(ids, *refs):
    parts, out = refs[:-1], refs[-1]
    depth = parts[0].shape[0]
    for k, y in enumerate(parts):
        out[pl.ds(pl.multiple_of((ids[1] ^ k) * depth, 16), depth), :] = y[...].astype(F32)


def weight_k_of(pack, head, uk_rows, tiles):
    rows = uk_rows // tiles
    peers = pack.shape[0]
    cols = []
    for t in range(tiles):
        cols.append(
            jnp.concatenate(
                [pack[r, head, t * rows : (t + 1) * rows, :] for r in range(peers)], axis=0
            )
        )
    return jnp.concatenate(cols, axis=1)


def stacked(pack, head, start, rows):
    peers = pack.shape[0]
    return jnp.concatenate([pack[r, head, start : start + rows, :] for r in range(peers)], axis=0)


def expand_kernel(sizes, pack, away, over_x, out):
    uk_rows, uv_rows, queries, tiles, latent = sizes
    peers, heads = pack.shape[0], pack.shape[1]
    for h in range(heads):
        wk = weight_k_of(pack, h, uk_rows, tiles)
        wv = stacked(pack, h, uk_rows, uv_rows)
        qn = stacked(pack, h, uk_rows + uv_rows, queries)
        do = stacked(pack, h, uk_rows + uv_rows + queries, queries)
        q_lat = nn(qn, wk).astype(BF16)
        d_olat = nt(do, wv).astype(BF16)
        for r in range(peers):
            out[r, h, :, :latent] = q_lat[r * queries : (r + 1) * queries]
            out[r, h, :, latent:] = d_olat[r * queries : (r + 1) * queries]


def reduce_kernel(sizes, pack, lat, out):
    uk_rows, uv_rows, queries, tiles, latent = sizes
    peers, heads = pack.shape[0], pack.shape[1]
    for h in range(heads):
        wk = weight_k_of(pack, h, uk_rows, tiles)
        wv = stacked(pack, h, uk_rows, uv_rows)
        both = jnp.concatenate([lat[r, h] for r in range(peers)], axis=0)
        attn = nn(both[:, :latent], wv).astype(BF16)
        dqn = nt(both[:, latent:], wk).astype(BF16)
        for r in range(peers):
            out[r, h, :, : attn.shape[1]] = attn[r * queries : (r + 1) * queries]
            out[r, h, :, attn.shape[1] :] = dqn[r * queries : (r + 1) * queries]


def tokens_grad(grads, scale, do, cat, delta, kt, p, width):
    keep, send, at, depth = grads
    latent = do.shape[1]
    dp = nn(do[...], kt[:latent])
    ds = (p.astype(F32) * (dp - delta) * scale).astype(BF16)
    part = nt(ds, kt[:width])
    dk = nn(cat[...], jnp.concatenate([ds, p], axis=0)).astype(BF16)
    for k, ref in enumerate((keep, send, keep, send)):
        ref[k // 2, :, at] = dk[k * depth : (k + 1) * depth]
    return part


def attend_kernel(scale, per_peer, ids, sel, rope, qd, *refs):
    keys, refs = (refs[:4], refs[4:8]), refs[8:]
    keeps, sends, lat, d_rope, refs = (refs[0], refs[2]), (refs[1], refs[3]), refs[4], refs[5], refs[6:]
    kt_near, kt_far, pb_near, pb_far, qx, do, sc, flip, cat, o_full, dq = refs
    rows, latent = do.shape
    heads, queries, rope_dim = rope.shape
    width = latent + rope_dim
    slots = qx.shape[1] - width
    depth, half = keys[0][0].shape
    kts, pbs = (kt_near, kt_far), (pb_near, pb_far)

    picks = sel[...] ^ (ids[0] * per_peer)
    slot = lax.broadcasted_iota(jnp.int32, (queries, slots), 1)
    chosen = picks[:, 0:1] == slot
    for j in range(1, picks.shape[1]):
        chosen = chosen | (picks[:, j : j + 1] == slot)
    bias = jnp.where(chosen, 0.0, HIDDEN).astype(BF16)
    bias = jnp.broadcast_to(bias[None], (heads, queries, slots)).reshape(rows, slots)
    qx[:, :latent] = qd[:, :latent]
    qx[:, latent:] = jnp.concatenate([rope[...].reshape(rows, rope_dim), bias], axis=1)
    do[...] = qd[:, latent:]
    for c in range(2):
        for k in range(4):
            at = pl.ds(pl.multiple_of((ids[1] ^ k) * depth, 16), depth)
            kts[c][at, :] = keys[c][k][...]
        place = lax.broadcasted_iota(jnp.int32, (slots, half), 0)
        block = lax.broadcasted_iota(jnp.int32, (slots, half), 1) // BLOCK_LEN
        block = block + (block // per_peer + c) * per_peer
        kts[c][width:, :] = jnp.where(block == place, 1.0, 0.0).astype(BF16)

    scale2 = scale * math.log2(math.e)
    step = 1024
    chunks = [(c, i) for c in range(2) for i in range(0, half, step)]
    top = jnp.full((rows, 1), -jnp.inf, F32)
    total = jnp.zeros((rows, 1), F32)
    tops = []
    for n, (c, i) in enumerate(chunks):
        s = nn(qx[...], kts[c][:, i : i + step]) * scale2
        high = jnp.maximum(top, jnp.max(s, axis=1, keepdims=True))
        e = jnp.exp2(s - high)
        sc[:, n * step : (n + 1) * step] = e
        total = total * jnp.exp2(top - high) + jnp.sum(e, axis=1, keepdims=True)
        top = high
        tops.append(high)
    inv = 1.0 / total
    for n, (c, i) in enumerate(chunks):
        pb = (sc[:, n * step : (n + 1) * step] * (jnp.exp2(tops[n] - top) * inv)).astype(BF16)
        pbs[c][:, i : i + step] = pb
        part = nt(pb, kts[c][:latent, i : i + step])
        if n == 0:
            o_full[...] = part
        else:
            o_full[...] += part
    lat[:, :latent] = o_full[...].astype(BF16)
    delta = jnp.sum(o_full[...] * do[...].astype(F32), axis=1, keepdims=True)

    flip[:, :rows] = qx[:, :width].T
    flip[:latent, rows:] = do[...].T
    flip[latent:, rows:] = jnp.zeros((rope_dim, rows), BF16)
    for k in range(4):
        at = pl.ds(pl.multiple_of((ids[1] ^ k) * depth, 16), depth)
        cat[k * depth : (k + 1) * depth] = flip[at, :]
    for n, (c, i) in enumerate([(c, i) for c in (1, 0) for i in range(0, half, step)]):
        at = slice(i, i + step)
        grads = (keeps[c], sends[c], at, depth)
        kt = kts[c].at[:, at]
        part = tokens_grad(grads, scale, do, cat, delta, kt, pbs[c][:, at], width)
        if n == 0:
            dq[...] = part
        else:
            dq[...] += part
    lat[:, latent:] = dq[:, :latent].astype(BF16)
    d_rope[...] = dq[:, latent:].astype(BF16)


def pair_kernel(keep, got, a0, *a2):
    total = keep[...].astype(F32) + got[...].astype(F32)
    a0[...] = total[0].astype(BF16)
    lanes = a2[0].shape[1]
    for i, a in enumerate(a2):
        a[...] = total[1, :, i * lanes : (i + 1) * lanes].astype(BF16)


def owner_kernel(a0, got, *outs):
    total = (a0[...].astype(F32) + got[...].astype(F32)).astype(BF16)
    lanes = outs[0].shape[1]
    for i, out in enumerate(outs):
        out[...] = total[:, i * lanes : (i + 1) * lanes]


def local(q_nope, q_rope, cache, w_uk, w_uv, d_out, sel, slot_blocks):
    peers = lax.axis_size("seq")
    groups = lax.axis_size("grp")
    queries, heads, nope = q_nope.shape
    rope = q_rope.shape[2]
    width = cache.shape[1]
    latent = width - rope
    value = d_out.shape[2]
    slots = slot_blocks.shape[1]
    per_peer = slots // peers
    if not (peers == 8 and groups == 4 and heads % peers == 0 and per_peer % 2 == 0):
        return local_general(q_nope, q_rope, cache, w_uk, w_uv, d_out, sel, slot_blocks)
    ids = jnp.stack([lax.axis_index("seq"), lax.axis_index("grp")]).astype(jnp.int32)
    tokens = cache.shape[0]
    depth = width // groups
    lanes = per_peer * BLOCK_LEN
    held = peers // 2
    half = held * lanes
    share = heads // peers
    rows = heads * queries
    scale = 1.0 / math.sqrt(nope + rope)

    row1 = swap(slot_blocks, "seq", 1)
    (c0,) = call(cut_kernel, "cut", (ids, cache.T), [SMEM, VMEM], [((depth, tokens), BF16)])
    asked_y = jnp.concatenate([slot_blocks, row1], axis=0)
    asked = jnp.concatenate([asked_y] + [swap(asked_y, "seq", bit) for bit in (2, 4, 6)], axis=0)
    c2 = swap(c0, "seq", 4)
    c1 = swap(c0, "seq", 2)

    (c2,) = call(tie_kernel, "after", (asked, c1), [ANY] * 2, [], tied=c2)
    c3 = swap(c2, "seq", 2)
    away, k0 = call(
        functools.partial(gather_kernel, per_peer),
        "gather",
        (ids, slot_blocks, row1, c0, c1, c2, c3),
        [SMEM] * 3 + [VMEM] * 4,
        [((depth, half), BF16)] * 2,
    )
    k_away, k0_x = swap(away, "seq", 1), swap(k0, "grp", 2)

    n_rows = w_uk.shape[1] // latent
    l_rows = w_uv.shape[1] // value
    tiles = latent // LANES
    uk = w_uk.reshape(heads, n_rows, tiles, LANES).transpose(0, 2, 1, 3)
    pack = jnp.concatenate(
        [
            uk.reshape(heads, n_rows * tiles, LANES),
            w_uv.reshape(heads, l_rows, value),
            q_nope.transpose(1, 0, 2),
            d_out.transpose(1, 0, 2),
        ],
        axis=1,
    )
    (pack,) = call(tie_kernel, "after", (c1, c3), [ANY] * 2, [], tied=pack)
    pack = seq_swap(pack).reshape(peers, share, -1, LANES)
    sizes = (n_rows * tiles, l_rows, queries, tiles, latent)
    (lat,) = call(
        functools.partial(expand_kernel, sizes),
        "expand",
        (pack, k_away, k0_x),
        [VMEM, ANY, ANY],
        [((peers, share, queries, 2 * latent), BF16)],
    )
    qd = seq_swap(lat).reshape(rows, 2 * latent)

    keys = []
    for k, k2 in ((k0, k0_x), (k_away, swap(k_away, "grp", 2))):
        keys += [k, swap(k, "grp", 1), k2, swap(k2, "grp", 1)]
    rope_rows = q_rope.transpose(1, 0, 2)
    near_keep, near_send, far_keep, far_send, lat, d_rope = call(
        functools.partial(attend_kernel, scale, per_peer),
        "attend",
        (ids, sel, rope_rows, qd, *keys),
        [SMEM] + [VMEM] * 11,
        [((2, depth, half), BF16)] * 4 + [((rows, 2 * latent), BF16), ((rows, rope), BF16)],
        [pltpu.VMEM((width + slots, half), BF16)] * 2
        + [pltpu.VMEM((rows, half), BF16)] * 2
        + [
            pltpu.VMEM((rows, width + slots), BF16),
            pltpu.VMEM((rows, latent), BF16),
            pltpu.VMEM((rows, 2 * half), F32),
            pltpu.VMEM((width, 2 * rows), BF16),
            pltpu.VMEM((width, 2 * rows), BF16),
            pltpu.VMEM((rows, latent), F32),
            pltpu.VMEM((rows, width), F32),
        ],
        60,
    )

    def pair(keep, send, tied=None):
        outs = [((depth, half), BF16)] * 2
        return call(pair_kernel, "pair", (keep, swap(send, "grp", 1)), [VMEM] * 2, outs, tied=tied)


    def owner(a0, a2):
        outs = [((depth, lanes), BF16)] * held
        return call(owner_kernel, "owner", (a0, swap(a2, "grp", 2)), [VMEM] * 2, outs)

    far = pair(far_keep, far_send)
    first, *near = pair(near_keep, near_send, tied=far[0])
    far = owner(first, far[1])
    lat = seq_swap(lat.reshape(peers, share, queries, 2 * latent))
    (res,) = call(
        functools.partial(reduce_kernel, sizes),
        "reduce",
        (pack, lat),
        [VMEM] * 2,
        [((peers, share, queries, value + nope), BF16)],
    )
    near = owner(*near)
    got = [near[0]] + [None] * (peers - 1)
    for k in (7, 5, 3, 1, 6, 4, 2):
        got[k] = swap((far if k % 2 else near)[k // 2], "seq", k)
    res = seq_swap(res).reshape(heads, queries, value + nope)

    (y0,) = call(
        functools.partial(scatter_kernel, per_peer),
        "scatter",
        (ids, asked, *got),
        [SMEM, SMEM] + [VMEM] * len(got),
        [((depth, tokens), BF16)],
        [pltpu.VMEM((depth, tokens), F32)],
    )
    y2 = swap(y0, "grp", 2)
    y1 = swap(y0, "grp", 1)
    y3 = swap(y2, "grp", 1)
    (d_cache,) = call(
        assemble_kernel,
        "assemble",
        (ids, y0, y1, y2, y3),
        [SMEM] + [VMEM] * 4,
        [((width, tokens), F32)],
    )
    return (
        res[:, :, :value].transpose(1, 0, 2),
        res[:, :, value:].transpose(1, 0, 2),
        d_rope.reshape(heads, queries, rope).transpose(1, 0, 2),
        d_cache.T,
    )


def local_general(q_nope, q_rope, cache, w_uk, w_uv, d_out, sel, slot_blocks):
    peers = lax.axis_size("seq")
    queries, heads, nope = q_nope.shape
    rope = q_rope.shape[2]
    width = cache.shape[1]
    latent = width - rope
    value = d_out.shape[2]
    slot_total = slot_blocks.shape[1]
    per_peer = slot_total // peers
    own_blocks = cache.shape[0] // BLOCK_LEN
    scale = 1.0 / math.sqrt(nope + rope)
    gathered_k, gathered_v = (
        lax.all_gather(w_uk, "seq", axis=1, tiled=True),
        lax.all_gather(w_uv, "seq", axis=1, tiled=True),
    )
    weight_k = gathered_k.reshape(heads, nope, latent)
    weight_v = gathered_v.reshape(heads, latent, value)
    wanted = slot_blocks.reshape(peers, per_peer)
    asked = lax.all_to_all(wanted, "seq", split_axis=0, concat_axis=0, tiled=True)
    blocks = cache.reshape(own_blocks, BLOCK_LEN, width)
    arrived = lax.all_to_all(blocks[asked], "seq", split_axis=0, concat_axis=0, tiled=True)
    keys = arrived.reshape(slot_total * BLOCK_LEN, width)
    keys_lat = keys[:, :latent]
    q_lat = jnp.einsum("qhn,hnl->qhl", q_nope, weight_k, preferred_element_type=jnp.float32).astype(
        jnp.bfloat16
    )
    qfull = jnp.concatenate([q_lat, q_rope], axis=-1)
    chosen = jnp.any(
        sel[:, :, None] == jnp.arange(slot_total, dtype=jnp.int32)[None, None, :], axis=1
    )
    live = jnp.repeat(chosen, BLOCK_LEN, axis=1)[:, None, :]
    score = jnp.einsum("qhc,tc->qht", qfull, keys, preferred_element_type=jnp.float32) * scale
    score = jnp.where(live, score, -jnp.inf)
    prob = jax.nn.softmax(score, axis=-1)
    prob_low = prob.astype(jnp.bfloat16)
    olat = jnp.einsum("qht,tl->qhl", prob_low, keys_lat, preferred_element_type=jnp.float32).astype(
        jnp.bfloat16
    )
    attn_out = jnp.einsum(
        "qhl,hlv->qhv", olat, weight_v, preferred_element_type=jnp.float32
    ).astype(jnp.bfloat16)
    d_olat = jnp.einsum("qhv,hlv->qhl", d_out, weight_v, preferred_element_type=jnp.float32).astype(
        jnp.bfloat16
    )
    dprob = jnp.einsum("qhl,tl->qht", d_olat, keys_lat, preferred_element_type=jnp.float32)
    delta = jnp.sum(prob * dprob, axis=-1, keepdims=True)
    dscore = (prob * (dprob - delta) * scale).astype(jnp.bfloat16)
    dquery = jnp.einsum("qht,tc->qhc", dscore, keys, preferred_element_type=jnp.float32)
    d_q_rope = dquery[:, :, latent:].astype(jnp.bfloat16)
    d_qlat = dquery[:, :, :latent].astype(jnp.bfloat16)
    d_q_nope = jnp.einsum(
        "qhl,hnl->qhn", d_qlat, weight_k, preferred_element_type=jnp.float32
    ).astype(jnp.bfloat16)
    value_part = jnp.einsum("qht,qhl->tl", prob_low, d_olat, preferred_element_type=jnp.float32)
    dkeys = jnp.einsum("qht,qhc->tc", dscore, qfull, preferred_element_type=jnp.float32)
    dkeys = dkeys + jnp.pad(value_part, ((0, 0), (0, rope)))
    one_hot = (
        asked.reshape(-1)[:, None] == jnp.arange(own_blocks, dtype=jnp.int32)[None, :]
    ).astype(jnp.float32)
    returned = lax.all_to_all(
        dkeys.reshape(peers, per_peer, BLOCK_LEN * width).astype(jnp.bfloat16),
        "seq",
        split_axis=0,
        concat_axis=0,
        tiled=True,
    ).astype(jnp.float32)
    local_grad = jnp.dot(
        one_hot.T,
        returned.reshape(peers * per_peer, BLOCK_LEN * width),
        precision=lax.Precision.HIGHEST,
    )
    d_cache = (
        lax.psum(local_grad.astype(jnp.bfloat16), "grp")
        .astype(jnp.float32)
        .reshape(own_blocks * BLOCK_LEN, width)
    )
    return (attn_out, d_q_nope, d_q_rope, d_cache)


def solution(mesh):
    return jax.shard_map(
        local,
        mesh=mesh,
        in_specs=(
            P("seq", "grp", None),
            P("seq", "grp", None),
            P("seq", None),
            P("grp", "seq"),
            P("grp", "seq"),
            P("seq", "grp", None),
            P("seq", None),
            P("seq", None),
        ),
        out_specs=(
            P("seq", "grp", None),
            P("seq", "grp", None),
            P("seq", "grp", None),
            P("seq", None),
        ),
        check_vma=False,
    )
```

```python
import functools
import math

import jax
import jax.numpy as jnp
from jax import lax
from jax.experimental import pallas as pl
from jax.experimental.pallas import tpu as pltpu
from jax.sharding import PartitionSpec as P

BLOCK_LEN = 64
LANES = 128
HIDDEN = -1e30
VMEM = pl.BlockSpec(memory_space=pltpu.VMEM)
SMEM = pl.BlockSpec(memory_space=pltpu.SMEM)
ANY = pl.BlockSpec(memory_space=pl.ANY)
F32 = jnp.float32
BF16 = jnp.bfloat16


def call(kernel, name, args, specs, outs, scratch=(), mib=32, tied=None, out_specs=None):
    out_shape = [jax.ShapeDtypeStruct(s, d) for s, d in outs]
    out_specs = out_specs or [VMEM] * len(outs)
    aliases = {}
    body = kernel
    if tied is not None:
        args, specs = (tied, *args), [ANY] + specs
        out_shape, out_specs = [jax.ShapeDtypeStruct(tied.shape, tied.dtype)] + out_shape, [ANY] + out_specs
        aliases = {0: 0}
        n_in = len(args)

        def body(*refs):
            kernel(*refs[1:n_in], *refs[n_in + 1 :])

    return pl.pallas_call(
        body,
        out_shape=out_shape,
        in_specs=specs,
        out_specs=out_specs,
        scratch_shapes=list(scratch),
        input_output_aliases=aliases,
        compiler_params=pltpu.CompilerParams(vmem_limit_bytes=mib * 2**20),
        name=name,
    )(*args)


def nt(a, b):
    return lax.dot_general(a, b, (((1,), (1,)), ((), ())), preferred_element_type=F32)


def nn(a, b):
    return lax.dot_general(a, b, (((1,), (0,)), ((), ())), preferred_element_type=F32)


def swap(x, axis, bit):
    n = lax.axis_size(axis)
    return lax.ppermute(x, axis, [(i, i ^ bit) for i in range(n)])


def seq_swap(x):
    return lax.all_to_all(x, "seq", split_axis=0, concat_axis=0, tiled=True)


def tie_kernel(*refs):
    pass


def cut_kernel(ids, cache, out, sem):
    depth = out.shape[0]
    part = cache.at[pl.ds(pl.multiple_of(ids[1] * depth, 16), depth), :]
    copy = pltpu.make_async_copy(part, out, sem)
    copy.start()
    copy.wait()


def gather_kernel(per_peer, ids, own, other, *refs):
    owners = len(refs) - 2
    caches, outs = refs[:owners], refs[owners:]
    lanes = per_peer * BLOCK_LEN

    def block(row, i, j):
        b = row[0, (ids[0] ^ (2 * i)) * per_peer + j]
        tile = caches[i][:, pl.ds(pl.multiple_of((b >> 1) * LANES, LANES), LANES)]
        return jnp.where((b & 1) == 1, tile[:, BLOCK_LEN:], tile[:, :BLOCK_LEN])

    for row, out in zip((other, own), outs):
        for i in range(owners):
            for j in range(0, per_peer, 2):
                both = jnp.concatenate([block(row, i, j), block(row, i, j + 1)], axis=1)
                at = i * lanes + j * BLOCK_LEN
                out[:, at : at + 2 * BLOCK_LEN] = both


def scatter_kernel(per_peer, ids, rows, *refs):
    got, out, acc = refs[:-2], refs[-2], refs[-1]
    me = ids[0]
    depth = out.shape[0]
    acc[...] = jnp.zeros_like(acc)
    blank = jnp.zeros((depth, BLOCK_LEN), F32)
    for k, piece in enumerate(got):
        for j in range(per_peer):
            b = rows[k, me * per_peer + j]
            at = pl.ds(pl.multiple_of((b >> 1) * LANES, LANES), LANES)
            g = piece[:, j * BLOCK_LEN : (j + 1) * BLOCK_LEN].astype(F32)
            low = jnp.concatenate([g, blank], axis=1)
            high = jnp.concatenate([blank, g], axis=1)
            acc[:, at] = acc[:, at] + jnp.where((b & 1) == 1, high, low)
    out[...] = acc[...].astype(BF16)


def assemble_kernel(ids, *refs):
    parts, out = refs[:-1], refs[-1]
    depth = parts[0].shape[0]
    for k, y in enumerate(parts):
        out[pl.ds(pl.multiple_of((ids[1] ^ k) * depth, 16), depth), :] = y[...].astype(F32)


def weight_k_of(pack, head, uk_rows, tiles):
    rows = uk_rows // tiles
    peers = pack.shape[0]
    cols = []
    for t in range(tiles):
        cols.append(
            jnp.concatenate(
                [pack[r, head, t * rows : (t + 1) * rows, :] for r in range(peers)], axis=0
            )
        )
    return jnp.concatenate(cols, axis=1)


def stacked(pack, head, start, rows):
    peers = pack.shape[0]
    return jnp.concatenate([pack[r, head, start : start + rows, :] for r in range(peers)], axis=0)


def expand_kernel(sizes, pack, away, over_x, out):
    uk_rows, uv_rows, queries, tiles, latent = sizes
    peers, heads = pack.shape[0], pack.shape[1]
    for h in range(heads):
        wk = weight_k_of(pack, h, uk_rows, tiles)
        wv = stacked(pack, h, uk_rows, uv_rows)
        qn = stacked(pack, h, uk_rows + uv_rows, queries)
        do = stacked(pack, h, uk_rows + uv_rows + queries, queries)
        q_lat = nn(qn, wk).astype(BF16)
        d_olat = nt(do, wv).astype(BF16)
        for r in range(peers):
            out[r, h, :, :latent] = q_lat[r * queries : (r + 1) * queries]
            out[r, h, :, latent:] = d_olat[r * queries : (r + 1) * queries]


def reduce_kernel(sizes, pack, lat, out):
    uk_rows, uv_rows, queries, tiles, latent = sizes
    peers, heads = pack.shape[0], pack.shape[1]
    for h in range(heads):
        wk = weight_k_of(pack, h, uk_rows, tiles)
        wv = stacked(pack, h, uk_rows, uv_rows)
        both = jnp.concatenate([lat[r, h] for r in range(peers)], axis=0)
        attn = nn(both[:, :latent], wv).astype(BF16)
        dqn = nt(both[:, latent:], wk).astype(BF16)
        for r in range(peers):
            out[r, h, :, : attn.shape[1]] = attn[r * queries : (r + 1) * queries]
            out[r, h, :, attn.shape[1] :] = dqn[r * queries : (r + 1) * queries]


def tokens_grad(grads, scale, do, cat, delta, kt, p, width):
    keep, send, at, depth = grads
    latent = do.shape[1]
    dp = nn(do[...], kt[:latent])
    ds = (p.astype(F32) * (dp - delta) * scale).astype(BF16)
    part = nt(ds, kt[:width])
    dk = nn(cat[...], jnp.concatenate([ds, p], axis=0)).astype(BF16)
    for k, ref in enumerate((keep, send, keep, send)):
        ref[k // 2, :, at] = dk[k * depth : (k + 1) * depth]
    return part


def attend_kernel(scale, per_peer, ids, sel, rope, qd, *refs):
    keys, refs = (refs[:4], refs[4:8]), refs[8:]
    keeps, sends, lat, d_rope, refs = (refs[0], refs[2]), (refs[1], refs[3]), refs[4], refs[5], refs[6:]
    kt_near, kt_far, pb_near, pb_far, qx, do, sc, flip, cat, o_full, dq = refs[:11]
    keep_far, send_far, key_sems, out_sems = refs[11:]
    leaving = [
        pltpu.make_async_copy(src, dst, out_sems.at[n])
        for n, (src, dst) in enumerate(((keep_far, keeps[1]), (send_far, sends[1])))
    ]
    keeps, sends = (keeps[0], keep_far), (sends[0], send_far)
    rows, latent = do.shape
    heads, queries, rope_dim = rope.shape
    width = latent + rope_dim
    slots = qx.shape[1] - width
    depth, half = keys[0][0].shape
    kts, pbs = (kt_near, kt_far), (pb_near, pb_far)

    arriving = []
    for c in range(2):
        place = lax.broadcasted_iota(jnp.int32, (slots, half), 0)
        block = lax.broadcasted_iota(jnp.int32, (slots, half), 1) // BLOCK_LEN
        block = block + (block // per_peer + c) * per_peer
        kts[c][width:, :] = jnp.where(block == place, 1.0, 0.0).astype(BF16)
        for k in range(4):
            at = pl.ds(pl.multiple_of((ids[1] ^ k) * depth, 16), depth)
            copy = pltpu.make_async_copy(keys[c][k], kts[c].at[at, :], key_sems.at[4 * c + k])
            copy.start()
            arriving.append(copy)

    picks = sel[...] ^ (ids[0] * per_peer)
    slot = lax.broadcasted_iota(jnp.int32, (queries, slots), 1)
    chosen = picks[:, 0:1] == slot
    for j in range(1, picks.shape[1]):
        chosen = chosen | (picks[:, j : j + 1] == slot)
    bias = jnp.where(chosen, 0.0, HIDDEN).astype(BF16)
    bias = jnp.broadcast_to(bias[None], (heads, queries, slots)).reshape(rows, slots)
    qx[:, :latent] = qd[:, :latent]
    qx[:, latent:] = jnp.concatenate([rope[...].reshape(rows, rope_dim), bias], axis=1)
    do[...] = qd[:, latent:]
    scale2 = scale * math.log2(math.e)
    step = 1024
    chunks = [(c, i) for c in range(2) for i in range(0, half, step)]
    top = jnp.full((rows, 1), -jnp.inf, F32)
    total = jnp.zeros((rows, 1), F32)
    tops = []
    for n, (c, i) in enumerate(chunks):
        if i == 0:
            for copy in arriving[4 * c : 4 * c + 4]:
                copy.wait()
        s = nn(qx[...], kts[c][:, i : i + step]) * scale2
        high = jnp.maximum(top, jnp.max(s, axis=1, keepdims=True))
        e = jnp.exp2(s - high)
        sc[:, n * step : (n + 1) * step] = e
        total = total * jnp.exp2(top - high) + jnp.sum(e, axis=1, keepdims=True)
        top = high
        tops.append(high)
    inv = 1.0 / total
    for n, (c, i) in enumerate(chunks):
        pb = (sc[:, n * step : (n + 1) * step] * (jnp.exp2(tops[n] - top) * inv)).astype(BF16)
        pbs[c][:, i : i + step] = pb
        part = nt(pb, kts[c][:latent, i : i + step])
        if n == 0:
            o_full[...] = part
        else:
            o_full[...] += part
    lat[:, :latent] = o_full[...].astype(BF16)
    delta = jnp.sum(o_full[...] * do[...].astype(F32), axis=1, keepdims=True)

    flip[:, :rows] = qx[:, :width].T
    flip[:latent, rows:] = do[...].T
    flip[latent:, rows:] = jnp.zeros((rope_dim, rows), BF16)
    for k in range(4):
        at = pl.ds(pl.multiple_of((ids[1] ^ k) * depth, 16), depth)
        cat[k * depth : (k + 1) * depth] = flip[at, :]
    for n, (c, i) in enumerate([(c, i) for c in (1, 0) for i in range(0, half, step)]):
        if c == 0 and i == 0:
            for copy in leaving:
                copy.start()
        at = slice(i, i + step)
        grads = (keeps[c], sends[c], at, depth)
        kt = kts[c].at[:, at]
        part = tokens_grad(grads, scale, do, cat, delta, kt, pbs[c][:, at], width)
        if n == 0:
            dq[...] = part
        else:
            dq[...] += part
    lat[:, latent:] = dq[:, :latent].astype(BF16)
    d_rope[...] = dq[:, latent:].astype(BF16)
    for copy in leaving:
        copy.wait()


def pair_kernel(keep, got, a0, *a2):
    total = keep[...].astype(F32) + got[...].astype(F32)
    a0[...] = total[0].astype(BF16)
    lanes = a2[0].shape[1]
    for i, a in enumerate(a2):
        a[...] = total[1, :, i * lanes : (i + 1) * lanes].astype(BF16)


def owner_kernel(a0, got, *outs):
    total = (a0[...].astype(F32) + got[...].astype(F32)).astype(BF16)
    lanes = outs[0].shape[1]
    for i, out in enumerate(outs):
        out[...] = total[:, i * lanes : (i + 1) * lanes]


def local(q_nope, q_rope, cache, w_uk, w_uv, d_out, sel, slot_blocks):
    peers = lax.axis_size("seq")
    groups = lax.axis_size("grp")
    queries, heads, nope = q_nope.shape
    rope = q_rope.shape[2]
    width = cache.shape[1]
    latent = width - rope
    value = d_out.shape[2]
    slots = slot_blocks.shape[1]
    per_peer = slots // peers
    if not (peers == 8 and groups == 4 and heads % peers == 0 and per_peer % 2 == 0):
        return local_general(q_nope, q_rope, cache, w_uk, w_uv, d_out, sel, slot_blocks)
    ids = jnp.stack([lax.axis_index("seq"), lax.axis_index("grp")]).astype(jnp.int32)
    tokens = cache.shape[0]
    depth = width // groups
    lanes = per_peer * BLOCK_LEN
    held = peers // 2
    half = held * lanes
    share = heads // peers
    rows = heads * queries
    scale = 1.0 / math.sqrt(nope + rope)

    row1 = swap(slot_blocks, "seq", 1)
    (c0,) = call(
        cut_kernel,
        "cut",
        (ids, cache.T),
        [SMEM, ANY],
        [((depth, tokens), BF16)],
        [pltpu.SemaphoreType.DMA],
    )
    asked_y = jnp.concatenate([slot_blocks, row1], axis=0)
    asked = jnp.concatenate([asked_y] + [swap(asked_y, "seq", bit) for bit in (2, 4, 6)], axis=0)
    c2 = swap(c0, "seq", 4)
    c1 = swap(c0, "seq", 2)

    (c2,) = call(tie_kernel, "after", (asked, c1), [ANY] * 2, [], tied=c2)
    c3 = swap(c2, "seq", 2)
    away, k0 = call(
        functools.partial(gather_kernel, per_peer),
        "gather",
        (ids, slot_blocks, row1, c0, c1, c2, c3),
        [SMEM] * 3 + [VMEM] * 4,
        [((depth, half), BF16)] * 2,
    )
    k_away, k0_x = swap(away, "seq", 1), swap(k0, "grp", 2)

    n_rows = w_uk.shape[1] // latent
    l_rows = w_uv.shape[1] // value
    tiles = latent // LANES
    uk = w_uk.reshape(heads, n_rows, tiles, LANES).transpose(0, 2, 1, 3)
    pack = jnp.concatenate(
        [
            uk.reshape(heads, n_rows * tiles, LANES),
            w_uv.reshape(heads, l_rows, value),
            q_nope.transpose(1, 0, 2),
            d_out.transpose(1, 0, 2),
        ],
        axis=1,
    )
    (pack,) = call(tie_kernel, "after", (c1, c3), [ANY] * 2, [], tied=pack)
    pack = seq_swap(pack).reshape(peers, share, -1, LANES)
    sizes = (n_rows * tiles, l_rows, queries, tiles, latent)
    (lat,) = call(
        functools.partial(expand_kernel, sizes),
        "expand",
        (pack, k_away, k0_x),
        [VMEM, ANY, ANY],
        [((peers, share, queries, 2 * latent), BF16)],
    )
    qd = seq_swap(lat).reshape(rows, 2 * latent)

    keys = []
    for k, k2 in ((k0, k0_x), (k_away, swap(k_away, "grp", 2))):
        keys += [k, swap(k, "grp", 1), k2, swap(k2, "grp", 1)]
    rope_rows = q_rope.transpose(1, 0, 2)
    near_keep, near_send, far_keep, far_send, lat, d_rope = call(
        functools.partial(attend_kernel, scale, per_peer),
        "attend",
        (ids, sel, rope_rows, qd, *keys),
        [SMEM] + [VMEM] * 3 + [ANY] * 8,
        [((2, depth, half), BF16)] * 4 + [((rows, 2 * latent), BF16), ((rows, rope), BF16)],
        [pltpu.VMEM((width + slots, half), BF16)] * 2
        + [pltpu.VMEM((rows, half), BF16)] * 2
        + [
            pltpu.VMEM((rows, width + slots), BF16),
            pltpu.VMEM((rows, latent), BF16),
            pltpu.VMEM((rows, 2 * half), F32),
            pltpu.VMEM((width, 2 * rows), BF16),
            pltpu.VMEM((width, 2 * rows), BF16),
            pltpu.VMEM((rows, latent), F32),
            pltpu.VMEM((rows, width), F32),
            pltpu.VMEM((2, depth, half), BF16),
            pltpu.VMEM((2, depth, half), BF16),
            pltpu.SemaphoreType.DMA((8,)),
            pltpu.SemaphoreType.DMA((2,)),
        ],
        60,
        out_specs=[VMEM, VMEM, ANY, ANY, VMEM, VMEM],
    )

    def pair(keep, send, tied=None):
        outs = [((depth, half), BF16)] * 2
        return call(pair_kernel, "pair", (keep, swap(send, "grp", 1)), [VMEM] * 2, outs, tied=tied)


    def owner(a0, a2):
        outs = [((depth, lanes), BF16)] * held
        return call(owner_kernel, "owner", (a0, swap(a2, "grp", 2)), [VMEM] * 2, outs)

    far = pair(far_keep, far_send)
    first, *near = pair(near_keep, near_send, tied=far[0])
    far = owner(first, far[1])
    lat = seq_swap(lat.reshape(peers, share, queries, 2 * latent))
    (res,) = call(
        functools.partial(reduce_kernel, sizes),
        "reduce",
        (pack, lat),
        [VMEM] * 2,
        [((peers, share, queries, value + nope), BF16)],
    )
    near = owner(*near)
    got = [near[0]] + [None] * (peers - 1)
    for k in (7, 5, 3, 1, 6, 4, 2):
        got[k] = swap((far if k % 2 else near)[k // 2], "seq", k)
    res = seq_swap(res).reshape(heads, queries, value + nope)

    (y0,) = call(
        functools.partial(scatter_kernel, per_peer),
        "scatter",
        (ids, asked, *got),
        [SMEM, SMEM] + [VMEM] * len(got),
        [((depth, tokens), BF16)],
        [pltpu.VMEM((depth, tokens), F32)],
    )
    y2 = swap(y0, "grp", 2)
    y1 = swap(y0, "grp", 1)
    y3 = swap(y2, "grp", 1)
    (d_cache,) = call(
        assemble_kernel,
        "assemble",
        (ids, y0, y1, y2, y3),
        [SMEM] + [VMEM] * 4,
        [((width, tokens), F32)],
    )
    return (
        res[:, :, :value].transpose(1, 0, 2),
        res[:, :, value:].transpose(1, 0, 2),
        d_rope.reshape(heads, queries, rope).transpose(1, 0, 2),
        d_cache.T,
    )


def local_general(q_nope, q_rope, cache, w_uk, w_uv, d_out, sel, slot_blocks):
    peers = lax.axis_size("seq")
    queries, heads, nope = q_nope.shape
    rope = q_rope.shape[2]
    width = cache.shape[1]
    latent = width - rope
    value = d_out.shape[2]
    slot_total = slot_blocks.shape[1]
    per_peer = slot_total // peers
    own_blocks = cache.shape[0] // BLOCK_LEN
    scale = 1.0 / math.sqrt(nope + rope)
    gathered_k, gathered_v = (
        lax.all_gather(w_uk, "seq", axis=1, tiled=True),
        lax.all_gather(w_uv, "seq", axis=1, tiled=True),
    )
    weight_k = gathered_k.reshape(heads, nope, latent)
    weight_v = gathered_v.reshape(heads, latent, value)
    wanted = slot_blocks.reshape(peers, per_peer)
    asked = lax.all_to_all(wanted, "seq", split_axis=0, concat_axis=0, tiled=True)
    blocks = cache.reshape(own_blocks, BLOCK_LEN, width)
    arrived = lax.all_to_all(blocks[asked], "seq", split_axis=0, concat_axis=0, tiled=True)
    keys = arrived.reshape(slot_total * BLOCK_LEN, width)
    keys_lat = keys[:, :latent]
    q_lat = jnp.einsum("qhn,hnl->qhl", q_nope, weight_k, preferred_element_type=jnp.float32).astype(
        jnp.bfloat16
    )
    qfull = jnp.concatenate([q_lat, q_rope], axis=-1)
    chosen = jnp.any(
        sel[:, :, None] == jnp.arange(slot_total, dtype=jnp.int32)[None, None, :], axis=1
    )
    live = jnp.repeat(chosen, BLOCK_LEN, axis=1)[:, None, :]
    score = jnp.einsum("qhc,tc->qht", qfull, keys, preferred_element_type=jnp.float32) * scale
    score = jnp.where(live, score, -jnp.inf)
    prob = jax.nn.softmax(score, axis=-1)
    prob_low = prob.astype(jnp.bfloat16)
    olat = jnp.einsum("qht,tl->qhl", prob_low, keys_lat, preferred_element_type=jnp.float32).astype(
        jnp.bfloat16
    )
    attn_out = jnp.einsum(
        "qhl,hlv->qhv", olat, weight_v, preferred_element_type=jnp.float32
    ).astype(jnp.bfloat16)
    d_olat = jnp.einsum("qhv,hlv->qhl", d_out, weight_v, preferred_element_type=jnp.float32).astype(
        jnp.bfloat16
    )
    dprob = jnp.einsum("qhl,tl->qht", d_olat, keys_lat, preferred_element_type=jnp.float32)
    delta = jnp.sum(prob * dprob, axis=-1, keepdims=True)
    dscore = (prob * (dprob - delta) * scale).astype(jnp.bfloat16)
    dquery = jnp.einsum("qht,tc->qhc", dscore, keys, preferred_element_type=jnp.float32)
    d_q_rope = dquery[:, :, latent:].astype(jnp.bfloat16)
    d_qlat = dquery[:, :, :latent].astype(jnp.bfloat16)
    d_q_nope = jnp.einsum(
        "qhl,hnl->qhn", d_qlat, weight_k, preferred_element_type=jnp.float32
    ).astype(jnp.bfloat16)
    value_part = jnp.einsum("qht,qhl->tl", prob_low, d_olat, preferred_element_type=jnp.float32)
    dkeys = jnp.einsum("qht,qhc->tc", dscore, qfull, preferred_element_type=jnp.float32)
    dkeys = dkeys + jnp.pad(value_part, ((0, 0), (0, rope)))
    one_hot = (
        asked.reshape(-1)[:, None] == jnp.arange(own_blocks, dtype=jnp.int32)[None, :]
    ).astype(jnp.float32)
    returned = lax.all_to_all(
        dkeys.reshape(peers, per_peer, BLOCK_LEN * width).astype(jnp.bfloat16),
        "seq",
        split_axis=0,
        concat_axis=0,
        tiled=True,
    ).astype(jnp.float32)
    local_grad = jnp.dot(
        one_hot.T,
        returned.reshape(peers * per_peer, BLOCK_LEN * width),
        precision=lax.Precision.HIGHEST,
    )
    d_cache = (
        lax.psum(local_grad.astype(jnp.bfloat16), "grp")
        .astype(jnp.float32)
        .reshape(own_blocks * BLOCK_LEN, width)
    )
    return (attn_out, d_q_nope, d_q_rope, d_cache)


def solution(mesh):
    return jax.shard_map(
        local,
        mesh=mesh,
        in_specs=(
            P("seq", "grp", None),
            P("seq", "grp", None),
            P("seq", None),
            P("grp", "seq"),
            P("grp", "seq"),
            P("seq", "grp", None),
            P("seq", None),
            P("seq", None),
        ),
        out_specs=(
            P("seq", "grp", None),
            P("seq", "grp", None),
            P("seq", "grp", None),
            P("seq", None),
        ),
        check_vma=False,
    )
```

```python
import functools
import math

import jax
import jax.numpy as jnp
from jax import lax
from jax.experimental import pallas as pl
from jax.experimental.pallas import tpu as pltpu
from jax.sharding import PartitionSpec as P

BLOCK_LEN = 64
LANES = 128
HIDDEN = -1e30
VMEM = pl.BlockSpec(memory_space=pltpu.VMEM)
SMEM = pl.BlockSpec(memory_space=pltpu.SMEM)
ANY = pl.BlockSpec(memory_space=pl.ANY)
F32 = jnp.float32
BF16 = jnp.bfloat16


def call(kernel, name, args, specs, outs, scratch=(), mib=32, tied=None):
    out_shape = [jax.ShapeDtypeStruct(s, d) for s, d in outs]
    out_specs = [VMEM] * len(outs)
    aliases = {}
    body = kernel
    if tied is not None:
        args, specs = (tied, *args), [ANY] + specs
        out_shape, out_specs = [jax.ShapeDtypeStruct(tied.shape, tied.dtype)] + out_shape, [ANY] + out_specs
        aliases = {0: 0}
        n_in = len(args)

        def body(*refs):
            kernel(*refs[1:n_in], *refs[n_in + 1 :])

    return pl.pallas_call(
        body,
        out_shape=out_shape,
        in_specs=specs,
        out_specs=out_specs,
        scratch_shapes=list(scratch),
        input_output_aliases=aliases,
        compiler_params=pltpu.CompilerParams(vmem_limit_bytes=mib * 2**20),
        name=name,
    )(*args)


def nt(a, b):
    return lax.dot_general(a, b, (((1,), (1,)), ((), ())), preferred_element_type=F32)


def nn(a, b):
    return lax.dot_general(a, b, (((1,), (0,)), ((), ())), preferred_element_type=F32)


def swap(x, axis, bit):
    n = lax.axis_size(axis)
    return lax.ppermute(x, axis, [(i, i ^ bit) for i in range(n)])


def seq_swap(x):
    return lax.all_to_all(x, "seq", split_axis=0, concat_axis=0, tiled=True)


def tie_kernel(*refs):
    pass


def cut_kernel(ids, cache, out, sem):
    depth = out.shape[0]
    part = cache.at[pl.ds(pl.multiple_of(ids[1] * depth, 16), depth), :]
    copy = pltpu.make_async_copy(part, out, sem)
    copy.start()
    copy.wait()


def gather_kernel(per_peer, ids, own, other, *refs):
    owners = len(refs) - 2
    caches, outs = refs[:owners], refs[owners:]
    lanes = per_peer * BLOCK_LEN

    def block(row, i, j):
        b = row[0, (ids[0] ^ (2 * i)) * per_peer + j]
        tile = caches[i][:, pl.ds(pl.multiple_of((b >> 1) * LANES, LANES), LANES)]
        return jnp.where((b & 1) == 1, tile[:, BLOCK_LEN:], tile[:, :BLOCK_LEN])

    for row, out in zip((other, own), outs):
        for i in range(owners):
            for j in range(0, per_peer, 2):
                both = jnp.concatenate([block(row, i, j), block(row, i, j + 1)], axis=1)
                at = i * lanes + j * BLOCK_LEN
                out[:, at : at + 2 * BLOCK_LEN] = both


def scatter_kernel(per_peer, ids, rows, *refs):
    got, out, acc = refs[:-2], refs[-2], refs[-1]
    me = ids[0]
    depth = out.shape[0]
    acc[...] = jnp.zeros_like(acc)
    blank = jnp.zeros((depth, BLOCK_LEN), F32)
    for k, piece in enumerate(got):
        for j in range(per_peer):
            b = rows[k, me * per_peer + j]
            at = pl.ds(pl.multiple_of((b >> 1) * LANES, LANES), LANES)
            g = piece[:, j * BLOCK_LEN : (j + 1) * BLOCK_LEN].astype(F32)
            low = jnp.concatenate([g, blank], axis=1)
            high = jnp.concatenate([blank, g], axis=1)
            acc[:, at] = acc[:, at] + jnp.where((b & 1) == 1, high, low)
    out[...] = acc[...].astype(BF16)


def assemble_kernel(ids, *refs):
    parts, out = refs[:-1], refs[-1]
    depth = parts[0].shape[0]
    for k, y in enumerate(parts):
        out[pl.ds(pl.multiple_of((ids[1] ^ k) * depth, 16), depth), :] = y[...].astype(F32)


def weight_k_of(pack, head, uk_rows, tiles):
    rows = uk_rows // tiles
    peers = pack.shape[0]
    cols = []
    for t in range(tiles):
        cols.append(
            jnp.concatenate(
                [pack[r, head, t * rows : (t + 1) * rows, :] for r in range(peers)], axis=0
            )
        )
    return jnp.concatenate(cols, axis=1)


def stacked(pack, head, start, rows):
    peers = pack.shape[0]
    return jnp.concatenate([pack[r, head, start : start + rows, :] for r in range(peers)], axis=0)


def expand_kernel(sizes, pack, away, over_x, out):
    uk_rows, uv_rows, queries, tiles, latent = sizes
    peers, heads = pack.shape[0], pack.shape[1]
    for h in range(heads):
        wk = weight_k_of(pack, h, uk_rows, tiles)
        wv = stacked(pack, h, uk_rows, uv_rows)
        qn = stacked(pack, h, uk_rows + uv_rows, queries)
        do = stacked(pack, h, uk_rows + uv_rows + queries, queries)
        q_lat = nn(qn, wk).astype(BF16)
        d_olat = nt(do, wv).astype(BF16)
        for r in range(peers):
            out[r, h, :, :latent] = q_lat[r * queries : (r + 1) * queries]
            out[r, h, :, latent:] = d_olat[r * queries : (r + 1) * queries]


def reduce_kernel(sizes, pack, lat, out):
    uk_rows, uv_rows, queries, tiles, latent = sizes
    peers, heads = pack.shape[0], pack.shape[1]
    for h in range(heads):
        wk = weight_k_of(pack, h, uk_rows, tiles)
        wv = stacked(pack, h, uk_rows, uv_rows)
        both = jnp.concatenate([lat[r, h] for r in range(peers)], axis=0)
        attn = nn(both[:, :latent], wv).astype(BF16)
        dqn = nt(both[:, latent:], wk).astype(BF16)
        for r in range(peers):
            out[r, h, :, : attn.shape[1]] = attn[r * queries : (r + 1) * queries]
            out[r, h, :, attn.shape[1] :] = dqn[r * queries : (r + 1) * queries]


def tokens_grad(grads, scale, do, cat, delta, kt, p, width):
    keep, send, at, depth = grads
    latent = do.shape[1]
    dp = nn(do[...], kt[:latent])
    ds = (p.astype(F32) * (dp - delta) * scale).astype(BF16)
    part = nt(ds, kt[:width])
    dk = nn(cat[...], jnp.concatenate([ds, p], axis=0)).astype(BF16)
    for k, ref in enumerate((keep, send, keep, send)):
        ref[k // 2, :, at] = dk[k * depth : (k + 1) * depth]
    return part


def attend_kernel(scale, per_peer, ids, sel, rope, qd, *refs):
    keys, refs = (refs[:4], refs[4:8]), refs[8:]
    keeps, sends, lat, d_rope, refs = (refs[0], refs[2]), (refs[1], refs[3]), refs[4], refs[5], refs[6:]
    kt_near, kt_far, pb_near, pb_far, qx, do, sc, flip, cat, o_full, dq = refs
    rows, latent = do.shape
    heads, queries, rope_dim = rope.shape
    width = latent + rope_dim
    slots = qx.shape[1] - width
    depth, half = keys[0][0].shape
    kts, pbs = (kt_near, kt_far), (pb_near, pb_far)

    picks = sel[...] ^ (ids[0] * per_peer)
    slot = lax.broadcasted_iota(jnp.int32, (queries, slots), 1)
    chosen = picks[:, 0:1] == slot
    for j in range(1, picks.shape[1]):
        chosen = chosen | (picks[:, j : j + 1] == slot)
    bias = jnp.where(chosen, 0.0, HIDDEN).astype(BF16)
    bias = jnp.broadcast_to(bias[None], (heads, queries, slots)).reshape(rows, slots)
    qx[:, :latent] = qd[:, :latent]
    qx[:, latent:] = jnp.concatenate([rope[...].reshape(rows, rope_dim), bias], axis=1)
    do[...] = qd[:, latent:]
    for c in range(2):
        for k in range(4):
            at = pl.ds(pl.multiple_of((ids[1] ^ k) * depth, 16), depth)
            kts[c][at, :] = keys[c][k][...]
        place = lax.broadcasted_iota(jnp.int32, (slots, half), 0)
        block = lax.broadcasted_iota(jnp.int32, (slots, half), 1) // BLOCK_LEN
        block = block + (block // per_peer + c) * per_peer
        kts[c][width:, :] = jnp.where(block == place, 1.0, 0.0).astype(BF16)

    scale2 = scale * math.log2(math.e)
    step = 1024
    chunks = [(c, i) for c in range(2) for i in range(0, half, step)]
    top = jnp.full((rows, 1), -jnp.inf, F32)
    total = jnp.zeros((rows, 1), F32)
    tops = []
    for n, (c, i) in enumerate(chunks):
        s = nn(qx[...], kts[c][:, i : i + step]) * scale2
        high = jnp.maximum(top, jnp.max(s, axis=1, keepdims=True))
        e = jnp.exp2(s - high)
        sc[:, n * step : (n + 1) * step] = e
        total = total * jnp.exp2(top - high) + jnp.sum(e, axis=1, keepdims=True)
        top = high
        tops.append(high)
    inv = 1.0 / total
    for n, (c, i) in enumerate(chunks):
        pb = (sc[:, n * step : (n + 1) * step] * (jnp.exp2(tops[n] - top) * inv)).astype(BF16)
        pbs[c][:, i : i + step] = pb
        part = nt(pb, kts[c][:latent, i : i + step])
        if n == 0:
            o_full[...] = part
        else:
            o_full[...] += part
    lat[:, :latent] = o_full[...].astype(BF16)
    delta = jnp.sum(o_full[...] * do[...].astype(F32), axis=1, keepdims=True)

    flip[:, :rows] = qx[:, :width].T
    flip[:latent, rows:] = do[...].T
    flip[latent:, rows:] = jnp.zeros((rope_dim, rows), BF16)
    for k in range(4):
        at = pl.ds(pl.multiple_of((ids[1] ^ k) * depth, 16), depth)
        cat[k * depth : (k + 1) * depth] = flip[at, :]
    for n, (c, i) in enumerate([(c, i) for c in (1, 0) for i in range(0, half, step)]):
        at = slice(i, i + step)
        grads = (keeps[c], sends[c], at, depth)
        kt = kts[c].at[:, at]
        part = tokens_grad(grads, scale, do, cat, delta, kt, pbs[c][:, at], width)
        if n == 0:
            dq[...] = part
        else:
            dq[...] += part
    lat[:, latent:] = dq[:, :latent].astype(BF16)
    d_rope[...] = dq[:, latent:].astype(BF16)


def pair_kernel(keep, got, a0, *a2):
    total = keep[...].astype(F32) + got[...].astype(F32)
    a0[...] = total[0].astype(BF16)
    lanes = a2[0].shape[1]
    for i, a in enumerate(a2):
        a[...] = total[1, :, i * lanes : (i + 1) * lanes].astype(BF16)


def owner_kernel(a0, got, *outs):
    total = (a0[...].astype(F32) + got[...].astype(F32)).astype(BF16)
    lanes = outs[0].shape[1]
    for i, out in enumerate(outs):
        out[...] = total[:, i * lanes : (i + 1) * lanes]


def local(q_nope, q_rope, cache, w_uk, w_uv, d_out, sel, slot_blocks):
    peers = lax.axis_size("seq")
    groups = lax.axis_size("grp")
    queries, heads, nope = q_nope.shape
    rope = q_rope.shape[2]
    width = cache.shape[1]
    latent = width - rope
    value = d_out.shape[2]
    slots = slot_blocks.shape[1]
    per_peer = slots // peers
    if not (peers == 8 and groups == 4 and heads % peers == 0 and per_peer % 2 == 0):
        return local_general(q_nope, q_rope, cache, w_uk, w_uv, d_out, sel, slot_blocks)
    ids = jnp.stack([lax.axis_index("seq"), lax.axis_index("grp")]).astype(jnp.int32)
    tokens = cache.shape[0]
    depth = width // groups
    lanes = per_peer * BLOCK_LEN
    held = peers // 2
    half = held * lanes
    share = heads // peers
    rows = heads * queries
    scale = 1.0 / math.sqrt(nope + rope)

    row1 = swap(slot_blocks, "seq", 1)
    (c0,) = call(
        cut_kernel,
        "cut",
        (ids, cache.T),
        [SMEM, ANY],
        [((depth, tokens), BF16)],
        [pltpu.SemaphoreType.DMA],
        62,
    )
    asked_y = jnp.concatenate([slot_blocks, row1], axis=0)
    asked = jnp.concatenate([asked_y] + [swap(asked_y, "seq", bit) for bit in (2, 4, 6)], axis=0)
    c2 = swap(c0, "seq", 4)
    c1 = swap(c0, "seq", 2)

    (c2,) = call(tie_kernel, "after", (asked, c1), [ANY] * 2, [], tied=c2)
    c3 = swap(c2, "seq", 2)
    away, k0 = call(
        functools.partial(gather_kernel, per_peer),
        "gather",
        (ids, slot_blocks, row1, c0, c1, c2, c3),
        [SMEM] * 3 + [VMEM] * 4,
        [((depth, half), BF16)] * 2,
    )
    k_away, k0_x = swap(away, "seq", 1), swap(k0, "grp", 2)

    n_rows = w_uk.shape[1] // latent
    l_rows = w_uv.shape[1] // value
    tiles = latent // LANES
    uk = w_uk.reshape(heads, n_rows, tiles, LANES).transpose(0, 2, 1, 3)
    pack = jnp.concatenate(
        [
            uk.reshape(heads, n_rows * tiles, LANES),
            w_uv.reshape(heads, l_rows, value),
            q_nope.transpose(1, 0, 2),
            d_out.transpose(1, 0, 2),
        ],
        axis=1,
    )
    (pack,) = call(tie_kernel, "after", (c1, c3), [ANY] * 2, [], tied=pack)
    pack = seq_swap(pack).reshape(peers, share, -1, LANES)
    sizes = (n_rows * tiles, l_rows, queries, tiles, latent)
    (lat,) = call(
        functools.partial(expand_kernel, sizes),
        "expand",
        (pack, k_away, k0_x),
        [VMEM, ANY, ANY],
        [((peers, share, queries, 2 * latent), BF16)],
    )
    qd = seq_swap(lat).reshape(rows, 2 * latent)

    keys = []
    for k, k2 in ((k0, k0_x), (k_away, swap(k_away, "grp", 2))):
        keys += [k, swap(k, "grp", 1), k2, swap(k2, "grp", 1)]
    rope_rows = q_rope.transpose(1, 0, 2)
    near_keep, near_send, far_keep, far_send, lat, d_rope = call(
        functools.partial(attend_kernel, scale, per_peer),
        "attend",
        (ids, sel, rope_rows, qd, *keys),
        [SMEM] + [VMEM] * 11,
        [((2, depth, half), BF16)] * 4 + [((rows, 2 * latent), BF16), ((rows, rope), BF16)],
        [pltpu.VMEM((width + slots, half), BF16)] * 2
        + [pltpu.VMEM((rows, half), BF16)] * 2
        + [
            pltpu.VMEM((rows, width + slots), BF16),
            pltpu.VMEM((rows, latent), BF16),
            pltpu.VMEM((rows, 2 * half), F32),
            pltpu.VMEM((width, 2 * rows), BF16),
            pltpu.VMEM((width, 2 * rows), BF16),
            pltpu.VMEM((rows, latent), F32),
            pltpu.VMEM((rows, width), F32),
        ],
        60,
    )

    def pair(keep, send, tied=None):
        outs = [((depth, half), BF16)] * 2
        return call(pair_kernel, "pair", (keep, swap(send, "grp", 1)), [VMEM] * 2, outs, tied=tied)


    def owner(a0, a2):
        outs = [((depth, lanes), BF16)] * held
        return call(owner_kernel, "owner", (a0, swap(a2, "grp", 2)), [VMEM] * 2, outs)

    far = pair(far_keep, far_send)
    first, *near = pair(near_keep, near_send, tied=far[0])
    far = owner(first, far[1])
    lat = seq_swap(lat.reshape(peers, share, queries, 2 * latent))
    (res,) = call(
        functools.partial(reduce_kernel, sizes),
        "reduce",
        (pack, lat),
        [VMEM] * 2,
        [((peers, share, queries, value + nope), BF16)],
    )
    near = owner(*near)
    got = [near[0]] + [None] * (peers - 1)
    for k in (7, 5, 3, 1, 6, 4, 2):
        got[k] = swap((far if k % 2 else near)[k // 2], "seq", k)
    res = seq_swap(res).reshape(heads, queries, value + nope)

    (y0,) = call(
        functools.partial(scatter_kernel, per_peer),
        "scatter",
        (ids, asked, *got),
        [SMEM, SMEM] + [VMEM] * len(got),
        [((depth, tokens), BF16)],
        [pltpu.VMEM((depth, tokens), F32)],
    )
    y2 = swap(y0, "grp", 2)
    y1 = swap(y0, "grp", 1)
    y3 = swap(y2, "grp", 1)
    (d_cache,) = call(
        assemble_kernel,
        "assemble",
        (ids, y0, y1, y2, y3),
        [SMEM] + [VMEM] * 4,
        [((width, tokens), F32)],
    )
    return (
        res[:, :, :value].transpose(1, 0, 2),
        res[:, :, value:].transpose(1, 0, 2),
        d_rope.reshape(heads, queries, rope).transpose(1, 0, 2),
        d_cache.T,
    )


def local_general(q_nope, q_rope, cache, w_uk, w_uv, d_out, sel, slot_blocks):
    peers = lax.axis_size("seq")
    queries, heads, nope = q_nope.shape
    rope = q_rope.shape[2]
    width = cache.shape[1]
    latent = width - rope
    value = d_out.shape[2]
    slot_total = slot_blocks.shape[1]
    per_peer = slot_total // peers
    own_blocks = cache.shape[0] // BLOCK_LEN
    scale = 1.0 / math.sqrt(nope + rope)
    gathered_k, gathered_v = (
        lax.all_gather(w_uk, "seq", axis=1, tiled=True),
        lax.all_gather(w_uv, "seq", axis=1, tiled=True),
    )
    weight_k = gathered_k.reshape(heads, nope, latent)
    weight_v = gathered_v.reshape(heads, latent, value)
    wanted = slot_blocks.reshape(peers, per_peer)
    asked = lax.all_to_all(wanted, "seq", split_axis=0, concat_axis=0, tiled=True)
    blocks = cache.reshape(own_blocks, BLOCK_LEN, width)
    arrived = lax.all_to_all(blocks[asked], "seq", split_axis=0, concat_axis=0, tiled=True)
    keys = arrived.reshape(slot_total * BLOCK_LEN, width)
    keys_lat = keys[:, :latent]
    q_lat = jnp.einsum("qhn,hnl->qhl", q_nope, weight_k, preferred_element_type=jnp.float32).astype(
        jnp.bfloat16
    )
    qfull = jnp.concatenate([q_lat, q_rope], axis=-1)
    chosen = jnp.any(
        sel[:, :, None] == jnp.arange(slot_total, dtype=jnp.int32)[None, None, :], axis=1
    )
    live = jnp.repeat(chosen, BLOCK_LEN, axis=1)[:, None, :]
    score = jnp.einsum("qhc,tc->qht", qfull, keys, preferred_element_type=jnp.float32) * scale
    score = jnp.where(live, score, -jnp.inf)
    prob = jax.nn.softmax(score, axis=-1)
    prob_low = prob.astype(jnp.bfloat16)
    olat = jnp.einsum("qht,tl->qhl", prob_low, keys_lat, preferred_element_type=jnp.float32).astype(
        jnp.bfloat16
    )
    attn_out = jnp.einsum(
        "qhl,hlv->qhv", olat, weight_v, preferred_element_type=jnp.float32
    ).astype(jnp.bfloat16)
    d_olat = jnp.einsum("qhv,hlv->qhl", d_out, weight_v, preferred_element_type=jnp.float32).astype(
        jnp.bfloat16
    )
    dprob = jnp.einsum("qhl,tl->qht", d_olat, keys_lat, preferred_element_type=jnp.float32)
    delta = jnp.sum(prob * dprob, axis=-1, keepdims=True)
    dscore = (prob * (dprob - delta) * scale).astype(jnp.bfloat16)
    dquery = jnp.einsum("qht,tc->qhc", dscore, keys, preferred_element_type=jnp.float32)
    d_q_rope = dquery[:, :, latent:].astype(jnp.bfloat16)
    d_qlat = dquery[:, :, :latent].astype(jnp.bfloat16)
    d_q_nope = jnp.einsum(
        "qhl,hnl->qhn", d_qlat, weight_k, preferred_element_type=jnp.float32
    ).astype(jnp.bfloat16)
    value_part = jnp.einsum("qht,qhl->tl", prob_low, d_olat, preferred_element_type=jnp.float32)
    dkeys = jnp.einsum("qht,qhc->tc", dscore, qfull, preferred_element_type=jnp.float32)
    dkeys = dkeys + jnp.pad(value_part, ((0, 0), (0, rope)))
    one_hot = (
        asked.reshape(-1)[:, None] == jnp.arange(own_blocks, dtype=jnp.int32)[None, :]
    ).astype(jnp.float32)
    returned = lax.all_to_all(
        dkeys.reshape(peers, per_peer, BLOCK_LEN * width).astype(jnp.bfloat16),
        "seq",
        split_axis=0,
        concat_axis=0,
        tiled=True,
    ).astype(jnp.float32)
    local_grad = jnp.dot(
        one_hot.T,
        returned.reshape(peers * per_peer, BLOCK_LEN * width),
        precision=lax.Precision.HIGHEST,
    )
    d_cache = (
        lax.psum(local_grad.astype(jnp.bfloat16), "grp")
        .astype(jnp.float32)
        .reshape(own_blocks * BLOCK_LEN, width)
    )
    return (attn_out, d_q_nope, d_q_rope, d_cache)


def solution(mesh):
    return jax.shard_map(
        local,
        mesh=mesh,
        in_specs=(
            P("seq", "grp", None),
            P("seq", "grp", None),
            P("seq", None),
            P("grp", "seq"),
            P("grp", "seq"),
            P("seq", "grp", None),
            P("seq", None),
            P("seq", None),
        ),
        out_specs=(
            P("seq", "grp", None),
            P("seq", "grp", None),
            P("seq", "grp", None),
            P("seq", None),
        ),
        check_vma=False,
    )
```
